512 devices in a mesh: gx: 16 (over z), gy: 4 (over x), gz: 8 (over y, core).
Axes of the slice: x: 4, y: 4, z: 16, core: 2. Of those that a mesh axis runs over, the one named last changes fastest.
Arguments:
- velocity: float32 [3, 128, 64, 1024], P(None, 'gx', 'gy', 'gz'), may hold values from -6 to 6
- density: float32 [128, 64, 1024], P('gx', 'gy', 'gz'), may hold values from 0 to 2
- offsets: int32 [3, 128, 64, 1024], P(None, 'gx', 'gy', 'gz'), may hold values from -4 to 3
- eighths: int32 [3, 128, 64, 1024], P(None, 'gx', 'gy', 'gz'), may hold values from 0 to 7
Outputs:
- new_velocity: float32 [3, 128, 64, 1024], P(None, 'gx', 'gy', 'gz')
- new_density: float32 [128, 64, 1024], P('gx', 'gy', 'gz')
- pressure: float32 [128, 64, 1024], P('gx', 'gy', 'gz')
The draws below stay inside these ranges and needn't reach their ends.
All inputs are finite; a program needn't handle non-finite values.
Results may differ from the reference program's by a relative error of at most 0.00002.
Values sent between devices are 32-bit elements; how exact they have to be, the bound alone decides.
No kernel may reach another device: no remote copies, remote signals or barrier semaphores. Data moves between devices by JAX's collectives and lax.ppermute only.
A program may use at most 64 MiB of HBM per device.

```python
import jax
import jax.numpy as jnp
from jax import lax

NX = 128
NY = 64
NZ = 1024


def set_ends(values, key, low, high):
    index_at = [jax.random.randint(jax.random.fold_in(key, axis), (), 0, length) for axis, length in enumerate(values.shape)]
    main_axis = values.shape.index(max(values.shape))
    next_to = index_at[:main_axis] + [(index_at[main_axis] + 1) % values.shape[main_axis]] + index_at[main_axis + 1:]
    return values.at[tuple(index_at)].set(low).at[tuple(next_to)].set(high)


def block_levels(key, dims, split, smallest, top_value):
    def one(dim, blocks):
        steps = jax.random.uniform(jax.random.fold_in(jax.random.fold_in(key, 6), dim), (blocks,), jnp.float32, smallest / len(split), top_value / len(split))
        return jnp.repeat(jnp.exp(steps), dims[dim] // blocks).reshape((-1,) + (1,) * (len(dims) - dim - 1))

    level = one(*split[0])
    for cut in split[1:]:
        level = level * one(*cut)
    return level


def noise(own_key, shape, width, limit, shards=(), held_as=jnp.bfloat16):
    gain = block_levels(own_key, shape, shards, -0.22, 0.18) if shards else 1.0
    array = jax.random.normal(own_key, shape, jnp.float32) * width * gain
    return jnp.minimum(jnp.maximum(array, -limit), limit).astype(held_as)


def setup_inputs(seed: int = 0) -> dict:
    key_list = jax.random.split(jax.random.key(seed), 5)
    velocity = noise(key_list[0], (3, NX, NY, NZ), 1.0, 6.0, ((1, 16), (2, 4), (3, 8)), jnp.float32)
    density = jnp.clip(2.0 * jax.random.uniform(key_list[1], (NX, NY, NZ), jnp.float32) ** block_levels(key_list[1], (NX, NY, NZ), ((0, 16), (1, 4), (2, 8)), -0.2, 0.2), 0.0, 2.0)
    offsets = set_ends(jax.random.randint(key_list[2], (3, NX, NY, NZ), -4, 4), jax.random.fold_in(key_list[2], 1), -4, 3).astype(jnp.int32)
    eighths = set_ends(jax.random.randint(key_list[3], (3, NX, NY, NZ), 0, 8), jax.random.fold_in(key_list[3], 1), 0, 7).astype(jnp.int32)
    return dict(velocity=velocity, density=density, offsets=offsets, eighths=eighths)


RELAX_WEIGHT = 6.0 / 7.0


def neighbours(padded):
    summed = padded[2:, 1:-1, 1:-1] + padded[:-2, 1:-1, 1:-1]
    summed = summed + padded[1:-1, 2:, 1:-1] + padded[1:-1, :-2, 1:-1]
    summed = summed + padded[1:-1, 1:-1, 2:] + padded[1:-1, 1:-1, :-2]
    return summed


def operate(padded):
    return 6.0 * padded[1:-1, 1:-1, 1:-1] - neighbours(padded)


def advect_block(padded, offsets, eighths):
    field_count = padded.shape[0]
    stride_y = padded.shape[3]
    stride_x = padded.shape[2] * padded.shape[3]
    flattened = padded.reshape(field_count, -1)
    box_shape = offsets.shape[1:]
    base_x = lax.broadcasted_iota(jnp.int32, box_shape, 0) + 4 + offsets[0]
    base_y = lax.broadcasted_iota(jnp.int32, box_shape, 1) + 4 + offsets[1]
    base_z = lax.broadcasted_iota(jnp.int32, box_shape, 2) + 4 + offsets[2]
    fraction = eighths.astype(jnp.float32) / 8.0
    summed = jnp.zeros((field_count,) + box_shape, jnp.float32)
    for shift_x in (0, 1):
        weight_x = fraction[0] if shift_x else 1.0 - fraction[0]
        for shift_y in (0, 1):
            weight_y = fraction[1] if shift_y else 1.0 - fraction[1]
            for shift_z in (0, 1):
                weight_z = fraction[2] if shift_z else 1.0 - fraction[2]
                weight = weight_x * weight_y * weight_z
                position = (base_x + shift_x) * stride_x + (base_y + shift_y) * stride_y + base_z + shift_z
                picked = jnp.take(flattened, position.reshape(-1), axis=1).reshape(summed.shape)
                summed = summed + weight[None] * picked
    return summed


def divergence_of(velocity_pad):
    part_x = velocity_pad[0, 2:, 1:-1, 1:-1] - velocity_pad[0, :-2, 1:-1, 1:-1]
    part_y = velocity_pad[1, 1:-1, 2:, 1:-1] - velocity_pad[1, 1:-1, :-2, 1:-1]
    part_z = velocity_pad[2, 1:-1, 1:-1, 2:] - velocity_pad[2, 1:-1, 1:-1, :-2]
    return 0.5 * (part_x + part_y + part_z)


def gradient_of(pressure_pad):
    part_x = pressure_pad[2:, 1:-1, 1:-1] - pressure_pad[:-2, 1:-1, 1:-1]
    part_y = pressure_pad[1:-1, 2:, 1:-1] - pressure_pad[1:-1, :-2, 1:-1]
    part_z = pressure_pad[1:-1, 1:-1, 2:] - pressure_pad[1:-1, 1:-1, :-2]
    return 0.5 * jnp.stack([part_x, part_y, part_z], axis=0)


def restrict(field):
    return field.reshape(field.shape[0] // 2, 2, field.shape[1] // 2, 2, field.shape[2] // 2, 2).mean(axis=(1, 3, 5))


def prolong(field):
    return jnp.repeat(jnp.repeat(jnp.repeat(field, 2, axis=0), 2, axis=1), 2, axis=2)


def sweeps(source, spacing):
    relaxation = RELAX_WEIGHT / 6.0
    first_sweep = relaxation * spacing * source
    second_sweep = first_sweep + relaxation * (spacing * source - operate(jnp.pad(first_sweep, 1)))
    return second_sweep


def smooth_level(source, spacing):
    second_sweep = sweeps(source, spacing)
    residual = source - operate(jnp.pad(second_sweep, 1)) / spacing
    return second_sweep, residual


def reference(velocity, density, offsets, eighths):
    fields = jnp.concatenate([velocity, density[None]], axis=0)
    padded = jnp.pad(fields, ((0, 0), (4, 4), (4, 4), (4, 4)))
    advected = advect_block(padded, offsets, eighths)
    velocity_pad = jnp.pad(advected[:3], ((0, 0), (1, 1), (1, 1), (1, 1)))
    divergence = divergence_of(velocity_pad)
    fine_sweep, fine_residual = smooth_level(-divergence, 1.0)
    middle_sweep, middle_residual = smooth_level(restrict(fine_residual), 4.0)
    coarse_sweep = sweeps(restrict(middle_residual), 16.0)
    pressure = fine_sweep + prolong(middle_sweep + prolong(coarse_sweep))
    gradient = gradient_of(jnp.pad(pressure, 1))
    return advected[:3] - gradient, advected[3], pressure
```

```python
import functools

import jax
import jax.numpy as jnp
from jax import lax
from jax.experimental import pallas as pl
from jax.experimental.pallas import tpu as pltpu
from jax.sharding import PartitionSpec as P

RELAX_WEIGHT = 6.0 / 7.0
VMEM = pl.BlockSpec(memory_space=pltpu.VMEM)
SMEM = pl.BlockSpec(memory_space=pltpu.SMEM)
PARAMS = pltpu.CompilerParams(vmem_limit_bytes=48 * 1024 * 1024)


def call(kernel, outs, scratch=(), scalars=0, inputs=0):
    return pl.pallas_call(
        kernel,
        out_shape=[jax.ShapeDtypeStruct(shape, dtype) for shape, dtype in outs],
        in_specs=[SMEM] * scalars + [VMEM] * inputs,
        out_specs=[VMEM] * len(outs),
        scratch_shapes=list(scratch),
        compiler_params=PARAMS,
    )


def shift_ring(value, axis, step):
    count = lax.axis_size(axis)
    return lax.ppermute(value, axis, [(i, (i + step) % count) for i in range(count)])


def own_kernel(velocity, density, offsets, eighths, fields_t, code_t):
    for a in range(3):
        fields_t[a] = velocity[a].reshape(128, 128).T
    fields_t[3] = density[...].reshape(128, 128).T
    code = (offsets[0] + 4) + (offsets[1] + 4) * 8 + (offsets[2] + 4) * 64
    code = code + eighths[0] * 512 + eighths[1] * 4096 + eighths[2] * 32768
    code_t[...] = code.astype(jnp.float32).reshape(128, 128).T.astype(jnp.int32)


def rows_kernel(inside, velocity, density, low, high, to_low, to_high):
    for f in range(4):
        for pair in range(8):
            for half in range(2):
                plane = 2 * pair + half
                if plane < 4:
                    rows = low[f, plane] * inside[0]
                elif plane >= 12:
                    rows = high[f, plane - 12] * inside[1]
                elif f < 3:
                    rows = velocity[f, plane - 4]
                else:
                    rows = density[plane - 4]
                to_low[f, pair, 4 * half : 4 * half + 4] = rows[0:4]
                to_high[f, pair, 4 * half : 4 * half + 4] = rows[12:16]


def planes_kernel(inside, low, high, planes_t):
    for f in range(4):
        both = jnp.concatenate(
            [low[f].reshape(64, 128) * inside[0], high[f].reshape(64, 128) * inside[1]], axis=0
        )
        planes_t[f] = both.T


def columns_kernel(inside, fields_t, planes_t, low, high, rows_t, to_low, to_high):
    for f in range(4):
        both = jnp.concatenate(
            [low[f].reshape(64, 128) * inside[2], high[f].reshape(64, 128) * inside[3]], axis=0
        )
        turned = both.T
        rows_t[f] = turned
        for group, source in enumerate((fields_t[f], planes_t[f], turned)):
            to_low[f, group] = source[0:8]
            to_high[f, group] = source[120:128]


def advect_kernel(inside, code_t, fields_t, planes_t, rows_t, low, high, moved_t, moved, padded):
    for f in range(4):
        for group, source in enumerate((fields_t, planes_t, rows_t)):
            padded[f, group, 8:136] = source[f]
            padded[f, group, 0:8] = low[f, group] * inside[4]
            padded[f, group, 136:144] = high[f, group] * inside[5]

    def tile(step, carry):
        start = pl.multiple_of(step * 8, 8)
        code = code_t[pl.ds(start, 8), :]
        lane = lax.broadcasted_iota(jnp.int32, (8, 128), 1)
        x = (lane >> 4) + (code & 7)
        y = (lane & 15) + ((code >> 3) & 7)
        level = (code >> 6) & 7
        fx = ((code >> 9) & 7).astype(jnp.float32) / 8.0
        fy = ((code >> 12) & 7).astype(jnp.float32) / 8.0
        fz = ((code >> 15) & 7).astype(jnp.float32) / 8.0
        corners = []
        for cx in (0, 1):
            for cy in (0, 1):
                xc, yc = x + cx, y + cy
                low_x, high_x = xc < 4, xc >= 12
                in_rows = (yc < 4) | (yc >= 20)
                in_planes = low_x | high_x
                plane = xc - jnp.where(low_x, 0, jnp.where(high_x, 8, 4))
                by_rows = xc * 4 + (yc & 3) + jnp.where(yc >= 20, 64, 0)
                at = jnp.where(in_rows, by_rows, plane * 16 + yc - 4)
                weight = (fx if cx else 1.0 - fx) * (fy if cy else 1.0 - fy)
                corners.append((at, in_rows, in_planes, weight))
        sums = [jnp.zeros((8, 128), jnp.float32) for _ in range(4)]
        for dz in range(9):
            weight_z = jnp.where(level == dz, 1.0 - fz, jnp.where(level == dz - 1, fz, 0.0))
            for f in range(4):
                groups = [padded[f, group, pl.ds(start + (4 + dz), 8), :] for group in range(3)]
                total = None
                for at, in_rows, in_planes, weight in corners:
                    picked = [
                        jnp.take_along_axis(group, at, axis=1, mode="promise_in_bounds")
                        for group in groups
                    ]
                    value = jnp.where(
                        in_rows, picked[2], jnp.where(in_planes, picked[1], picked[0])
                    )
                    total = weight * value if total is None else total + weight * value
                sums[f] = sums[f] + weight_z * total
        for f in range(4):
            moved_t[f, pl.ds(start, 8), :] = sums[f]
        return carry

    lax.fori_loop(0, 16, tile, 0)
    for f in range(4):
        moved[f] = moved_t[f].T.reshape(8, 16, 128)


def ends(axis):
    place = lax.axis_index(axis)
    return [place > 0, place < lax.axis_size(axis) - 1]


def advect(inside, velocity, density, offsets, eighths):
    f32 = jnp.float32
    low_planes = jnp.concatenate([velocity[:, 0:4], density[None, 0:4]], axis=0)
    high_planes = jnp.concatenate([velocity[:, 4:8], density[None, 4:8]], axis=0)
    low = shift_ring(high_planes, "gx", 1)
    high = shift_ring(low_planes, "gx", -1)
    fields_t, code_t = call(
        own_kernel, [((4, 128, 128), f32), ((128, 128), jnp.int32)], inputs=4
    )(velocity, density, offsets, eighths)
    strip = ((4, 8, 8, 128), f32)
    to_low, to_high = call(rows_kernel, [strip, strip], scalars=1, inputs=4)(
        inside, velocity, density, low, high
    )
    rows_low = shift_ring(to_high, "gy", 1)
    rows_high = shift_ring(to_low, "gy", -1)
    (planes_t,) = call(planes_kernel, [((4, 128, 128), f32)], scalars=1, inputs=2)(
        inside, low, high
    )
    edge = ((4, 3, 8, 128), f32)
    rows_t, to_low, to_high = call(
        columns_kernel, [((4, 128, 128), f32), edge, edge], scalars=1, inputs=4
    )(inside, fields_t, planes_t, rows_low, rows_high)
    columns_low = shift_ring(to_high, "gz", 1)
    columns_high = shift_ring(to_low, "gz", -1)
    return call(
        advect_kernel,
        [((4, 128, 128), f32), ((4, 8, 16, 128), f32)],
        scratch=[pltpu.VMEM((4, 3, 144, 128), f32)],
        scalars=1,
        inputs=6,
    )(inside, code_t, fields_t, planes_t, rows_t, columns_low, columns_high)


def padded_2(block, sides, width):
    for axis, dim in sides:
        count = lax.axis_size(axis)
        forward = [(i, i + 1) for i in range(count - 1)]
        backward = [(target, source) for source, target in forward]
        low = lax.ppermute(
            lax.slice_in_dim(block, block.shape[dim] - width, None, axis=dim), axis, forward
        )
        high = lax.ppermute(lax.slice_in_dim(block, 0, width, axis=dim), axis, backward)
        block = jnp.concatenate([low, block, high], axis=dim)
    return block


def with_halo(value, sides, width):
    edges = {}
    for axis, dim in sides:
        peers, length = (lax.axis_size(axis), value.shape[dim])
        up = [(i, (i + 1) % peers) for i in range(peers - 1)]
        last = lax.slice_in_dim(value, length - width, length, axis=dim)
        initial = lax.slice_in_dim(value, 0, width, axis=dim)
        edges[dim] = (
            lax.ppermute(last, axis, up),
            lax.ppermute(initial, axis, [(b, a) for a, b in up]),
        )
    done = []
    for _, dim in sides:
        low, high = edges[dim]
        around = [(width, width) if d in done else (0, 0) for d in range(value.ndim)]
        value = jnp.concatenate([jnp.pad(low, around), value, jnp.pad(high, around)], axis=dim)
        done.append(dim)
    return value


def neighbours(padded):
    summed = padded[2:, 1:-1, 1:-1] + padded[:-2, 1:-1, 1:-1]
    summed = summed + padded[1:-1, 2:, 1:-1] + padded[1:-1, :-2, 1:-1]
    summed = summed + padded[1:-1, 1:-1, 2:] + padded[1:-1, 1:-1, :-2]
    return summed


def operate(padded):
    return 6.0 * padded[1:-1, 1:-1, 1:-1] - neighbours(padded)


def divergence_of(velocity_pad):
    part_x = velocity_pad[0, 2:, 1:-1, 1:-1] - velocity_pad[0, :-2, 1:-1, 1:-1]
    part_y = velocity_pad[1, 1:-1, 2:, 1:-1] - velocity_pad[1, 1:-1, :-2, 1:-1]
    part_z = velocity_pad[2, 1:-1, 1:-1, 2:] - velocity_pad[2, 1:-1, 1:-1, :-2]
    return 0.5 * (part_x + part_y + part_z)


def gradient_of(pressure_pad):
    part_x = pressure_pad[2:, 1:-1, 1:-1] - pressure_pad[:-2, 1:-1, 1:-1]
    part_y = pressure_pad[1:-1, 2:, 1:-1] - pressure_pad[1:-1, :-2, 1:-1]
    part_z = pressure_pad[1:-1, 1:-1, 2:] - pressure_pad[1:-1, 1:-1, :-2]
    return 0.5 * jnp.stack([part_x, part_y, part_z], axis=0)


def restrict(field):
    return field.reshape(
        field.shape[0] // 2, 2, field.shape[1] // 2, 2, field.shape[2] // 2, 2
    ).mean(axis=(1, 3, 5))


def prolong(field):
    return jnp.repeat(jnp.repeat(jnp.repeat(field, 2, axis=0), 2, axis=1), 2, axis=2)


def inside_box(extents, margin):
    box_shape = (extents[0] + 2 * margin, extents[1] + 2 * margin, extents[2] + 2 * margin)
    coord_x = (
        lax.broadcasted_iota(jnp.int32, box_shape, 0) - margin + lax.axis_index("gx") * extents[0]
    )
    coord_y = (
        lax.broadcasted_iota(jnp.int32, box_shape, 1) - margin + lax.axis_index("gy") * extents[1]
    )
    coord_z = (
        lax.broadcasted_iota(jnp.int32, box_shape, 2) - margin + lax.axis_index("gz") * extents[2]
    )
    inside = (coord_x >= 0) & (coord_x < extents[0] * lax.axis_size("gx"))
    inside = inside & (coord_y >= 0) & (coord_y < extents[1] * lax.axis_size("gy"))
    inside = inside & (coord_z >= 0) & (coord_z < extents[2] * lax.axis_size("gz"))
    return inside


def smooth_level(source, spacing):
    relaxation = RELAX_WEIGHT / 6.0
    source_pad = padded_2(source, (("gx", 0), ("gy", 1), ("gz", 2)), 2)
    first_sweep = relaxation * spacing * source_pad
    second_wide = first_sweep[1:-1, 1:-1, 1:-1] + relaxation * (
        spacing * source_pad[1:-1, 1:-1, 1:-1] - operate(first_sweep)
    )
    second_wide = jnp.where(inside_box(source.shape, 1), second_wide, 0.0)
    residual = source - operate(second_wide) / spacing
    second_sweep = second_wide[1:-1, 1:-1, 1:-1]
    return (second_sweep, residual)


def solve_coarse(source):
    relaxation = RELAX_WEIGHT / 6.0
    spacing = 16.0
    first_sweep = relaxation * spacing * source
    first_pad = with_halo(first_sweep, (("gx", 0), ("gy", 1), ("gz", 2)), 1)
    return first_sweep + relaxation * (spacing * source - operate(first_pad))


def body(velocity, density, offsets, eighths):
    inside = jnp.stack(ends("gx") + ends("gy") + ends("gz")).astype(jnp.float32)
    _, advected = advect(inside, velocity, density, offsets, eighths)
    new_density = advected[3]
    moved_velocity = advected[:3]
    velocity_pad = with_halo(moved_velocity, (("gx", 1), ("gy", 2), ("gz", 3)), 1)
    divergence = divergence_of(velocity_pad)
    fine_sweep, fine_residual = smooth_level(-divergence, 1.0)
    middle_sweep, middle_residual = smooth_level(restrict(fine_residual), 4.0)
    coarse_sweep = solve_coarse(restrict(middle_residual))
    pressure = fine_sweep + prolong(middle_sweep + prolong(coarse_sweep))
    pressure_pad = with_halo(pressure, (("gx", 0), ("gy", 1), ("gz", 2)), 1)
    gradient = gradient_of(pressure_pad)
    return (moved_velocity - gradient, new_density, pressure)


def solution(mesh):
    return jax.shard_map(
        body,
        mesh=mesh,
        in_specs=(
            P(None, "gx", "gy", "gz"),
            P("gx", "gy", "gz"),
            P(None, "gx", "gy", "gz"),
            P(None, "gx", "gy", "gz"),
        ),
        out_specs=(P(None, "gx", "gy", "gz"), P("gx", "gy", "gz"), P("gx", "gy", "gz")),
        check_vma=False,
    )
```

```python
import functools

import jax
import jax.numpy as jnp
from jax import lax
from jax.experimental import pallas as pl
from jax.experimental.pallas import tpu as pltpu
from jax.sharding import PartitionSpec as P

RELAX_WEIGHT = 6.0 / 7.0
VMEM = pl.BlockSpec(memory_space=pltpu.VMEM)
SMEM = pl.BlockSpec(memory_space=pltpu.SMEM)
PARAMS = pltpu.CompilerParams(vmem_limit_bytes=48 * 1024 * 1024)


def call(kernel, outs, scratch=(), scalars=0, inputs=0):
    return pl.pallas_call(
        kernel,
        out_shape=[jax.ShapeDtypeStruct(shape, dtype) for shape, dtype in outs],
        in_specs=[SMEM] * scalars + [VMEM] * inputs,
        out_specs=[VMEM] * len(outs),
        scratch_shapes=list(scratch),
        compiler_params=PARAMS,
    )


def shift_ring(value, axis, step):
    count = lax.axis_size(axis)
    return lax.ppermute(value, axis, [(i, (i + step) % count) for i in range(count)])


def own_kernel(velocity, density, offsets, eighths, fields_t, code_t):
    for a in range(3):
        fields_t[a] = velocity[a].reshape(128, 128).T
    fields_t[3] = density[...].reshape(128, 128).T
    code = (offsets[0] + 4) + (offsets[1] + 4) * 8 + (offsets[2] + 4) * 64
    code = code + eighths[0] * 512 + eighths[1] * 4096 + eighths[2] * 32768
    code_t[...] = code.astype(jnp.float32).reshape(128, 128).T.astype(jnp.int32)


def rows_kernel(inside, velocity, density, low, high, to_low, to_high):
    for f in range(4):
        for pair in range(8):
            for half in range(2):
                plane = 2 * pair + half
                if plane < 4:
                    rows = low[f, plane] * inside[0]
                elif plane >= 12:
                    rows = high[f, plane - 12] * inside[1]
                elif f < 3:
                    rows = velocity[f, plane - 4]
                else:
                    rows = density[plane - 4]
                to_low[f, pair, 4 * half : 4 * half + 4] = rows[0:4]
                to_high[f, pair, 4 * half : 4 * half + 4] = rows[12:16]


def planes_kernel(inside, low, high, planes_t):
    for f in range(4):
        both = jnp.concatenate(
            [low[f].reshape(64, 128) * inside[0], high[f].reshape(64, 128) * inside[1]], axis=0
        )
        planes_t[f] = both.T


def columns_kernel(inside, fields_t, planes_t, low, high, rows_t, to_low, to_high):
    for f in range(4):
        both = jnp.concatenate(
            [low[f].reshape(64, 128) * inside[2], high[f].reshape(64, 128) * inside[3]], axis=0
        )
        turned = both.T
        rows_t[f] = turned
        for group, source in enumerate((fields_t[f], planes_t[f], turned)):
            to_low[f, group] = source[0:8]
            to_high[f, group] = source[120:128]


def advect_kernel(inside, code_t, fields_t, planes_t, rows_t, low, high, moved_t, moved, padded):
    for f in range(4):
        for group, source in enumerate((fields_t, planes_t, rows_t)):
            padded[f, group, 8:136] = source[f]
            padded[f, group, 0:8] = low[f, group] * inside[4]
            padded[f, group, 136:144] = high[f, group] * inside[5]

    def tile(step, carry):
        start = pl.multiple_of(step * 8, 8)
        code = code_t[pl.ds(start, 8), :]
        lane = lax.broadcasted_iota(jnp.int32, (8, 128), 1)
        x = (lane >> 4) + (code & 7)
        y = (lane & 15) + ((code >> 3) & 7)
        level = (code >> 6) & 7
        fx = ((code >> 9) & 7).astype(jnp.float32) / 8.0
        fy = ((code >> 12) & 7).astype(jnp.float32) / 8.0
        fz = ((code >> 15) & 7).astype(jnp.float32) / 8.0
        corners = []
        for cx in (0, 1):
            for cy in (0, 1):
                xc, yc = x + cx, y + cy
                low_x, high_x = xc < 4, xc >= 12
                in_rows = (yc < 4) | (yc >= 20)
                in_planes = low_x | high_x
                plane = xc - jnp.where(low_x, 0, jnp.where(high_x, 8, 4))
                by_rows = xc * 4 + (yc & 3) + jnp.where(yc >= 20, 64, 0)
                at = jnp.where(in_rows, by_rows, plane * 16 + yc - 4)
                weight = (fx if cx else 1.0 - fx) * (fy if cy else 1.0 - fy)
                corners.append((at, in_rows, in_planes, weight))
        sums = [jnp.zeros((8, 128), jnp.float32) for _ in range(4)]
        for dz in range(9):
            weight_z = jnp.where(level == dz, 1.0 - fz, jnp.where(level == dz - 1, fz, 0.0))
            for f in range(4):
                groups = [padded[f, group, pl.ds(start + (4 + dz), 8), :] for group in range(3)]
                total = None
                for at, in_rows, in_planes, weight in corners:
                    picked = [
                        jnp.take_along_axis(group, at, axis=1, mode="promise_in_bounds")
                        for group in groups
                    ]
                    value = jnp.where(
                        in_rows, picked[2], jnp.where(in_planes, picked[1], picked[0])
                    )
                    total = weight * value if total is None else total + weight * value
                sums[f] = sums[f] + weight_z * total
        for f in range(4):
            moved_t[f, pl.ds(start, 8), :] = sums[f]
        return carry

    lax.fori_loop(0, 16, tile, 0)
    for f in range(4):
        moved[f] = moved_t[f].T.reshape(8, 16, 128)


def ends(axis):
    place = lax.axis_index(axis)
    return [place > 0, place < lax.axis_size(axis) - 1]


def advect(inside, velocity, density, offsets, eighths):
    f32 = jnp.float32
    low_planes = jnp.concatenate([velocity[:, 0:4], density[None, 0:4]], axis=0)
    high_planes = jnp.concatenate([velocity[:, 4:8], density[None, 4:8]], axis=0)
    low = shift_ring(high_planes, "gx", 1)
    high = shift_ring(low_planes, "gx", -1)
    fields_t, code_t = call(
        own_kernel, [((4, 128, 128), f32), ((128, 128), jnp.int32)], inputs=4
    )(velocity, density, offsets, eighths)
    strip = ((4, 8, 8, 128), f32)
    to_low, to_high = call(rows_kernel, [strip, strip], scalars=1, inputs=4)(
        inside, velocity, density, low, high
    )
    rows_low = shift_ring(to_high, "gy", 1)
    rows_high = shift_ring(to_low, "gy", -1)
    (planes_t,) = call(planes_kernel, [((4, 128, 128), f32)], scalars=1, inputs=2)(
        inside, low, high
    )
    edge = ((4, 3, 8, 128), f32)
    rows_t, to_low, to_high = call(
        columns_kernel, [((4, 128, 128), f32), edge, edge], scalars=1, inputs=4
    )(inside, fields_t, planes_t, rows_low, rows_high)
    columns_low = shift_ring(to_high, "gz", 1)
    columns_high = shift_ring(to_low, "gz", -1)
    return call(
        advect_kernel,
        [((4, 128, 128), f32), ((4, 8, 16, 128), f32)],
        scratch=[pltpu.VMEM((4, 3, 144, 128), f32)],
        scalars=1,
        inputs=6,
    )(inside, code_t, fields_t, planes_t, rows_t, columns_low, columns_high)


def roll(value, shift, dim):
    return pltpu.roll(value, shift % value.shape[dim], dim)


def neighbours(value):
    none = jnp.zeros_like(value[:1])
    summed = jnp.concatenate([value[1:], none], axis=0) + jnp.concatenate([none, value[:-1]], axis=0)
    summed = summed + roll(value, -1, 1) + roll(value, 1, 1)
    return summed + roll(value, -1, 2) + roll(value, 1, 2)


def grid_mask(inside, planes, rows, lanes):
    shape = (rows[0], lanes[0])
    row = lax.broadcasted_iota(jnp.int32, shape, 0)
    lane = lax.broadcasted_iota(jnp.int32, shape, 1)
    by_row = jnp.where(
        row < rows[1], 1.0, jnp.where(row < (rows[0] + rows[1]) // 2, inside[3], inside[2])
    )
    by_lane = jnp.where(
        lane < lanes[1], 1.0, jnp.where(lane < (lanes[0] + lanes[1]) // 2, inside[5], inside[4])
    )
    both = by_row * by_lane
    first, count, block = planes
    parts = [
        both * inside[0] if x < 0 else (both * inside[1] if x >= block else both)
        for x in range(first, first + count)
    ]
    return jnp.stack(parts, axis=0)


def smooth(source, spacing, mask, want_residual):
    relaxation = RELAX_WEIGHT / 6.0
    first = relaxation * spacing * source
    second = first + relaxation * (spacing * source - (6.0 * first - neighbours(first)))
    second = second * mask
    if not want_residual:
        return second
    residual = source - (6.0 * second - neighbours(second)) / spacing
    return second, residual * mask


def pick_lanes(value, index):
    parts = [
        jnp.take_along_axis(value[r : r + 8], index, axis=1, mode="promise_in_bounds")
        for r in range(0, value.shape[0], 8)
    ]
    return jnp.concatenate(parts, axis=0)


def lane_numbers(rows):
    return lax.broadcasted_iota(jnp.int32, (rows, 128), 1)


def row_numbers(rows):
    return lax.broadcasted_iota(jnp.int32, (rows, 128), 0)


def pair_sum(value):
    value = value + roll(value, -1, 1)
    return value + roll(value, -1, 2)


def restrict_fine(residual, halves):
    lane = lane_numbers(8)
    index = (lane * 2) & 127
    left = lane_numbers(16) < 64
    row = row_numbers(8)
    planes = []
    pairs = pair_sum(
        jnp.stack([residual[2 * p] + residual[2 * p + 1] for p in range(8)], axis=0)
    )
    for p in range(8):
        even = []
        for side in range(2):
            both = pairs[p, :, 128 * side : 128 * side + 128]
            halves[side, p, 0:16] = both[0:16]
            halves[side, p, 16:24] = jnp.where(row < 4, both[16:24], 0.0)
            halves[side, p, 24:32] = jnp.where(row >= 4, both[16:24], 0.0)
            even.append(pick_lanes(halves[side, p, pl.ds(0, 16, stride=2), :], index))
        planes.append(jnp.where(left, even[0], even[1]))
    return jnp.stack(planes, axis=0) * 0.125


def restrict_middle(residual, halves):
    index = (lane_numbers(8) * 2) & 127
    row, lane = row_numbers(16), lane_numbers(16)
    valid = ((row < 6) | (row >= 14)) & ((lane < 36) | (lane >= 124))
    pairs = pair_sum(
        jnp.stack([residual[2 * p] + residual[2 * p + 1] for p in range(6)], axis=0)
    )
    planes = []
    for p in range(6):
        halves[0, p, 0:16] = pairs[p]
        even = pick_lanes(halves[0, p, pl.ds(0, 8, stride=2), :], index)
        planes.append(jnp.where(valid, jnp.concatenate([even, even], axis=0), 0.0))
    return jnp.stack(planes, axis=0) * 0.125


def with_planes(value, count):
    none = jnp.zeros((count,) + value.shape[1:], value.dtype)
    return jnp.concatenate([none, value, none], axis=0)


def levels_kernel(
    inside, moved, to_low, to_high, to_low_2, to_high_2, fine, middle, coarse, halves
):
    def spread(a):
        block = jnp.concatenate([moved[a], jnp.zeros((8, 8, 128), jnp.float32)], axis=1)
        block = jnp.concatenate([block, jnp.zeros((8, 24, 128), jnp.float32)], axis=2)
        return with_planes(block, 4)

    u = spread(0)
    none = jnp.zeros_like(u[:1])
    slope = jnp.concatenate([u[1:], none], axis=0) - jnp.concatenate([none, u[:-1]], axis=0)
    u = spread(1)
    slope = slope + (roll(u, -1, 1) - roll(u, 1, 1))
    u = spread(2)
    slope = slope + (roll(u, -1, 2) - roll(u, 1, 2))
    mask = grid_mask(inside, (-4, 16, 8), (24, 16), (256, 128))
    second, residual = smooth(slope * mask * -0.5, 1.0, mask, True)
    mask = grid_mask(inside, (-4, 12, 4), (16, 8), (128, 64))
    source = with_planes(restrict_fine(residual, halves), 2)
    second_1, residual = smooth(source, 4.0, mask, True)
    mask = grid_mask(inside, (-3, 8, 2), (16, 4), (128, 32))
    source = with_planes(restrict_middle(residual, halves), 1)
    second_2 = smooth(source, 16.0, mask, False)
    fine[...] = second[3:13]
    middle[...] = second_1[3:9]
    coarse[...] = second_2[2:6]
    for out, at_0, at_1, at_2 in ((to_high, 11, 7, 4), (to_low, 2, 1, 0)):
        sides = None
        for k in range(3):
            out[24 * k : 24 * k + 24] = second[at_0 + k][:, 0:128]
            side = roll(second[at_0 + k][:, 128:256], 16 * k, 1)
            sides = side if sides is None else sides + side
        out[72:96] = sides
        for k in range(4):
            out[96 + 16 * k : 112 + 16 * k] = second_1[at_1 + k] + roll(second_2[at_2 + k], 80, 1)
    for k in range(2):
        to_high_2[16 * k : 16 * k + 16] = second_2[6 + k]
        to_low_2[16 * k : 16 * k + 16] = second_2[k]


def near_end(lane):
    return (lane < 8) | (lane >= 120)


def split_levels(both):
    lane = lane_numbers(both.shape[0])
    middle = jnp.where((lane < 72) | (lane >= 120), both, 0.0)
    coarse = jnp.where((lane >= 72) & (lane < 120), both, 0.0)
    return middle, roll(coarse, -80, 1)


def planes_sum_kernel(
    inside, fine, middle, coarse, low, high, low_2, high_2, to_low, to_high, fine_o, middle_o, coarse_o
):
    f = [fine[k] for k in range(10)]
    m = [middle[k] for k in range(6)]
    c = [coarse[k] for k in range(4)]
    lane = lane_numbers(24)
    for got, flag, at_0, at_1 in ((low, inside[0], 0, 0), (high, inside[1], 7, 2)):
        sides = got[72:96] * flag
        for k in range(3):
            side = jnp.where(near_end(lane), roll(sides, -16 * k, 1), 0.0)
            centre = got[24 * k : 24 * k + 24] * flag
            f[at_0 + k] = f[at_0 + k] + jnp.concatenate([centre, side], axis=1)
        for k in range(4):
            add_m, add_c = split_levels(got[96 + 16 * k : 112 + 16 * k] * flag)
            m[at_1 + k] = m[at_1 + k] + add_m
            c[k] = c[k] + add_c
    for k in range(2):
        c[k] = c[k] + low_2[16 * k : 16 * k + 16] * inside[6]
        c[2 + k] = c[2 + k] + high_2[16 * k : 16 * k + 16] * inside[7]
    c[0], c[3] = c[0] * inside[0], c[3] * inside[1]
    for k in range(10):
        fine_o[k] = f[k]
    for k in range(6):
        middle_o[k] = m[k]
    for k in range(4):
        coarse_o[k] = c[k]
    for out, at_0, at_1, at_2 in ((to_high, 15, 7, 3), (to_low, -2, -3, -3)):
        sides = None
        for k in range(10):
            rows = roll(f[k], -at_0, 0)[0:8]
            out[4 * k : 4 * k + 4] = rows[0:4, 0:128]
            side = roll(jnp.where(near_end(lane_numbers(8)), rows[:, 128:256], 0.0), 8 + 12 * k, 1)
            sides = side if sides is None else sides + side
        out[40:48] = sides
        for k in range(6):
            rows = roll(m[k], -at_1, 0)[0:8]
            if k < 4:
                rows = rows + roll(roll(c[k], -at_2, 0)[0:8], 80, 1)
            out[48 + 4 * k : 52 + 4 * k] = rows[0:4]


def rows_sum_kernel(
    inside, fine, middle, coarse, low, high, to_low, to_high, fine_o, middle_o, coarse_o
):
    f = [fine[k] for k in range(10)]
    m = [middle[k] for k in range(6)]
    c = [coarse[k] for k in range(4)]
    row = row_numbers(8)

    def place(rows, count, first):
        none = jnp.zeros((count - 8,) + rows.shape[1:], jnp.float32)
        return roll(jnp.concatenate([rows, none], axis=0), first, 0)

    def four(got, at, flag):
        tile = got[at - at % 8 : at - at % 8 + 8] * flag
        tile = roll(tile, -4, 0) if at % 8 else tile
        return jnp.where(row < 4, tile, 0.0)

    for got, flag, at_0, at_1, at_2 in (
        (low, inside[2], -1, -1, -1),
        (high, inside[3], 14, 5, 1),
    ):
        sides = jnp.where(row < 3, got[40:48] * flag, 0.0)
        for k in range(10):
            side = jnp.where(four_lanes(8), roll(sides, -(8 + 12 * k), 1), 0.0)
            rows = jnp.where(row < 3, four(got, 4 * k, flag), 0.0)
            f[k] = f[k] + place(jnp.concatenate([rows, side], axis=1), 24, at_0)
        for k in range(6):
            add_m, add_c = split_levels(four(got, 48 + 4 * k, flag))
            m[k] = m[k] + place(add_m, 16, at_1)
            if k < 4:
                c[k] = c[k] + place(add_c, 16, at_2)
    for k in range(10):
        fine_o[k] = f[k]
    for k in range(6):
        middle_o[k] = m[k]
    for k in range(4):
        coarse_o[k] = c[k]
    lane = lane_numbers(24)
    lane_16 = lane_numbers(16)
    none = jnp.zeros((8, 128), jnp.float32)

    def strip(value, first, count, at):
        lanes = lane_numbers(value.shape[0])
        moved = roll(value, at - first, 1)
        return jnp.where((lanes >= at) & (lanes < at + count), moved, 0.0)

    for out, at_0, at_1, at_2 in ((to_high, 127, 63, 31), (to_low, 126, 125, 125)):
        total = jnp.zeros((24, 128), jnp.float32)
        for k in range(10):
            own = lane == 127 if at_0 == 127 else lane == 0
            total = total + strip(jnp.where(own, f[k][:, 0:128], f[k][:, 128:256]), at_0, 3, 4 * k)
        part = jnp.zeros((16, 128), jnp.float32)
        for k in range(6):
            part = part + strip(m[k], at_1, 4, 40 + 4 * k)
        for k in range(4):
            part = part + strip(c[k], at_2, 4, 64 + 4 * k)
        out[...] = total + jnp.concatenate([part, none], axis=0)


def four_lanes(rows):
    lane = lane_numbers(rows)
    return (lane < 4) | (lane >= 124)


def pressure_kernel(inside, moved, fine, middle, coarse, low, high, velocity, pressure, halves):
    f = [fine[k] for k in range(10)]
    m = [middle[k] for k in range(6)]
    c = [coarse[k] for k in range(4)]

    def strip(value, at, count, first):
        lanes = lane_numbers(value.shape[0])
        kept = jnp.where((lanes >= at) & (lanes < at + count), value, 0.0)
        return roll(kept, first - at, 1)

    lane = lane_numbers(24)
    for got, flag, at_0, at_1, at_2 in (
        (low, inside[4], -1, -1, -1),
        (high, inside[5], 126, 61, 29),
    ):
        whole = got[...] * flag
        part = whole[0:16]
        for k in range(10):
            add = strip(whole, 4 * k, 3, at_0)
            own = (lane < 64) if at_0 < 0 else (lane >= 64)
            add = jnp.concatenate([jnp.where(own, add, 0.0), jnp.where(own, 0.0, add)], axis=1)
            f[k] = f[k] + add
        for k in range(6):
            m[k] = m[k] + strip(part, 40 + 4 * k, 4, at_1)
        for k in range(4):
            c[k] = c[k] + strip(part, 64 + 4 * k, 4, at_2)
    row = row_numbers(8)
    lane = lane_numbers(8)
    to_middle = (lane >> 1) + jnp.where(lane < 96, 0, 64)
    for k in range(4):
        wide = pick_lanes(c[k], to_middle)
        halves[0, k, pl.ds(0, 16, stride=2), :] = wide
        halves[0, k, pl.ds(1, 16, stride=2), :] = wide
    for k in range(6):
        at = (k + 1) // 2
        tail = jnp.where(row < 4, halves[0, at, 8:16], halves[0, at, 24:32])
        m[k] = m[k] + jnp.concatenate([halves[0, at, 0:8], tail], axis=0)
    to_centre = lane >> 1
    to_side = to_centre + 64
    for k in range(6):
        for side, index in enumerate((to_centre, to_side)):
            wide = pick_lanes(m[k], index)
            halves[side, k, pl.ds(0, 16, stride=2), :] = wide
            halves[side, k, pl.ds(1, 16, stride=2), :] = wide
    for k in range(10):
        at = (k + 1) // 2
        sides = []
        for side in range(2):
            tail = jnp.where(row < 4, halves[side, at, 16:24], halves[side, at, 24:32])
            sides.append(jnp.concatenate([halves[side, at, 0:16], tail], axis=0))
        f[k] = f[k] + jnp.concatenate(sides, axis=1)
    for k in range(8):
        here = f[k + 1]
        pressure[k] = here[0:16, 0:128]
        velocity[0, k] = moved[0, k] - 0.5 * (f[k + 2][0:16, 0:128] - f[k][0:16, 0:128])
        slope = roll(here, -1, 0) - roll(here, 1, 0)
        velocity[1, k] = moved[1, k] - 0.5 * slope[0:16, 0:128]
        here = here[0:16]
        slope = roll(here, -1, 1) - roll(here, 1, 1)
        velocity[2, k] = moved[2, k] - 0.5 * slope[:, 0:128]


def project(inside, moved):
    f32 = jnp.float32
    held = [((10, 24, 256), f32), ((6, 16, 128), f32), ((4, 16, 128), f32)]
    halves = [pltpu.VMEM((2, 8, 32, 128), f32)]
    side, side_2 = ((160, 128), f32), ((32, 128), f32)
    to_low, to_high, to_low_2, to_high_2, *sums = call(
        levels_kernel, [side, side, side_2, side_2] + held, halves, scalars=1, inputs=1
    )(inside, moved)
    low = shift_ring(to_high, "gx", 1)
    high = shift_ring(to_low, "gx", -1)
    low_2 = shift_ring(to_high_2, "gx", 2)
    high_2 = shift_ring(to_low_2, "gx", -2)
    side = ((72, 128), f32)
    to_low, to_high, *sums = call(
        planes_sum_kernel, [side, side] + held, scalars=1, inputs=7
    )(inside, *sums, low, high, low_2, high_2)
    low = shift_ring(to_high, "gy", 1)
    high = shift_ring(to_low, "gy", -1)
    side = ((24, 128), f32)
    to_low, to_high, *sums = call(rows_sum_kernel, [side, side] + held, scalars=1, inputs=5)(
        inside, *sums, low, high
    )
    low = shift_ring(to_high, "gz", 1)
    high = shift_ring(to_low, "gz", -1)
    return call(
        pressure_kernel,
        [((3, 8, 16, 128), f32), ((8, 16, 128), f32)],
        halves,
        scalars=1,
        inputs=6,
    )(inside, moved, *sums, low, high)


def body(velocity, density, offsets, eighths):
    place = lax.axis_index("gx")
    beyond = [place > 1, place < lax.axis_size("gx") - 2]
    inside = jnp.stack(ends("gx") + ends("gy") + ends("gz") + beyond).astype(jnp.float32)
    _, moved = advect(inside, velocity, density, offsets, eighths)
    new_velocity, pressure = project(inside, moved)
    return new_velocity, moved[3], pressure


def solution(mesh):
    return jax.shard_map(
        body,
        mesh=mesh,
        in_specs=(
            P(None, "gx", "gy", "gz"),
            P("gx", "gy", "gz"),
            P(None, "gx", "gy", "gz"),
            P(None, "gx", "gy", "gz"),
        ),
        out_specs=(P(None, "gx", "gy", "gz"), P("gx", "gy", "gz"), P("gx", "gy", "gz")),
        check_vma=False,
    )
```

```python
import functools

import jax
import jax.numpy as jnp
from jax import lax
from jax.experimental import pallas as pl
from jax.experimental.pallas import tpu as pltpu
from jax.sharding import PartitionSpec as P

RELAX_WEIGHT = 6.0 / 7.0
VMEM = pl.BlockSpec(memory_space=pltpu.VMEM)
SMEM = pl.BlockSpec(memory_space=pltpu.SMEM)
PARAMS = pltpu.CompilerParams(vmem_limit_bytes=48 * 1024 * 1024)


def call(kernel, outs, scratch=(), scalars=0, inputs=0):
    return pl.pallas_call(
        kernel,
        out_shape=[jax.ShapeDtypeStruct(shape, dtype) for shape, dtype in outs],
        in_specs=[SMEM] * scalars + [VMEM] * inputs,
        out_specs=[VMEM] * len(outs),
        scratch_shapes=list(scratch),
        compiler_params=PARAMS,
    )


def shift_ring(value, axis, step):
    count = lax.axis_size(axis)
    return lax.ppermute(value, axis, [(i, (i + step) % count) for i in range(count)])


def pack_kernel(velocity, density, low_planes, high_planes):
    for f in range(4):
        field = velocity[f] if f < 3 else density[...]
        low_planes[f] = field[0:4]
        high_planes[f] = field[4:8]


def own_kernel(velocity, density, offsets, eighths, fields_t, code_t):
    for a in range(3):
        fields_t[a] = velocity[a].reshape(128, 128).T
    fields_t[3] = density[...].reshape(128, 128).T
    code = (offsets[0] + 4) + (offsets[1] + 4) * 8 + (offsets[2] + 4) * 64
    code = code + eighths[0] * 512 + eighths[1] * 4096 + eighths[2] * 32768
    code_t[...] = code.astype(jnp.float32).reshape(128, 128).T.astype(jnp.int32)


def rows_kernel(inside, velocity, density, low, high, after, to_low, to_high):
    for f in range(4):
        for pair in range(8):
            for half in range(2):
                plane = 2 * pair + half
                if plane < 4:
                    rows = low[f, plane] * inside[0]
                elif plane >= 12:
                    rows = high[f, plane - 12] * inside[1]
                elif f < 3:
                    rows = velocity[f, plane - 4]
                else:
                    rows = density[plane - 4]
                to_low[f, pair, 4 * half : 4 * half + 4] = rows[0:4]
                to_high[f, pair, 4 * half : 4 * half + 4] = rows[12:16]


def planes_kernel(inside, low, high, planes_t):
    for f in range(4):
        both = jnp.concatenate(
            [low[f].reshape(64, 128) * inside[0], high[f].reshape(64, 128) * inside[1]], axis=0
        )
        planes_t[f] = both.T


def columns_kernel(inside, fields_t, planes_t, low, high, after, rows_t, to_low, to_high):
    for f in range(4):
        both = jnp.concatenate(
            [low[f].reshape(64, 128) * inside[2], high[f].reshape(64, 128) * inside[3]], axis=0
        )
        turned = both.T
        rows_t[f] = turned
        for group, source in enumerate((fields_t[f], planes_t[f], turned)):
            to_low[f, group] = source[0:8]
            to_high[f, group] = source[120:128]


def corners_of(code):
    lane = lax.broadcasted_iota(jnp.int32, (8, 128), 1)
    x = (lane >> 4) + (code & 7)
    y = (lane & 15) + ((code >> 3) & 7)
    fx = ((code >> 9) & 7).astype(jnp.float32) / 8.0
    fy = ((code >> 12) & 7).astype(jnp.float32) / 8.0
    corners = []
    for cx in (0, 1):
        for cy in (0, 1):
            xc, yc = x + cx, y + cy
            low_x, high_x = xc < 4, xc >= 12
            in_rows = (yc < 4) | (yc >= 20)
            in_planes = low_x | high_x
            plane = xc - jnp.where(low_x, 0, jnp.where(high_x, 8, 4))
            by_rows = xc * 4 + (yc & 3) + jnp.where(yc >= 20, 64, 0)
            at = jnp.where(in_rows, by_rows, plane * 16 + yc - 4)
            weight = (fx if cx else 1.0 - fx) * (fy if cy else 1.0 - fy)
            in_block = jnp.where(in_rows, 0.0, weight)
            weights = (
                jnp.where(in_planes, 0.0, in_block),
                jnp.where(in_planes, in_block, 0.0),
                jnp.where(in_rows, weight, 0.0),
            )
            corners.append((at, weights))
    return corners


def weights_z(code, shifts):
    level = (code >> 6) & 7
    fz = ((code >> 15) & 7).astype(jnp.float32) / 8.0
    return [
        jnp.where(level == dz, 1.0 - fz, jnp.where(level == dz - 1, fz, 0.0)) for dz in shifts
    ]


def gathered(at, weights, rows_of):
    parts = [None] * 4
    for shift, weight in enumerate(weights):
        for f in range(4):
            taken = jnp.take_along_axis(
                rows_of(f, shift), at, axis=1, mode="promise_in_bounds"
            )
            parts[f] = weight * taken if shift == 0 else parts[f] + weight * taken
    return parts


def group_kernel(group, code_t, source_t, *refs):
    before, (after, padded) = refs[:-2], refs[-2:]
    none = jnp.zeros((8, 128), jnp.float32)
    for f in range(4):
        padded[f, 8:136] = source_t[f]
        padded[f, 0:8] = none
        padded[f, 136:144] = none

    def tile(step, carry):
        start = pl.multiple_of(step * 8, 8)
        code = code_t[pl.ds(start, 8), :]
        by_shift = weights_z(code, range(9))
        sums = [before[0][f, pl.ds(start, 8), :] if before else none for f in range(4)]
        for at, weights in corners_of(code):
            parts = gathered(at, by_shift, lambda f, dz: padded[f, pl.ds(start + (4 + dz), 8), :])
            for f in range(4):
                sums[f] = sums[f] + weights[group] * parts[f]
        for f in range(4):
            after[f, pl.ds(start, 8), :] = sums[f]
        return carry

    lax.fori_loop(0, 16, tile, 0)


def edges_kernel(inside, code_t, sums_t, low, high, moved, moved_t, padded):
    none = jnp.zeros((8, 128), jnp.float32)
    for f in range(4):
        moved_t[f] = sums_t[f]
        for group in range(3):
            padded[0, f, group, 0:8] = low[f, group] * inside[4]
            padded[0, f, group, 8:16] = none
            padded[1, f, group, 0:8] = none
            padded[1, f, group, 8:16] = high[f, group] * inside[5]
    for end, start, first, shifts in ((0, 0, 4, range(0, 4)), (1, 120, 1, range(5, 9))):
        code = code_t[start : start + 8]
        by_shift = weights_z(code, shifts)
        sums = [sums_t[f, start : start + 8] for f in range(4)]
        for at, weights in corners_of(code):
            for group in range(3):
                parts = gathered(
                    at, by_shift, lambda f, k: padded[end, f, group, first + k : first + k + 8]
                )
                for f in range(4):
                    sums[f] = sums[f] + weights[group] * parts[f]
        for f in range(4):
            moved_t[f, start : start + 8] = sums[f]
    for f in range(4):
        moved[f] = moved_t[f].T.reshape(8, 16, 128)


def ends(axis):
    place = lax.axis_index(axis)
    return [place > 0, place < lax.axis_size(axis) - 1]


def advect(inside, velocity, density, offsets, eighths):
    f32 = jnp.float32
    turned = ((4, 128, 128), f32)

    def gather(group, *values):
        padded = [pltpu.VMEM((4, 144, 128), f32)]
        kernel = functools.partial(group_kernel, group)
        return call(kernel, [turned], padded, inputs=len(values))(*values)[0]

    planes = ((4, 4, 16, 128), f32)
    low_planes, high_planes = call(pack_kernel, [planes, planes], inputs=2)(velocity, density)
    low = shift_ring(high_planes, "gx", 1)
    high = shift_ring(low_planes, "gx", -1)
    fields_t, code_t = call(own_kernel, [turned, ((128, 128), jnp.int32)], inputs=4)(
        velocity, density, offsets, eighths
    )
    sums_t = gather(0, code_t, fields_t)
    strip = ((4, 8, 8, 128), f32)
    to_low, to_high = call(rows_kernel, [strip, strip], scalars=1, inputs=5)(
        inside, velocity, density, low, high, sums_t
    )
    rows_low = shift_ring(to_high, "gy", 1)
    rows_high = shift_ring(to_low, "gy", -1)
    (planes_t,) = call(planes_kernel, [turned], scalars=1, inputs=2)(inside, low, high)
    sums_t = gather(1, code_t, planes_t, sums_t)
    edge = ((4, 3, 8, 128), f32)
    rows_t, to_low, to_high = call(
        columns_kernel, [turned, edge, edge], scalars=1, inputs=5
    )(inside, fields_t, planes_t, rows_low, rows_high, sums_t)
    columns_low = shift_ring(to_high, "gz", 1)
    columns_high = shift_ring(to_low, "gz", -1)
    sums_t = gather(2, code_t, rows_t, sums_t)
    scratch = [pltpu.VMEM((4, 128, 128), f32), pltpu.VMEM((2, 4, 3, 16, 128), f32)]
    return call(edges_kernel, [((4, 8, 16, 128), f32)], scratch, scalars=1, inputs=4)(
        inside, code_t, sums_t, columns_low, columns_high
    )[0]


def roll(value, shift, dim):
    return pltpu.roll(value, shift % value.shape[dim], dim)


def neighbours(value):
    none = jnp.zeros_like(value[:1])
    summed = jnp.concatenate([value[1:], none], axis=0) + jnp.concatenate([none, value[:-1]], axis=0)
    summed = summed + roll(value, -1, 1) + roll(value, 1, 1)
    return summed + roll(value, -1, 2) + roll(value, 1, 2)


def grid_mask(inside, planes, rows, lanes):
    shape = (rows[0], lanes[0])
    row = lax.broadcasted_iota(jnp.int32, shape, 0)
    lane = lax.broadcasted_iota(jnp.int32, shape, 1)
    by_row = jnp.where(
        row < rows[1], 1.0, jnp.where(row < (rows[0] + rows[1]) // 2, inside[3], inside[2])
    )
    by_lane = jnp.where(
        lane < lanes[1], 1.0, jnp.where(lane < (lanes[0] + lanes[1]) // 2, inside[5], inside[4])
    )
    both = by_row * by_lane
    first, count, block = planes
    parts = [
        both * inside[0] if x < 0 else (both * inside[1] if x >= block else both)
        for x in range(first, first + count)
    ]
    return jnp.stack(parts, axis=0)


def smooth(source, spacing, mask, want_residual):
    relaxation = RELAX_WEIGHT / 6.0
    first = relaxation * spacing * source
    second = first + relaxation * (spacing * source - (6.0 * first - neighbours(first)))
    second = second * mask
    if not want_residual:
        return second
    residual = source - (6.0 * second - neighbours(second)) / spacing
    return second, residual * mask


def pick_lanes(value, index):
    parts = [
        jnp.take_along_axis(value[r : r + 8], index, axis=1, mode="promise_in_bounds")
        for r in range(0, value.shape[0], 8)
    ]
    return jnp.concatenate(parts, axis=0)


def lane_numbers(rows):
    return lax.broadcasted_iota(jnp.int32, (rows, 128), 1)


def row_numbers(rows):
    return lax.broadcasted_iota(jnp.int32, (rows, 128), 0)


def pair_sum(value):
    value = value + roll(value, -1, 1)
    return value + roll(value, -1, 2)


def restrict_fine(residual, halves):
    lane = lane_numbers(8)
    index = (lane * 2) & 127
    left = lane_numbers(16) < 64
    row = row_numbers(8)
    planes = []
    pairs = pair_sum(
        jnp.stack([residual[2 * p] + residual[2 * p + 1] for p in range(8)], axis=0)
    )
    for p in range(8):
        even = []
        for side in range(2):
            both = pairs[p, :, 128 * side : 128 * side + 128]
            halves[side, p, 0:16] = both[0:16]
            halves[side, p, 16:24] = jnp.where(row < 4, both[16:24], 0.0)
            halves[side, p, 24:32] = jnp.where(row >= 4, both[16:24], 0.0)
            even.append(pick_lanes(halves[side, p, pl.ds(0, 16, stride=2), :], index))
        planes.append(jnp.where(left, even[0], even[1]))
    return jnp.stack(planes, axis=0) * 0.125


def restrict_middle(residual, halves):
    index = (lane_numbers(8) * 2) & 127
    row, lane = row_numbers(16), lane_numbers(16)
    valid = ((row < 6) | (row >= 14)) & ((lane < 36) | (lane >= 124))
    pairs = pair_sum(
        jnp.stack([residual[2 * p] + residual[2 * p + 1] for p in range(6)], axis=0)
    )
    planes = []
    for p in range(6):
        halves[0, p, 0:16] = pairs[p]
        even = pick_lanes(halves[0, p, pl.ds(0, 8, stride=2), :], index)
        planes.append(jnp.where(valid, jnp.concatenate([even, even], axis=0), 0.0))
    return jnp.stack(planes, axis=0) * 0.125


def with_planes(value, count):
    none = jnp.zeros((count,) + value.shape[1:], value.dtype)
    return jnp.concatenate([none, value, none], axis=0)


def levels_kernel(
    inside, moved, to_low, to_high, to_low_2, to_high_2, fine, middle, coarse, halves
):
    def spread(a):
        block = jnp.concatenate([moved[a], jnp.zeros((8, 8, 128), jnp.float32)], axis=1)
        block = jnp.concatenate([block, jnp.zeros((8, 24, 128), jnp.float32)], axis=2)
        return with_planes(block, 4)

    u = spread(0)
    none = jnp.zeros_like(u[:1])
    slope = jnp.concatenate([u[1:], none], axis=0) - jnp.concatenate([none, u[:-1]], axis=0)
    u = spread(1)
    slope = slope + (roll(u, -1, 1) - roll(u, 1, 1))
    u = spread(2)
    slope = slope + (roll(u, -1, 2) - roll(u, 1, 2))
    mask = grid_mask(inside, (-4, 16, 8), (24, 16), (256, 128))
    second, residual = smooth(slope * mask * -0.5, 1.0, mask, True)
    mask = grid_mask(inside, (-4, 12, 4), (16, 8), (128, 64))
    source = with_planes(restrict_fine(residual, halves), 2)
    second_1, residual = smooth(source, 4.0, mask, True)
    mask = grid_mask(inside, (-3, 8, 2), (16, 4), (128, 32))
    source = with_planes(restrict_middle(residual, halves), 1)
    second_2 = smooth(source, 16.0, mask, False)
    fine[...] = second[3:13]
    middle[...] = second_1[3:9]
    coarse[...] = second_2[2:6]
    for out, at_0, at_1, at_2 in ((to_high, 11, 7, 4), (to_low, 2, 1, 0)):
        sides = None
        for k in range(3):
            out[24 * k : 24 * k + 24] = second[at_0 + k][:, 0:128]
            side = roll(second[at_0 + k][:, 128:256], 16 * k, 1)
            sides = side if sides is None else sides + side
        out[72:96] = sides
        for k in range(4):
            out[96 + 16 * k : 112 + 16 * k] = second_1[at_1 + k] + roll(second_2[at_2 + k], 80, 1)
    for k in range(2):
        to_high_2[16 * k : 16 * k + 16] = second_2[6 + k]
        to_low_2[16 * k : 16 * k + 16] = second_2[k]


def near_end(lane):
    return (lane < 8) | (lane >= 120)


def split_levels(both):
    lane = lane_numbers(both.shape[0])
    middle = jnp.where((lane < 72) | (lane >= 120), both, 0.0)
    coarse = jnp.where((lane >= 72) & (lane < 120), both, 0.0)
    return middle, roll(coarse, -80, 1)


def planes_sum_kernel(
    inside, fine, middle, coarse, low, high, low_2, high_2, to_low, to_high, fine_o, middle_o, coarse_o
):
    f = [fine[k] for k in range(10)]
    m = [middle[k] for k in range(6)]
    c = [coarse[k] for k in range(4)]
    lane = lane_numbers(24)
    for got, flag, at_0, at_1 in ((low, inside[0], 0, 0), (high, inside[1], 7, 2)):
        sides = got[72:96] * flag
        for k in range(3):
            side = jnp.where(near_end(lane), roll(sides, -16 * k, 1), 0.0)
            centre = got[24 * k : 24 * k + 24] * flag
            f[at_0 + k] = f[at_0 + k] + jnp.concatenate([centre, side], axis=1)
        for k in range(4):
            add_m, add_c = split_levels(got[96 + 16 * k : 112 + 16 * k] * flag)
            m[at_1 + k] = m[at_1 + k] + add_m
            c[k] = c[k] + add_c
    for k in range(2):
        c[k] = c[k] + low_2[16 * k : 16 * k + 16] * inside[6]
        c[2 + k] = c[2 + k] + high_2[16 * k : 16 * k + 16] * inside[7]
    c[0], c[3] = c[0] * inside[0], c[3] * inside[1]
    for k in range(10):
        fine_o[k] = f[k]
    for k in range(6):
        middle_o[k] = m[k]
    for k in range(4):
        coarse_o[k] = c[k]
    for out, at_0, at_1, at_2 in ((to_high, 15, 7, 3), (to_low, -2, -3, -3)):
        sides = None
        for k in range(10):
            rows = roll(f[k], -at_0, 0)[0:8]
            out[4 * k : 4 * k + 4] = rows[0:4, 0:128]
            side = roll(jnp.where(near_end(lane_numbers(8)), rows[:, 128:256], 0.0), 8 + 12 * k, 1)
            sides = side if sides is None else sides + side
        out[40:48] = sides
        for k in range(6):
            rows = roll(m[k], -at_1, 0)[0:8]
            if k < 4:
                rows = rows + roll(roll(c[k], -at_2, 0)[0:8], 80, 1)
            out[48 + 4 * k : 52 + 4 * k] = rows[0:4]


def rows_sum_kernel(
    inside, fine, middle, coarse, low, high, to_low, to_high, fine_o, middle_o, coarse_o
):
    f = [fine[k] for k in range(10)]
    m = [middle[k] for k in range(6)]
    c = [coarse[k] for k in range(4)]
    row = row_numbers(8)

    def place(rows, count, first):
        none = jnp.zeros((count - 8,) + rows.shape[1:], jnp.float32)
        return roll(jnp.concatenate([rows, none], axis=0), first, 0)

    def four(got, at, flag):
        tile = got[at - at % 8 : at - at % 8 + 8] * flag
        tile = roll(tile, -4, 0) if at % 8 else tile
        return jnp.where(row < 4, tile, 0.0)

    for got, flag, at_0, at_1, at_2 in (
        (low, inside[2], -1, -1, -1),
        (high, inside[3], 14, 5, 1),
    ):
        sides = jnp.where(row < 3, got[40:48] * flag, 0.0)
        for k in range(10):
            side = jnp.where(four_lanes(8), roll(sides, -(8 + 12 * k), 1), 0.0)
            rows = jnp.where(row < 3, four(got, 4 * k, flag), 0.0)
            f[k] = f[k] + place(jnp.concatenate([rows, side], axis=1), 24, at_0)
        for k in range(6):
            add_m, add_c = split_levels(four(got, 48 + 4 * k, flag))
            m[k] = m[k] + place(add_m, 16, at_1)
            if k < 4:
                c[k] = c[k] + place(add_c, 16, at_2)
    for k in range(10):
        fine_o[k] = f[k]
    for k in range(6):
        middle_o[k] = m[k]
    for k in range(4):
        coarse_o[k] = c[k]
    lane = lane_numbers(24)
    lane_16 = lane_numbers(16)
    none = jnp.zeros((8, 128), jnp.float32)

    def strip(value, first, count, at):
        lanes = lane_numbers(value.shape[0])
        moved = roll(value, at - first, 1)
        return jnp.where((lanes >= at) & (lanes < at + count), moved, 0.0)

    for out, at_0, at_1, at_2 in ((to_high, 127, 63, 31), (to_low, 126, 125, 125)):
        total = jnp.zeros((24, 128), jnp.float32)
        for k in range(10):
            own = lane == 127 if at_0 == 127 else lane == 0
            total = total + strip(jnp.where(own, f[k][:, 0:128], f[k][:, 128:256]), at_0, 3, 4 * k)
        part = jnp.zeros((16, 128), jnp.float32)
        for k in range(6):
            part = part + strip(m[k], at_1, 4, 40 + 4 * k)
        for k in range(4):
            part = part + strip(c[k], at_2, 4, 64 + 4 * k)
        out[...] = total + jnp.concatenate([part, none], axis=0)


def four_lanes(rows):
    lane = lane_numbers(rows)
    return (lane < 4) | (lane >= 124)


def pressure_kernel(inside, moved, fine, middle, coarse, low, high, velocity, pressure, halves):
    f = [fine[k] for k in range(10)]
    m = [middle[k] for k in range(6)]
    c = [coarse[k] for k in range(4)]

    def strip(value, at, count, first):
        lanes = lane_numbers(value.shape[0])
        kept = jnp.where((lanes >= at) & (lanes < at + count), value, 0.0)
        return roll(kept, first - at, 1)

    lane = lane_numbers(24)
    for got, flag, at_0, at_1, at_2 in (
        (low, inside[4], -1, -1, -1),
        (high, inside[5], 126, 61, 29),
    ):
        whole = got[...] * flag
        part = whole[0:16]
        for k in range(10):
            add = strip(whole, 4 * k, 3, at_0)
            own = (lane < 64) if at_0 < 0 else (lane >= 64)
            add = jnp.concatenate([jnp.where(own, add, 0.0), jnp.where(own, 0.0, add)], axis=1)
            f[k] = f[k] + add
        for k in range(6):
            m[k] = m[k] + strip(part, 40 + 4 * k, 4, at_1)
        for k in range(4):
            c[k] = c[k] + strip(part, 64 + 4 * k, 4, at_2)
    row = row_numbers(8)
    lane = lane_numbers(8)
    to_middle = (lane >> 1) + jnp.where(lane < 96, 0, 64)
    for k in range(4):
        wide = pick_lanes(c[k], to_middle)
        halves[0, k, pl.ds(0, 16, stride=2), :] = wide
        halves[0, k, pl.ds(1, 16, stride=2), :] = wide
    for k in range(6):
        at = (k + 1) // 2
        tail = jnp.where(row < 4, halves[0, at, 8:16], halves[0, at, 24:32])
        m[k] = m[k] + jnp.concatenate([halves[0, at, 0:8], tail], axis=0)
    to_centre = lane >> 1
    to_side = to_centre + 64
    for k in range(6):
        for side, index in enumerate((to_centre, to_side)):
            wide = pick_lanes(m[k], index)
            halves[side, k, pl.ds(0, 16, stride=2), :] = wide
            halves[side, k, pl.ds(1, 16, stride=2), :] = wide
    for k in range(10):
        at = (k + 1) // 2
        sides = []
        for side in range(2):
            tail = jnp.where(row < 4, halves[side, at, 16:24], halves[side, at, 24:32])
            sides.append(jnp.concatenate([halves[side, at, 0:16], tail], axis=0))
        f[k] = f[k] + jnp.concatenate(sides, axis=1)
    for k in range(8):
        here = f[k + 1]
        pressure[k] = here[0:16, 0:128]
        velocity[0, k] = moved[0, k] - 0.5 * (f[k + 2][0:16, 0:128] - f[k][0:16, 0:128])
        slope = roll(here, -1, 0) - roll(here, 1, 0)
        velocity[1, k] = moved[1, k] - 0.5 * slope[0:16, 0:128]
        here = here[0:16]
        slope = roll(here, -1, 1) - roll(here, 1, 1)
        velocity[2, k] = moved[2, k] - 0.5 * slope[:, 0:128]


def project(inside, moved):
    f32 = jnp.float32
    held = [((10, 24, 256), f32), ((6, 16, 128), f32), ((4, 16, 128), f32)]
    halves = [pltpu.VMEM((2, 8, 32, 128), f32)]
    side, side_2 = ((160, 128), f32), ((32, 128), f32)
    to_low, to_high, to_low_2, to_high_2, *sums = call(
        levels_kernel, [side, side, side_2, side_2] + held, halves, scalars=1, inputs=1
    )(inside, moved)
    low = shift_ring(to_high, "gx", 1)
    high = shift_ring(to_low, "gx", -1)
    low_2 = shift_ring(to_high_2, "gx", 2)
    high_2 = shift_ring(to_low_2, "gx", -2)
    side = ((72, 128), f32)
    to_low, to_high, *sums = call(
        planes_sum_kernel, [side, side] + held, scalars=1, inputs=7
    )(inside, *sums, low, high, low_2, high_2)
    low = shift_ring(to_high, "gy", 1)
    high = shift_ring(to_low, "gy", -1)
    side = ((24, 128), f32)
    to_low, to_high, *sums = call(rows_sum_kernel, [side, side] + held, scalars=1, inputs=5)(
        inside, *sums, low, high
    )
    low = shift_ring(to_high, "gz", 1)
    high = shift_ring(to_low, "gz", -1)
    return call(
        pressure_kernel,
        [((3, 8, 16, 128), f32), ((8, 16, 128), f32)],
        halves,
        scalars=1,
        inputs=6,
    )(inside, moved, *sums, low, high)


def body(velocity, density, offsets, eighths):
    place = lax.axis_index("gx")
    beyond = [place > 1, place < lax.axis_size("gx") - 2]
    inside = jnp.stack(ends("gx") + ends("gy") + ends("gz") + beyond).astype(jnp.float32)
    moved = advect(inside, velocity, density, offsets, eighths)
    new_velocity, pressure = project(inside, moved)
    return new_velocity, moved[3], pressure


def solution(mesh):
    return jax.shard_map(
        body,
        mesh=mesh,
        in_specs=(
            P(None, "gx", "gy", "gz"),
            P("gx", "gy", "gz"),
            P(None, "gx", "gy", "gz"),
            P(None, "gx", "gy", "gz"),
        ),
        out_specs=(P(None, "gx", "gy", "gz"), P("gx", "gy", "gz"), P("gx", "gy", "gz")),
        check_vma=False,
    )
```

```python
import functools

import jax
import jax.numpy as jnp
from jax import lax
from jax.experimental import pallas as pl
from jax.experimental.pallas import tpu as pltpu
from jax.sharding import PartitionSpec as P

RELAX_WEIGHT = 6.0 / 7.0
VMEM = pl.BlockSpec(memory_space=pltpu.VMEM)
SMEM = pl.BlockSpec(memory_space=pltpu.SMEM)
FAR = pl.BlockSpec(memory_space=pl.ANY)
PARAMS = pltpu.CompilerParams(vmem_limit_bytes=48 * 1024 * 1024)


def call(kernel, outs, scratch=(), scalars=0, inputs=0, far=0):
    return pl.pallas_call(
        kernel,
        out_shape=[jax.ShapeDtypeStruct(shape, dtype) for shape, dtype in outs],
        in_specs=[SMEM] * scalars + [VMEM] * inputs + [FAR] * far,
        out_specs=[VMEM] * len(outs),
        scratch_shapes=list(scratch),
        compiler_params=PARAMS,
    )


def shift_ring(value, axis, step):
    count = lax.axis_size(axis)
    return lax.ppermute(value, axis, [(i, (i + step) % count) for i in range(count)])


def pack_kernel(velocity, density, low_planes, high_planes, arrived):
    copies = []
    for k, (out, first) in enumerate(((low_planes, 0), (high_planes, 4))):
        planes = pl.ds(first, 4)
        copies.append(
            pltpu.make_async_copy(velocity.at[:, planes], out.at[pl.ds(0, 3)], arrived.at[2 * k])
        )
        copies.append(pltpu.make_async_copy(density.at[planes], out.at[3], arrived.at[2 * k + 1]))
    for copy in copies:
        copy.start()
    for copy in copies:
        copy.wait()


def own_kernel(velocity, density, offsets, eighths, fields_t, code_t, own, whole, parts, arrived):
    copies = [
        pltpu.make_async_copy(velocity, own.at[pl.ds(0, 3)], arrived.at[0]),
        pltpu.make_async_copy(density, own.at[3], arrived.at[1]),
        pltpu.make_async_copy(offsets, whole, arrived.at[2]),
        pltpu.make_async_copy(eighths, parts, arrived.at[3]),
    ]
    for copy in copies:
        copy.start()
    for copy in copies:
        copy.wait()
    for f in range(4):
        fields_t[f] = own[f].reshape(128, 128).T
    code = (whole[0] + 4) + (whole[1] + 4) * 8 + (whole[2] + 4) * 64
    code = code + parts[0] * 512 + parts[1] * 4096 + parts[2] * 32768
    code_t[...] = code.astype(jnp.float32).reshape(128, 128).T.astype(jnp.int32)


def rows_kernel(inside, velocity, density, low, high, after, to_low, to_high):
    for f in range(4):
        for pair in range(8):
            for half in range(2):
                plane = 2 * pair + half
                if plane < 4:
                    rows = low[f, plane] * inside[0]
                elif plane >= 12:
                    rows = high[f, plane - 12] * inside[1]
                elif f < 3:
                    rows = velocity[f, plane - 4]
                else:
                    rows = density[plane - 4]
                to_low[f, pair, 4 * half : 4 * half + 4] = rows[0:4]
                to_high[f, pair, 4 * half : 4 * half + 4] = rows[12:16]


def planes_kernel(inside, low, high, planes_t):
    for f in range(4):
        both = jnp.concatenate(
            [low[f].reshape(64, 128) * inside[0], high[f].reshape(64, 128) * inside[1]], axis=0
        )
        planes_t[f] = both.T


def columns_kernel(inside, fields_t, planes_t, code_t, low, high, after, rows_t, to_low, to_high):
    for f in range(4):
        both = jnp.concatenate(
            [low[f].reshape(64, 128) * inside[2], high[f].reshape(64, 128) * inside[3]], axis=0
        )
        turned = both.T
        rows_t[f] = turned
        for group, source in enumerate((fields_t[f], planes_t[f], turned)):
            at = 24 * (3 * f + group)
            to_low[at : at + 24] = source[0:24]
            to_high[at : at + 24] = source[104:128]
    for out, first in ((to_low, 0), (to_high, 112)):
        code = code_t[first : first + 16]
        for k in range(6):
            out[288 + 16 * k : 304 + 16 * k] = ((code >> (3 * k)) & 7).astype(jnp.float32)


def corners_of(code):
    lane = lax.broadcasted_iota(jnp.int32, (8, 128), 1)
    x = (lane >> 4) + (code & 7)
    y = (lane & 15) + ((code >> 3) & 7)
    fx = ((code >> 9) & 7).astype(jnp.float32) / 8.0
    fy = ((code >> 12) & 7).astype(jnp.float32) / 8.0
    corners = []
    for cx in (0, 1):
        for cy in (0, 1):
            xc, yc = x + cx, y + cy
            low_x, high_x = xc < 4, xc >= 12
            in_rows = (yc < 4) | (yc >= 20)
            in_planes = low_x | high_x
            plane = xc - jnp.where(low_x, 0, jnp.where(high_x, 8, 4))
            by_rows = xc * 4 + (yc & 3) + jnp.where(yc >= 20, 64, 0)
            at = jnp.where(in_rows, by_rows, plane * 16 + yc - 4)
            weight = (fx if cx else 1.0 - fx) * (fy if cy else 1.0 - fy)
            in_block = jnp.where(in_rows, 0.0, weight)
            weights = (
                jnp.where(in_planes, 0.0, in_block),
                jnp.where(in_planes, in_block, 0.0),
                jnp.where(in_rows, weight, 0.0),
            )
            corners.append((at, weights))
    return corners


def weights_z(code, shifts):
    level = (code >> 6) & 7
    fz = ((code >> 15) & 7).astype(jnp.float32) / 8.0
    return [
        jnp.where(level == dz, 1.0 - fz, jnp.where(level == dz - 1, fz, 0.0)) for dz in shifts
    ]


def gathered(at, weights, rows_of, count=4):
    parts = [None] * count
    for shift, weight in enumerate(weights):
        for f in range(count):
            taken = jnp.take_along_axis(
                rows_of(f, shift), at, axis=1, mode="promise_in_bounds"
            )
            parts[f] = weight * taken if shift == 0 else parts[f] + weight * taken
    return parts


def group_kernel(group, code_t, source_t, *refs):
    before, after = refs[:-1], refs[-1]
    none = jnp.zeros((8, 128), jnp.float32)

    def tile(step, carry):
        start = pl.multiple_of(step * 8, 8)
        code = code_t[pl.ds(start, 8), :]
        by_shift = weights_z(code, range(9))
        sums = [before[0][f, pl.ds(start, 8), :] if before else none for f in range(4)]
        for at, weights in corners_of(code):
            parts = gathered(
                at, by_shift, lambda f, dz: source_t[f, pl.ds(start + (dz - 4), 8), :]
            )
            for f in range(4):
                sums[f] = sums[f] + weights[group] * parts[f]
        for f in range(4):
            after[f, pl.ds(start, 8), :] = sums[f]
        return carry

    lax.fori_loop(1, 15, tile, 0, unroll=7)


def edges_kernel(
    inside, code_t, sums_t, fields_t, planes_t, rows_t, low, high,
    moved, density, beyond, moved_t, beyond_t, padded, codes,
):
    for f in range(4):
        for group, source in enumerate((fields_t, planes_t, rows_t)):
            at = 24 * (3 * f + group)
            padded[0, f, group, 0:24] = low[at : at + 24] * inside[4]
            padded[0, f, group, 24:40] = source[f, 0:16]
            padded[1, f, group, 0:16] = source[f, 112:128]
            padded[1, f, group, 16:40] = high[at : at + 24] * inside[5]
    for end, got in ((0, low), (1, high)):
        code = jnp.zeros((16, 128), jnp.int32)
        for k in range(6):
            code = code + (got[288 + 16 * k : 304 + 16 * k].astype(jnp.int32) << (3 * k))
        if end == 0:
            codes[0, 0:16] = code
            codes[0, 16:24] = code_t[0:8]
        else:
            codes[1, 0:8] = code_t[120:128]
            codes[1, 8:24] = code
    for f in range(4):
        moved_t[f] = sums_t[f]

    def moved_tile(end, start, count):
        code = codes[end, pl.ds(start, 8), :]
        by_shift = weights_z(code, range(9))
        sums = [jnp.zeros((8, 128), jnp.float32)] * count
        for at, weights in corners_of(code):
            for group in range(3):
                parts = gathered(
                    at,
                    by_shift,
                    lambda f, dz: padded[end, f, group, pl.ds(start + (4 + dz), 8), :],
                    count,
                )
                for f in range(count):
                    sums[f] = sums[f] + weights[group] * parts[f]
        return sums

    def inner(end, carry):
        sums = moved_tile(end, pl.multiple_of(16 * (1 - end), 8), 4)
        for f in range(4):
            moved_t[f, pl.ds(pl.multiple_of(120 * end, 8), 8), :] = sums[f]
        return carry

    def outer(step, carry):
        end, half = step // 2, step % 2
        sums = moved_tile(end, pl.multiple_of(8 * (end + half), 8), 3)
        flag = jnp.where(end == 0, inside[4], inside[5])
        for f in range(3):
            beyond_t[f, pl.ds(pl.multiple_of(112 * (1 - end) + 8 * half, 8), 8), :] = sums[f] * flag
        return carry

    lax.fori_loop(0, 2, inner, 0, unroll=2)
    for f in range(3):
        beyond_t[f] = jnp.zeros((128, 128), jnp.float32)
    lax.fori_loop(0, 4, outer, 0, unroll=2)
    for f in range(3):
        moved[f] = moved_t[f].T.reshape(8, 16, 128)
        beyond[f] = beyond_t[f].T.reshape(8, 16, 128)
    density[...] = moved_t[3].T.reshape(8, 16, 128)


def ends(axis):
    place = lax.axis_index(axis)
    return [place > 0, place < lax.axis_size(axis) - 1]


def advect(inside, velocity, density, offsets, eighths):
    f32 = jnp.float32
    turned = ((4, 128, 128), f32)
    arrived = pltpu.SemaphoreType.DMA((4,))

    def gather(group, *values):
        kernel = functools.partial(group_kernel, group)
        return call(kernel, [turned], inputs=len(values))(*values)[0]

    planes = ((4, 4, 16, 128), f32)
    low_planes, high_planes = call(pack_kernel, [planes, planes], [arrived], far=2)(
        velocity, density
    )
    low = shift_ring(high_planes, "gx", 1)
    high = shift_ring(low_planes, "gx", -1)
    whole = pltpu.VMEM((3, 8, 16, 128), jnp.int32)
    scratch = [pltpu.VMEM((4, 8, 16, 128), f32), whole, whole, arrived]
    fields_t, code_t = call(own_kernel, [turned, ((128, 128), jnp.int32)], scratch, far=4)(
        velocity, density, offsets, eighths
    )
    sums_t = gather(0, code_t, fields_t)
    strip = ((4, 8, 8, 128), f32)
    to_low, to_high = call(rows_kernel, [strip, strip], scalars=1, inputs=5)(
        inside, velocity, density, low, high, sums_t
    )
    rows_low = shift_ring(to_high, "gy", 1)
    rows_high = shift_ring(to_low, "gy", -1)
    (planes_t,) = call(planes_kernel, [turned], scalars=1, inputs=2)(inside, low, high)
    sums_t = gather(1, code_t, planes_t, sums_t)
    edge = ((384, 128), f32)
    rows_t, to_low, to_high = call(
        columns_kernel, [turned, edge, edge], scalars=1, inputs=6
    )(inside, fields_t, planes_t, code_t, rows_low, rows_high, sums_t)
    columns_low = shift_ring(to_high, "gz", 1)
    columns_high = shift_ring(to_low, "gz", -1)
    sums_t = gather(2, code_t, rows_t, sums_t)
    scratch = [
        pltpu.VMEM((4, 128, 128), f32),
        pltpu.VMEM((3, 128, 128), f32),
        pltpu.VMEM((2, 4, 3, 40, 128), f32),
        pltpu.VMEM((2, 24, 128), jnp.int32),
    ]
    block = ((3, 8, 16, 128), f32)
    return call(
        edges_kernel, [block, ((8, 16, 128), f32), block], scratch, scalars=1, inputs=7
    )(inside, code_t, sums_t, fields_t, planes_t, rows_t, columns_low, columns_high)


def roll(value, shift, dim):
    return pltpu.roll(value, shift % value.shape[dim], dim)


def neighbours(value):
    none = jnp.zeros_like(value[:1])
    summed = jnp.concatenate([value[1:], none], axis=0) + jnp.concatenate([none, value[:-1]], axis=0)
    summed = summed + roll(value, -1, 1) + roll(value, 1, 1)
    return summed + roll(value, -1, 2) + roll(value, 1, 2)


def grid_mask(inside, planes, rows, lanes):
    shape = (rows[0], lanes[0])
    row = lax.broadcasted_iota(jnp.int32, shape, 0)
    lane = lax.broadcasted_iota(jnp.int32, shape, 1)
    by_row = jnp.where(
        row < rows[1], 1.0, jnp.where(row < (rows[0] + rows[1]) // 2, inside[3], inside[2])
    )
    by_lane = jnp.where(
        lane < lanes[1], 1.0, jnp.where(lane < (lanes[0] + lanes[1]) // 2, inside[5], inside[4])
    )
    both = by_row * by_lane
    first, count, block = planes
    parts = [
        both * inside[0] if x < 0 else (both * inside[1] if x >= block else both)
        for x in range(first, first + count)
    ]
    return jnp.stack(parts, axis=0)


def smooth(source, spacing, mask, want_residual):
    relaxation = RELAX_WEIGHT / 6.0
    first = relaxation * spacing * source
    second = first + relaxation * (spacing * source - (6.0 * first - neighbours(first)))
    second = second * mask
    if not want_residual:
        return second
    residual = source - (6.0 * second - neighbours(second)) / spacing
    return second, residual * mask


def pick_lanes(value, index):
    parts = [
        jnp.take_along_axis(value[r : r + 8], index, axis=1, mode="promise_in_bounds")
        for r in range(0, value.shape[0], 8)
    ]
    return jnp.concatenate(parts, axis=0)


def lane_numbers(rows):
    return lax.broadcasted_iota(jnp.int32, (rows, 128), 1)


def row_numbers(rows):
    return lax.broadcasted_iota(jnp.int32, (rows, 128), 0)


def pair_sum(value):
    value = value + roll(value, -1, 1)
    return value + roll(value, -1, 2)


def restrict_fine(residual, halves):
    lane = lane_numbers(8)
    index = (lane * 2) & 127
    left = lane_numbers(16) < 64
    row = row_numbers(8)
    planes = []
    pairs = pair_sum(
        jnp.stack([residual[2 * p] + residual[2 * p + 1] for p in range(8)], axis=0)
    )
    for p in range(8):
        even = []
        for side in range(2):
            both = pairs[p, :, 128 * side : 128 * side + 128]
            halves[side, p, 0:16] = both[0:16]
            halves[side, p, 16:24] = jnp.where(row < 4, both[16:24], 0.0)
            halves[side, p, 24:32] = jnp.where(row >= 4, both[16:24], 0.0)
            even.append(pick_lanes(halves[side, p, pl.ds(0, 16, stride=2), :], index))
        planes.append(jnp.where(left, even[0], even[1]))
    return jnp.stack(planes, axis=0) * 0.125


def restrict_middle(residual, halves):
    index = (lane_numbers(8) * 2) & 127
    row, lane = row_numbers(16), lane_numbers(16)
    valid = ((row < 6) | (row >= 14)) & ((lane < 36) | (lane >= 124))
    pairs = pair_sum(
        jnp.stack([residual[2 * p] + residual[2 * p + 1] for p in range(6)], axis=0)
    )
    planes = []
    for p in range(6):
        halves[0, p, 0:16] = pairs[p]
        even = pick_lanes(halves[0, p, pl.ds(0, 8, stride=2), :], index)
        planes.append(jnp.where(valid, jnp.concatenate([even, even], axis=0), 0.0))
    return jnp.stack(planes, axis=0) * 0.125


def with_planes(value, count):
    none = jnp.zeros((count,) + value.shape[1:], value.dtype)
    return jnp.concatenate([none, value, none], axis=0)


def levels_kernel(
    inside, moved, beyond, to_low, to_high, to_low_2, to_high_2, fine, middle, coarse, halves
):
    def spread(a):
        block = jnp.concatenate([moved[a], beyond[a]], axis=2)
        block = jnp.concatenate([block, jnp.zeros((8, 8, 256), jnp.float32)], axis=1)
        return with_planes(block, 4)

    u = spread(0)
    none = jnp.zeros_like(u[:1])
    slope = jnp.concatenate([u[1:], none], axis=0) - jnp.concatenate([none, u[:-1]], axis=0)
    u = spread(1)
    slope = slope + (roll(u, -1, 1) - roll(u, 1, 1))
    u = spread(2)
    slope = slope + (roll(u, -1, 2) - roll(u, 1, 2))
    mask = grid_mask(inside, (-4, 16, 8), (24, 16), (256, 128))
    second, residual = smooth(slope * mask * -0.5, 1.0, mask, True)
    mask = grid_mask(inside, (-4, 12, 4), (16, 8), (128, 64))
    source = with_planes(restrict_fine(residual, halves), 2)
    second_1, residual = smooth(source, 4.0, mask, True)
    mask = grid_mask(inside, (-3, 8, 2), (16, 4), (128, 32))
    source = with_planes(restrict_middle(residual, halves), 1)
    second_2 = smooth(source, 16.0, mask, False)
    lane = lax.broadcasted_iota(jnp.int32, (1, 24, 256), 2)
    second = jnp.where((lane < 132) | (lane >= 252), second, 0.0)
    lane = lane_numbers(16)[None]
    second_1 = jnp.where((lane < 72) | (lane >= 120), second_1, 0.0)
    second_2 = jnp.where((lane < 40) | (lane >= 120), second_2, 0.0)
    fine[...] = second[3:13]
    middle[...] = second_1[3:9]
    coarse[...] = second_2[2:6]
    for out, at_0, at_1, at_2 in ((to_high, 11, 7, 4), (to_low, 2, 1, 0)):
        sides = None
        for k in range(3):
            out[24 * k : 24 * k + 24] = second[at_0 + k][:, 0:128]
            side = roll(second[at_0 + k][:, 128:256], 16 * k, 1)
            sides = side if sides is None else sides + side
        out[72:96] = sides
        for k in range(4):
            out[96 + 16 * k : 112 + 16 * k] = second_1[at_1 + k] + roll(second_2[at_2 + k], 80, 1)
    for k in range(2):
        to_high_2[16 * k : 16 * k + 16] = second_2[6 + k]
        to_low_2[16 * k : 16 * k + 16] = second_2[k]


def near_end(lane):
    return (lane < 8) | (lane >= 120)


def split_levels(both):
    lane = lane_numbers(both.shape[0])
    middle = jnp.where((lane < 72) | (lane >= 120), both, 0.0)
    coarse = jnp.where((lane >= 72) & (lane < 120), both, 0.0)
    return middle, roll(coarse, -80, 1)


def planes_sum_kernel(
    inside, fine, middle, coarse, low, high, low_2, high_2, to_low, to_high, fine_o, middle_o, coarse_o
):
    f = [fine[k] for k in range(10)]
    m = [middle[k] for k in range(6)]
    c = [coarse[k] for k in range(4)]
    lane = lane_numbers(24)
    for got, flag, at_0, at_1 in ((low, inside[0], 0, 0), (high, inside[1], 7, 2)):
        sides = got[72:96] * flag
        for k in range(3):
            side = jnp.where(near_end(lane), roll(sides, -16 * k, 1), 0.0)
            centre = got[24 * k : 24 * k + 24] * flag
            f[at_0 + k] = f[at_0 + k] + jnp.concatenate([centre, side], axis=1)
        for k in range(4):
            add_m, add_c = split_levels(got[96 + 16 * k : 112 + 16 * k] * flag)
            m[at_1 + k] = m[at_1 + k] + add_m
            c[k] = c[k] + add_c
    for k in range(2):
        c[k] = c[k] + low_2[16 * k : 16 * k + 16] * inside[6]
        c[2 + k] = c[2 + k] + high_2[16 * k : 16 * k + 16] * inside[7]
    c[0], c[3] = c[0] * inside[0], c[3] * inside[1]
    for k in range(10):
        fine_o[k] = f[k]
    for k in range(6):
        middle_o[k] = m[k]
    for k in range(4):
        coarse_o[k] = c[k]
    for out, at_0, at_1, at_2 in ((to_high, 15, 7, 3), (to_low, -2, -3, -3)):
        sides = None
        for k in range(10):
            rows = roll(f[k], -at_0, 0)[0:8]
            out[4 * k : 4 * k + 4] = rows[0:4, 0:128]
            side = roll(jnp.where(near_end(lane_numbers(8)), rows[:, 128:256], 0.0), 8 + 12 * k, 1)
            sides = side if sides is None else sides + side
        out[40:48] = sides
        for k in range(6):
            rows = roll(m[k], -at_1, 0)[0:8]
            if k < 4:
                rows = rows + roll(roll(c[k], -at_2, 0)[0:8], 80, 1)
            out[48 + 4 * k : 52 + 4 * k] = rows[0:4]


def four_lanes(rows):
    lane = lane_numbers(rows)
    return (lane < 4) | (lane >= 124)


def pressure_kernel(
    inside, moved, fine, middle, coarse, low, high, velocity, pressure, halves
):
    f = [fine[k] for k in range(10)]
    m = [middle[k] for k in range(6)]
    c = [coarse[k] for k in range(4)]
    row = row_numbers(8)

    def place(rows, count, first):
        none = jnp.zeros((count - 8,) + rows.shape[1:], jnp.float32)
        return roll(jnp.concatenate([rows, none], axis=0), first, 0)

    def four(got, at, flag):
        tile = got[at - at % 8 : at - at % 8 + 8] * flag
        tile = roll(tile, -4, 0) if at % 8 else tile
        return jnp.where(row < 4, tile, 0.0)

    for got, flag, at_0, at_1, at_2 in (
        (low, inside[2], -1, -1, -1),
        (high, inside[3], 14, 5, 1),
    ):
        sides = jnp.where(row < 3, got[40:48] * flag, 0.0)
        for k in range(10):
            side = jnp.where(four_lanes(8), roll(sides, -(8 + 12 * k), 1), 0.0)
            rows = jnp.where(row < 3, four(got, 4 * k, flag), 0.0)
            f[k] = f[k] + place(jnp.concatenate([rows, side], axis=1), 24, at_0)
        for k in range(6):
            add_m, add_c = split_levels(four(got, 48 + 4 * k, flag))
            m[k] = m[k] + place(add_m, 16, at_1)
            if k < 4:
                c[k] = c[k] + place(add_c, 16, at_2)
    lane = lane_numbers(8)
    to_middle = (lane >> 1) + jnp.where(lane < 96, 0, 64)
    for k in range(4):
        wide = pick_lanes(c[k], to_middle)
        halves[0, k, pl.ds(0, 16, stride=2), :] = wide
        halves[0, k, pl.ds(1, 16, stride=2), :] = wide
    for k in range(6):
        at = (k + 1) // 2
        tail = jnp.where(row < 4, halves[0, at, 8:16], halves[0, at, 24:32])
        m[k] = m[k] + jnp.concatenate([halves[0, at, 0:8], tail], axis=0)
    to_centre = lane >> 1
    to_side = to_centre + 64
    for k in range(6):
        for side, index in enumerate((to_centre, to_side)):
            wide = pick_lanes(m[k], index)
            halves[side, k, pl.ds(0, 16, stride=2), :] = wide
            halves[side, k, pl.ds(1, 16, stride=2), :] = wide
    for k in range(10):
        at = (k + 1) // 2
        sides = []
        for side in range(2):
            tail = jnp.where(row < 4, halves[side, at, 16:24], halves[side, at, 24:32])
            sides.append(jnp.concatenate([halves[side, at, 0:16], tail], axis=0))
        f[k] = f[k] + jnp.concatenate(sides, axis=1)
    for k in range(8):
        here = f[k + 1]
        pressure[k] = here[0:16, 0:128]
        velocity[0, k] = moved[0, k] - 0.5 * (f[k + 2][0:16, 0:128] - f[k][0:16, 0:128])
        slope = roll(here, -1, 0) - roll(here, 1, 0)
        velocity[1, k] = moved[1, k] - 0.5 * slope[0:16, 0:128]
        here = here[0:16]
        slope = roll(here, -1, 1) - roll(here, 1, 1)
        velocity[2, k] = moved[2, k] - 0.5 * slope[:, 0:128]


def project(inside, moved, beyond):
    f32 = jnp.float32
    held = [((10, 24, 256), f32), ((6, 16, 128), f32), ((4, 16, 128), f32)]
    halves = [pltpu.VMEM((2, 8, 32, 128), f32)]
    side, side_2 = ((160, 128), f32), ((32, 128), f32)
    to_low, to_high, to_low_2, to_high_2, *sums = call(
        levels_kernel, [side, side, side_2, side_2] + held, halves, scalars=1, inputs=2
    )(inside, moved, beyond)
    low = shift_ring(to_high, "gx", 1)
    high = shift_ring(to_low, "gx", -1)
    low_2 = shift_ring(to_high_2, "gx", 2)
    high_2 = shift_ring(to_low_2, "gx", -2)
    side = ((72, 128), f32)
    to_low, to_high, *sums = call(
        planes_sum_kernel, [side, side] + held, scalars=1, inputs=7
    )(inside, *sums, low, high, low_2, high_2)
    low = shift_ring(to_high, "gy", 1)
    high = shift_ring(to_low, "gy", -1)
    return call(
        pressure_kernel,
        [((3, 8, 16, 128), f32), ((8, 16, 128), f32)],
        halves,
        scalars=1,
        inputs=6,
    )(inside, moved, *sums, low, high)


def body(velocity, density, offsets, eighths):
    place = lax.axis_index("gx")
    beyond = [place > 1, place < lax.axis_size("gx") - 2]
    inside = jnp.stack(ends("gx") + ends("gy") + ends("gz") + beyond).astype(jnp.float32)
    moved, new_density, past = advect(inside, velocity, density, offsets, eighths)
    new_velocity, pressure = project(inside, moved, past)
    return new_velocity, new_density, pressure


def solution(mesh):
    return jax.shard_map(
        body,
        mesh=mesh,
        in_specs=(
            P(None, "gx", "gy", "gz"),
            P("gx", "gy", "gz"),
            P(None, "gx", "gy", "gz"),
            P(None, "gx", "gy", "gz"),
        ),
        out_specs=(P(None, "gx", "gy", "gz"), P("gx", "gy", "gz"), P("gx", "gy", "gz")),
        check_vma=False,
    )
```

```python
import functools

import jax
import jax.numpy as jnp
from jax import lax
from jax.experimental import pallas as pl
from jax.experimental.pallas import tpu as pltpu
from jax.sharding import PartitionSpec as P

RELAX_WEIGHT = 6.0 / 7.0
VMEM = pl.BlockSpec(memory_space=pltpu.VMEM)
PARAMS = pltpu.CompilerParams(vmem_limit_bytes=48 * 1024 * 1024)


def call(kernel, outs, scratch=(), inputs=0):
    return pl.pallas_call(
        kernel,
        out_shape=[jax.ShapeDtypeStruct(shape, dtype) for shape, dtype in outs],
        in_specs=[VMEM] * inputs,
        out_specs=[VMEM] * len(outs),
        scratch_shapes=list(scratch),
        compiler_params=PARAMS,
    )


def inside_grid():
    found = []
    for axis, step in (("gx", 1), ("gy", 1), ("gz", 1), ("gx", 2)):
        place, count = lax.axis_index(axis), lax.axis_size(axis)
        found.append(jnp.where(place >= step, 1.0, 0.0))
        found.append(jnp.where(place < count - step, 1.0, 0.0))
    return found


def shift_ring(value, axis, step):
    count = lax.axis_size(axis)
    return lax.ppermute(value, axis, [(i, (i + step) % count) for i in range(count)])


def pack_kernel(velocity, density, low_planes, high_planes):
    for f in range(4):
        field = velocity[f] if f < 3 else density[...]
        low_planes[f] = field[0:4]
        high_planes[f] = field[4:8]


def own_kernel(velocity, density, code, fields_t, code_t):
    for a in range(3):
        fields_t[a] = velocity[a].reshape(128, 128).T
    fields_t[3] = density[...].reshape(128, 128).T
    code_t[...] = code[...].reshape(128, 128).T.astype(jnp.int32)


def rows_kernel(velocity, density, low, high, after, to_low, to_high):
    inside = inside_grid()
    for f in range(4):
        for pair in range(8):
            for half in range(2):
                plane = 2 * pair + half
                if plane < 4:
                    rows = low[f, plane] * inside[0]
                elif plane >= 12:
                    rows = high[f, plane - 12] * inside[1]
                elif f < 3:
                    rows = velocity[f, plane - 4]
                else:
                    rows = density[plane - 4]
                to_low[f, pair, 4 * half : 4 * half + 4] = rows[0:4]
                to_high[f, pair, 4 * half : 4 * half + 4] = rows[12:16]


def planes_kernel(low, high, planes_t):
    inside = inside_grid()
    for f in range(4):
        both = jnp.concatenate(
            [low[f].reshape(64, 128) * inside[0], high[f].reshape(64, 128) * inside[1]], axis=0
        )
        planes_t[f] = both.T


def columns_kernel(fields_t, planes_t, code_t, low, high, after, rows_t, to_low, to_high):
    inside = inside_grid()
    for f in range(4):
        both = jnp.concatenate(
            [low[f].reshape(64, 128) * inside[2], high[f].reshape(64, 128) * inside[3]], axis=0
        )
        turned = both.T
        rows_t[f] = turned
        for group, source in enumerate((fields_t[f], planes_t[f], turned)):
            at = 24 * (3 * f + group)
            to_low[at : at + 24] = source[0:24]
            to_high[at : at + 24] = source[104:128]
    for out, first in ((to_low, 0), (to_high, 112)):
        code = code_t[first : first + 16]
        for k in range(6):
            out[288 + 16 * k : 304 + 16 * k] = ((code >> (3 * k)) & 7).astype(jnp.float32)


def corners_of(code):
    lane = lax.broadcasted_iota(jnp.int32, (8, 128), 1)
    x = (lane >> 4) + (code & 7)
    y = (lane & 15) + ((code >> 3) & 7)
    fx = ((code >> 9) & 7).astype(jnp.float32) / 8.0
    fy = ((code >> 12) & 7).astype(jnp.float32) / 8.0
    corners = []
    for cx in (0, 1):
        for cy in (0, 1):
            xc, yc = x + cx, y + cy
            low_x, high_x = xc < 4, xc >= 12
            in_rows = (yc < 4) | (yc >= 20)
            in_planes = low_x | high_x
            plane = xc - jnp.where(low_x, 0, jnp.where(high_x, 8, 4))
            by_rows = xc * 4 + (yc & 3) + jnp.where(yc >= 20, 64, 0)
            at = jnp.where(in_rows, by_rows, plane * 16 + yc - 4)
            weight = (fx if cx else 1.0 - fx) * (fy if cy else 1.0 - fy)
            in_block = jnp.where(in_rows, 0.0, weight)
            weights = (
                jnp.where(in_planes, 0.0, in_block),
                jnp.where(in_planes, in_block, 0.0),
                jnp.where(in_rows, weight, 0.0),
            )
            corners.append((at, weights))
    return corners


def weights_z(code, shifts):
    level = (code >> 6) & 7
    fz = ((code >> 15) & 7).astype(jnp.float32) / 8.0
    return [
        jnp.where(level == dz, 1.0 - fz, jnp.where(level == dz - 1, fz, 0.0)) for dz in shifts
    ]


def gathered(at, weights, rows_of, count=4):
    parts = [None] * count
    for shift, weight in enumerate(weights):
        for f in range(count):
            taken = jnp.take_along_axis(
                rows_of(f, shift), at, axis=1, mode="promise_in_bounds"
            )
            parts[f] = weight * taken if shift == 0 else parts[f] + weight * taken
    return parts


def group_kernel(group, code_t, source_t, *refs):
    before, after = refs[:-1], refs[-1]
    none = jnp.zeros((8, 128), jnp.float32)

    def tile(step, carry):
        start = pl.multiple_of(step * 8, 8)
        code = code_t[pl.ds(start, 8), :]
        by_shift = weights_z(code, range(9))
        sums = [before[0][f, pl.ds(start, 8), :] if before else none for f in range(4)]
        for at, weights in corners_of(code):
            parts = gathered(
                at, by_shift, lambda f, dz: source_t[f, pl.ds(start + (dz - 4), 8), :]
            )
            for f in range(4):
                sums[f] = sums[f] + weights[group] * parts[f]
        for f in range(4):
            after[f, pl.ds(start, 8), :] = sums[f]
        return carry

    lax.fori_loop(1, 15, tile, 0, unroll=7)


def edges_kernel(
    code_t, sums_t, fields_t, planes_t, rows_t, low, high,
    moved, density, beyond, moved_t, beyond_t, padded, codes,
):
    inside = inside_grid()
    for f in range(4):
        for group, source in enumerate((fields_t, planes_t, rows_t)):
            at = 24 * (3 * f + group)
            padded[0, f, group, 0:24] = low[at : at + 24] * inside[4]
            padded[0, f, group, 24:40] = source[f, 0:16]
            padded[1, f, group, 0:16] = source[f, 112:128]
            padded[1, f, group, 16:40] = high[at : at + 24] * inside[5]
    for end, got in ((0, low), (1, high)):
        code = jnp.zeros((16, 128), jnp.int32)
        for k in range(6):
            code = code + (got[288 + 16 * k : 304 + 16 * k].astype(jnp.int32) << (3 * k))
        if end == 0:
            codes[0, 0:16] = code
            codes[0, 16:24] = code_t[0:8]
        else:
            codes[1, 0:8] = code_t[120:128]
            codes[1, 8:24] = code
    for f in range(4):
        moved_t[f] = sums_t[f]

    def moved_tile(end, start, count):
        code = codes[end, pl.ds(start, 8), :]
        by_shift = weights_z(code, range(9))
        sums = [jnp.zeros((8, 128), jnp.float32)] * count
        for at, weights in corners_of(code):
            for group in range(3):
                parts = gathered(
                    at,
                    by_shift,
                    lambda f, dz: padded[end, f, group, pl.ds(start + (4 + dz), 8), :],
                    count,
                )
                for f in range(count):
                    sums[f] = sums[f] + weights[group] * parts[f]
        return sums

    def inner(end, carry):
        sums = moved_tile(end, pl.multiple_of(16 * (1 - end), 8), 4)
        for f in range(4):
            moved_t[f, pl.ds(pl.multiple_of(120 * end, 8), 8), :] = sums[f]
        return carry

    def outer(step, carry):
        end, half = step // 2, step % 2
        sums = moved_tile(end, pl.multiple_of(8 * (end + half), 8), 3)
        flag = jnp.where(end == 0, inside[4], inside[5])
        for f in range(3):
            beyond_t[f, pl.ds(pl.multiple_of(112 * (1 - end) + 8 * half, 8), 8), :] = sums[f] * flag
        return carry

    lax.fori_loop(0, 2, inner, 0, unroll=2)
    for f in range(3):
        beyond_t[f] = jnp.zeros((128, 128), jnp.float32)
    lax.fori_loop(0, 4, outer, 0, unroll=2)
    for f in range(3):
        moved[f] = moved_t[f].T.reshape(8, 16, 128)
        beyond[f] = beyond_t[f].T.reshape(8, 16, 128)
    density[...] = moved_t[3].T.reshape(8, 16, 128)


def advect(velocity, density, offsets, eighths):
    f32 = jnp.float32
    turned = ((4, 128, 128), f32)

    def gather(group, *values):
        kernel = functools.partial(group_kernel, group)
        return call(kernel, [turned], inputs=len(values))(*values)[0]

    planes = ((4, 4, 16, 128), f32)
    low_planes, high_planes = call(pack_kernel, [planes, planes], inputs=2)(
        velocity, density
    )
    low = shift_ring(high_planes, "gx", 1)
    high = shift_ring(low_planes, "gx", -1)
    code = (offsets[0] + 4) + (offsets[1] + 4) * 8 + (offsets[2] + 4) * 64
    code = code + eighths[0] * 512 + eighths[1] * 4096 + eighths[2] * 32768
    fields_t, code_t = call(own_kernel, [turned, ((128, 128), jnp.int32)], inputs=3)(
        velocity, density, code.astype(f32)
    )
    sums_t = gather(0, code_t, fields_t)
    strip = ((4, 8, 8, 128), f32)
    to_low, to_high = call(rows_kernel, [strip, strip], inputs=5)(
        velocity, density, low, high, sums_t
    )
    rows_low = shift_ring(to_high, "gy", 1)
    rows_high = shift_ring(to_low, "gy", -1)
    (planes_t,) = call(planes_kernel, [turned], inputs=2)(low, high)
    sums_t = gather(1, code_t, planes_t, sums_t)
    edge = ((384, 128), f32)
    rows_t, to_low, to_high = call(
        columns_kernel, [turned, edge, edge], inputs=6
    )(fields_t, planes_t, code_t, rows_low, rows_high, sums_t)
    columns_low = shift_ring(to_high, "gz", 1)
    columns_high = shift_ring(to_low, "gz", -1)
    sums_t = gather(2, code_t, rows_t, sums_t)
    scratch = [
        pltpu.VMEM((4, 128, 128), f32),
        pltpu.VMEM((3, 128, 128), f32),
        pltpu.VMEM((2, 4, 3, 40, 128), f32),
        pltpu.VMEM((2, 24, 128), jnp.int32),
    ]
    block = ((3, 8, 16, 128), f32)
    return call(
        edges_kernel, [block, ((8, 16, 128), f32), block], scratch, inputs=7
    )(code_t, sums_t, fields_t, planes_t, rows_t, columns_low, columns_high)


def roll(value, shift, dim):
    return pltpu.roll(value, shift % value.shape[dim], dim)


def neighbours(value):
    none = jnp.zeros_like(value[:1])
    summed = jnp.concatenate([value[1:], none], axis=0) + jnp.concatenate([none, value[:-1]], axis=0)
    summed = summed + roll(value, -1, 1) + roll(value, 1, 1)
    return summed + roll(value, -1, 2) + roll(value, 1, 2)


def grid_mask(inside, planes, rows, lanes):
    shape = (rows[0], lanes[0])
    row = lax.broadcasted_iota(jnp.int32, shape, 0)
    lane = lax.broadcasted_iota(jnp.int32, shape, 1)
    by_row = jnp.where(
        row < rows[1], 1.0, jnp.where(row < (rows[0] + rows[1]) // 2, inside[3], inside[2])
    )
    by_lane = jnp.where(
        lane < lanes[1], 1.0, jnp.where(lane < (lanes[0] + lanes[1]) // 2, inside[5], inside[4])
    )
    both = by_row * by_lane
    first, count, block = planes
    parts = [
        both * inside[0] if x < 0 else (both * inside[1] if x >= block else both)
        for x in range(first, first + count)
    ]
    return jnp.stack(parts, axis=0)


def smooth(source, spacing, mask, want_residual):
    relaxation = RELAX_WEIGHT / 6.0
    first = relaxation * spacing * source
    second = first + relaxation * (spacing * source - (6.0 * first - neighbours(first)))
    second = second * mask
    if not want_residual:
        return second
    residual = source - (6.0 * second - neighbours(second)) / spacing
    return second, residual * mask


def pick_lanes(value, index):
    parts = [
        jnp.take_along_axis(value[r : r + 8], index, axis=1, mode="promise_in_bounds")
        for r in range(0, value.shape[0], 8)
    ]
    return jnp.concatenate(parts, axis=0)


def lane_numbers(rows):
    return lax.broadcasted_iota(jnp.int32, (rows, 128), 1)


def row_numbers(rows):
    return lax.broadcasted_iota(jnp.int32, (rows, 128), 0)


def pair_sum(value):
    value = value + roll(value, -1, 1)
    return value + roll(value, -1, 2)


def restrict_fine(residual, halves):
    lane = lane_numbers(8)
    index = (lane * 2) & 127
    left = lane_numbers(16) < 64
    row = row_numbers(8)
    planes = []
    pairs = pair_sum(
        jnp.stack([residual[2 * p] + residual[2 * p + 1] for p in range(8)], axis=0)
    )
    for p in range(8):
        even = []
        for side in range(2):
            both = pairs[p, :, 128 * side : 128 * side + 128]
            halves[side, p, 0:16] = both[0:16]
            halves[side, p, 16:24] = jnp.where(row < 4, both[16:24], 0.0)
            halves[side, p, 24:32] = jnp.where(row >= 4, both[16:24], 0.0)
            even.append(pick_lanes(halves[side, p, pl.ds(0, 16, stride=2), :], index))
        planes.append(jnp.where(left, even[0], even[1]))
    return jnp.stack(planes, axis=0) * 0.125


def restrict_middle(residual, halves):
    index = (lane_numbers(8) * 2) & 127
    row, lane = row_numbers(16), lane_numbers(16)
    valid = ((row < 6) | (row >= 14)) & ((lane < 36) | (lane >= 124))
    pairs = pair_sum(
        jnp.stack([residual[2 * p] + residual[2 * p + 1] for p in range(6)], axis=0)
    )
    planes = []
    for p in range(6):
        halves[0, p, 0:16] = pairs[p]
        even = pick_lanes(halves[0, p, pl.ds(0, 8, stride=2), :], index)
        planes.append(jnp.where(valid, jnp.concatenate([even, even], axis=0), 0.0))
    return jnp.stack(planes, axis=0) * 0.125


def with_planes(value, count):
    none = jnp.zeros((count,) + value.shape[1:], value.dtype)
    return jnp.concatenate([none, value, none], axis=0)


def levels_kernel(
    moved, beyond, to_low, to_high, to_low_2, to_high_2, fine, middle, coarse, halves
):
    inside = inside_grid()
    def spread(a):
        block = jnp.concatenate([moved[a], beyond[a]], axis=2)
        block = jnp.concatenate([block, jnp.zeros((8, 8, 256), jnp.float32)], axis=1)
        return with_planes(block, 4)

    u = spread(0)
    none = jnp.zeros_like(u[:1])
    slope = jnp.concatenate([u[1:], none], axis=0) - jnp.concatenate([none, u[:-1]], axis=0)
    u = spread(1)
    slope = slope + (roll(u, -1, 1) - roll(u, 1, 1))
    u = spread(2)
    slope = slope + (roll(u, -1, 2) - roll(u, 1, 2))
    mask = grid_mask(inside, (-4, 16, 8), (24, 16), (256, 128))
    second, residual = smooth(slope * mask * -0.5, 1.0, mask, True)
    mask = grid_mask(inside, (-4, 12, 4), (16, 8), (128, 64))
    source = with_planes(restrict_fine(residual, halves), 2)
    second_1, residual = smooth(source, 4.0, mask, True)
    mask = grid_mask(inside, (-3, 8, 2), (16, 4), (128, 32))
    source = with_planes(restrict_middle(residual, halves), 1)
    second_2 = smooth(source, 16.0, mask, False)
    lane = lax.broadcasted_iota(jnp.int32, (1, 24, 256), 2)
    second = jnp.where((lane < 132) | (lane >= 252), second, 0.0)
    lane = lane_numbers(16)[None]
    second_1 = jnp.where((lane < 72) | (lane >= 120), second_1, 0.0)
    second_2 = jnp.where((lane < 40) | (lane >= 120), second_2, 0.0)
    fine[...] = second[3:13]
    middle[...] = second_1[3:9]
    coarse[...] = second_2[2:6]
    for out, at_0, at_1, at_2 in ((to_high, 11, 7, 4), (to_low, 2, 1, 0)):
        sides = None
        for k in range(3):
            out[24 * k : 24 * k + 24] = second[at_0 + k][:, 0:128]
            side = roll(second[at_0 + k][:, 128:256], 16 * k, 1)
            sides = side if sides is None else sides + side
        out[72:96] = sides
        for k in range(4):
            out[96 + 16 * k : 112 + 16 * k] = second_1[at_1 + k] + roll(second_2[at_2 + k], 80, 1)
    for k in range(2):
        to_high_2[16 * k : 16 * k + 16] = second_2[6 + k]
        to_low_2[16 * k : 16 * k + 16] = second_2[k]


def near_end(lane):
    return (lane < 8) | (lane >= 120)


def split_levels(both):
    lane = lane_numbers(both.shape[0])
    middle = jnp.where((lane < 72) | (lane >= 120), both, 0.0)
    coarse = jnp.where((lane >= 72) & (lane < 120), both, 0.0)
    return middle, roll(coarse, -80, 1)


def planes_sum_kernel(
    fine, middle, coarse, low, high, low_2, high_2, to_low, to_high, fine_o, middle_o, coarse_o
):
    inside = inside_grid()
    f = [fine[k] for k in range(10)]
    m = [middle[k] for k in range(6)]
    c = [coarse[k] for k in range(4)]
    lane = lane_numbers(24)
    for got, flag, at_0, at_1 in ((low, inside[0], 0, 0), (high, inside[1], 7, 2)):
        sides = got[72:96] * flag
        for k in range(3):
            side = jnp.where(near_end(lane), roll(sides, -16 * k, 1), 0.0)
            centre = got[24 * k : 24 * k + 24] * flag
            f[at_0 + k] = f[at_0 + k] + jnp.concatenate([centre, side], axis=1)
        for k in range(4):
            add_m, add_c = split_levels(got[96 + 16 * k : 112 + 16 * k] * flag)
            m[at_1 + k] = m[at_1 + k] + add_m
            c[k] = c[k] + add_c
    for k in range(2):
        c[k] = c[k] + low_2[16 * k : 16 * k + 16] * inside[6]
        c[2 + k] = c[2 + k] + high_2[16 * k : 16 * k + 16] * inside[7]
    c[0], c[3] = c[0] * inside[0], c[3] * inside[1]
    for k in range(10):
        fine_o[k] = f[k]
    for k in range(6):
        middle_o[k] = m[k]
    for k in range(4):
        coarse_o[k] = c[k]
    for out, at_0, at_1, at_2 in ((to_high, 15, 7, 3), (to_low, -2, -3, -3)):
        sides = None
        for k in range(10):
            rows = roll(f[k], -at_0, 0)[0:8]
            out[4 * k : 4 * k + 4] = rows[0:4, 0:128]
            side = roll(jnp.where(near_end(lane_numbers(8)), rows[:, 128:256], 0.0), 8 + 12 * k, 1)
            sides = side if sides is None else sides + side
        out[40:48] = sides
        for k in range(6):
            rows = roll(m[k], -at_1, 0)[0:8]
            if k < 4:
                rows = rows + roll(roll(c[k], -at_2, 0)[0:8], 80, 1)
            out[48 + 4 * k : 52 + 4 * k] = rows[0:4]


def four_lanes(rows):
    lane = lane_numbers(rows)
    return (lane < 4) | (lane >= 124)


def pressure_kernel(
    moved, fine, middle, coarse, low, high, velocity, pressure, halves
):
    inside = inside_grid()
    f = [fine[k] for k in range(10)]
    m = [middle[k] for k in range(6)]
    c = [coarse[k] for k in range(4)]
    row = row_numbers(8)

    def place(rows, count, first):
        none = jnp.zeros((count - 8,) + rows.shape[1:], jnp.float32)
        return roll(jnp.concatenate([rows, none], axis=0), first, 0)

    def four(got, at, flag):
        tile = got[at - at % 8 : at - at % 8 + 8] * flag
        tile = roll(tile, -4, 0) if at % 8 else tile
        return jnp.where(row < 4, tile, 0.0)

    for got, flag, at_0, at_1, at_2 in (
        (low, inside[2], -1, -1, -1),
        (high, inside[3], 14, 5, 1),
    ):
        sides = jnp.where(row < 3, got[40:48] * flag, 0.0)
        for k in range(10):
            side = jnp.where(four_lanes(8), roll(sides, -(8 + 12 * k), 1), 0.0)
            rows = jnp.where(row < 3, four(got, 4 * k, flag), 0.0)
            f[k] = f[k] + place(jnp.concatenate([rows, side], axis=1), 24, at_0)
        for k in range(6):
            add_m, add_c = split_levels(four(got, 48 + 4 * k, flag))
            m[k] = m[k] + place(add_m, 16, at_1)
            if k < 4:
                c[k] = c[k] + place(add_c, 16, at_2)
    lane = lane_numbers(8)
    to_middle = (lane >> 1) + jnp.where(lane < 96, 0, 64)
    for k in range(4):
        wide = pick_lanes(c[k], to_middle)
        halves[0, k, pl.ds(0, 16, stride=2), :] = wide
        halves[0, k, pl.ds(1, 16, stride=2), :] = wide
    for k in range(6):
        at = (k + 1) // 2
        tail = jnp.where(row < 4, halves[0, at, 8:16], halves[0, at, 24:32])
        m[k] = m[k] + jnp.concatenate([halves[0, at, 0:8], tail], axis=0)
    to_centre = lane >> 1
    to_side = to_centre + 64
    for k in range(6):
        for side, index in enumerate((to_centre, to_side)):
            wide = pick_lanes(m[k], index)
            halves[side, k, pl.ds(0, 16, stride=2), :] = wide
            halves[side, k, pl.ds(1, 16, stride=2), :] = wide
    for k in range(10):
        at = (k + 1) // 2
        sides = []
        for side in range(2):
            tail = jnp.where(row < 4, halves[side, at, 16:24], halves[side, at, 24:32])
            sides.append(jnp.concatenate([halves[side, at, 0:16], tail], axis=0))
        f[k] = f[k] + jnp.concatenate(sides, axis=1)
    for k in range(8):
        here = f[k + 1]
        pressure[k] = here[0:16, 0:128]
        velocity[0, k] = moved[0, k] - 0.5 * (f[k + 2][0:16, 0:128] - f[k][0:16, 0:128])
        slope = roll(here, -1, 0) - roll(here, 1, 0)
        velocity[1, k] = moved[1, k] - 0.5 * slope[0:16, 0:128]
        here = here[0:16]
        slope = roll(here, -1, 1) - roll(here, 1, 1)
        velocity[2, k] = moved[2, k] - 0.5 * slope[:, 0:128]


def project(moved, beyond):
    f32 = jnp.float32
    held = [((10, 24, 256), f32), ((6, 16, 128), f32), ((4, 16, 128), f32)]
    halves = [pltpu.VMEM((2, 8, 32, 128), f32)]
    side, side_2 = ((160, 128), f32), ((32, 128), f32)
    to_low, to_high, to_low_2, to_high_2, *sums = call(
        levels_kernel, [side, side, side_2, side_2] + held, halves, inputs=2
    )(moved, beyond)
    low = shift_ring(to_high, "gx", 1)
    high = shift_ring(to_low, "gx", -1)
    low_2 = shift_ring(to_high_2, "gx", 2)
    high_2 = shift_ring(to_low_2, "gx", -2)
    side = ((72, 128), f32)
    to_low, to_high, *sums = call(
        planes_sum_kernel, [side, side] + held, inputs=7
    )(*sums, low, high, low_2, high_2)
    low = shift_ring(to_high, "gy", 1)
    high = shift_ring(to_low, "gy", -1)
    return call(
        pressure_kernel,
        [((3, 8, 16, 128), f32), ((8, 16, 128), f32)],
        halves,
        inputs=6,
    )(moved, *sums, low, high)


def body(velocity, density, offsets, eighths):
    moved, new_density, past = advect(velocity, density, offsets, eighths)
    new_velocity, pressure = project(moved, past)
    return new_velocity, new_density, pressure


def solution(mesh):
    return jax.shard_map(
        body,
        mesh=mesh,
        in_specs=(
            P(None, "gx", "gy", "gz"),
            P("gx", "gy", "gz"),
            P(None, "gx", "gy", "gz"),
            P(None, "gx", "gy", "gz"),
        ),
        out_specs=(P(None, "gx", "gy", "gz"), P("gx", "gy", "gz"), P("gx", "gy", "gz")),
        check_vma=False,
    )
```

```python
import functools

import jax
import jax.numpy as jnp
from jax import lax
from jax.experimental import pallas as pl
from jax.experimental.pallas import tpu as pltpu
from jax.sharding import PartitionSpec as P

RELAX_WEIGHT = 6.0 / 7.0
VMEM = pl.BlockSpec(memory_space=pltpu.VMEM)
PARAMS = pltpu.CompilerParams(vmem_limit_bytes=48 * 1024 * 1024)


def call(kernel, outs, scratch=(), inputs=0):
    return pl.pallas_call(
        kernel,
        out_shape=[jax.ShapeDtypeStruct(shape, dtype) for shape, dtype in outs],
        in_specs=[VMEM] * inputs,
        out_specs=[VMEM] * len(outs),
        scratch_shapes=list(scratch),
        compiler_params=PARAMS,
    )


def inside_grid():
    found = []
    for axis, step in (("gx", 1), ("gy", 1), ("gz", 1), ("gx", 2)):
        place, count = lax.axis_index(axis), lax.axis_size(axis)
        found.append(jnp.where(place >= step, 1.0, 0.0))
        found.append(jnp.where(place < count - step, 1.0, 0.0))
    return found


def shift_ring(value, axis, step):
    count = lax.axis_size(axis)
    return lax.ppermute(value, axis, [(i, (i + step) % count) for i in range(count)])


def pack_kernel(fields, low_planes, high_planes):
    low_planes[...] = fields[:, 0:4]
    high_planes[...] = fields[:, 4:8]


def own_kernel(fields, code, fields_t, code_t):
    for f in range(4):
        fields_t[f] = fields[f].reshape(128, 128).T
    code_t[...] = code[...].reshape(128, 128).T.astype(jnp.int32)


def rows_kernel(fields, low, high, after, to_low, to_high):
    inside = inside_grid()
    for f in range(4):
        for pair in range(8):
            for half in range(2):
                plane = 2 * pair + half
                if plane < 4:
                    rows = low[f, plane] * inside[0]
                elif plane >= 12:
                    rows = high[f, plane - 12] * inside[1]
                else:
                    rows = fields[f, plane - 4]
                to_low[f, pair, 4 * half : 4 * half + 4] = rows[0:4]
                to_high[f, pair, 4 * half : 4 * half + 4] = rows[12:16]


def planes_kernel(low, high, planes_t):
    inside = inside_grid()
    for f in range(4):
        both = jnp.concatenate(
            [low[f].reshape(64, 128) * inside[0], high[f].reshape(64, 128) * inside[1]], axis=0
        )
        planes_t[f] = both.T


def columns_kernel(fields_t, planes_t, code_t, low, high, after, rows_t, to_low, to_high):
    inside = inside_grid()
    for f in range(4):
        both = jnp.concatenate(
            [low[f].reshape(64, 128) * inside[2], high[f].reshape(64, 128) * inside[3]], axis=0
        )
        turned = both.T
        rows_t[f] = turned
        for group, source in enumerate((fields_t[f], planes_t[f], turned)):
            at = 24 * (3 * f + group)
            to_low[at : at + 24] = source[0:24]
            to_high[at : at + 24] = source[104:128]
    for out, first in ((to_low, 0), (to_high, 112)):
        code = code_t[first : first + 16]
        for k in range(6):
            out[288 + 16 * k : 304 + 16 * k] = ((code >> (3 * k)) & 7).astype(jnp.float32)


def corners_of(code):
    lane = lax.broadcasted_iota(jnp.int32, (8, 128), 1)
    x = (lane >> 4) + (code & 7)
    y = (lane & 15) + ((code >> 3) & 7)
    fx = ((code >> 9) & 7).astype(jnp.float32) / 8.0
    fy = ((code >> 12) & 7).astype(jnp.float32) / 8.0
    corners = []
    for cx in (0, 1):
        for cy in (0, 1):
            xc, yc = x + cx, y + cy
            low_x, high_x = xc < 4, xc >= 12
            in_rows = (yc < 4) | (yc >= 20)
            in_planes = low_x | high_x
            plane = xc - jnp.where(low_x, 0, jnp.where(high_x, 8, 4))
            by_rows = xc * 4 + (yc & 3) + jnp.where(yc >= 20, 64, 0)
            at = jnp.where(in_rows, by_rows, plane * 16 + yc - 4)
            weight = (fx if cx else 1.0 - fx) * (fy if cy else 1.0 - fy)
            in_block = jnp.where(in_rows, 0.0, weight)
            weights = (
                jnp.where(in_planes, 0.0, in_block),
                jnp.where(in_planes, in_block, 0.0),
                jnp.where(in_rows, weight, 0.0),
            )
            corners.append((at, weights))
    return corners


def weights_z(code, shifts):
    level = (code >> 6) & 7
    fz = ((code >> 15) & 7).astype(jnp.float32) / 8.0
    return [
        jnp.where(level == dz, 1.0 - fz, jnp.where(level == dz - 1, fz, 0.0)) for dz in shifts
    ]


def gathered(at, weights, rows_of, count=4):
    parts = [None] * count
    for shift, weight in enumerate(weights):
        for f in range(count):
            taken = jnp.take_along_axis(
                rows_of(f, shift), at, axis=1, mode="promise_in_bounds"
            )
            parts[f] = weight * taken if shift == 0 else parts[f] + weight * taken
    return parts


def group_kernel(group, code_t, source_t, *refs):
    before, after = refs[:-1], refs[-1]
    none = jnp.zeros((8, 128), jnp.float32)

    def tile(step, carry):
        start = pl.multiple_of(step * 8, 8)
        code = code_t[pl.ds(start, 8), :]
        by_shift = weights_z(code, range(9))
        sums = [before[0][f, pl.ds(start, 8), :] if before else none for f in range(4)]
        for at, weights in corners_of(code):
            parts = gathered(
                at, by_shift, lambda f, dz: source_t[f, pl.ds(start + (dz - 4), 8), :]
            )
            for f in range(4):
                sums[f] = sums[f] + weights[group] * parts[f]
        for f in range(4):
            after[f, pl.ds(start, 8), :] = sums[f]
        return carry

    lax.fori_loop(1, 15, tile, 0, unroll=7)


def ends_kernel(code_t, rows_t, before, fields_t, planes_t, after, padded):
    group_kernel(2, code_t, rows_t, before, after)
    none = jnp.zeros((8, 128), jnp.float32)
    for f in range(4):
        for group, source in enumerate((fields_t, planes_t, rows_t)):
            padded[0, f, group, 0:8] = none
            padded[0, f, group, 8:24] = source[f, 0:16]
            padded[1, f, group, 0:16] = source[f, 112:128]
            padded[1, f, group, 16:24] = none
    for end, start in ((0, 0), (1, 120)):
        code = code_t[start : start + 8]
        by_shift = weights_z(code, range(9))
        sums = [none] * 4
        for at, weights in corners_of(code):
            for group in range(3):
                parts = gathered(
                    at, by_shift, lambda f, dz: padded[end, f, group, 4 + dz : 12 + dz]
                )
                for f in range(4):
                    sums[f] = sums[f] + weights[group] * parts[f]
        for f in range(4):
            after[f, start : start + 8] = sums[f]


def edges_kernel(
    code_t, sums_t, fields_t, planes_t, rows_t, low, high,
    moved, density, beyond, moved_t, beyond_t, padded, codes, only_past,
):
    inside = inside_grid()
    none = jnp.zeros((8, 128), jnp.float32)
    for f in range(4):
        for group, source in enumerate((fields_t, planes_t, rows_t)):
            at = 24 * (3 * f + group)
            padded[0, f, group, 0:24] = low[at : at + 24] * inside[4]
            padded[0, f, group, 24:40] = source[f, 0:16]
            padded[1, f, group, 0:16] = source[f, 112:128]
            padded[1, f, group, 16:40] = high[at : at + 24] * inside[5]
            only_past[0, f, group, 0:8] = low[at + 16 : at + 24] * inside[4]
            only_past[0, f, group, 8:16] = none
            only_past[1, f, group, 0:8] = none
            only_past[1, f, group, 8:16] = high[at : at + 8] * inside[5]
    for end, got in ((0, low), (1, high)):
        code = jnp.zeros((16, 128), jnp.int32)
        for k in range(6):
            code = code + (got[288 + 16 * k : 304 + 16 * k].astype(jnp.int32) << (3 * k))
        codes[end] = code
    for f in range(4):
        moved_t[f] = sums_t[f]

    def moved_tile(end, half, start, count):
        code = codes[end, pl.ds(pl.multiple_of(8 * half, 8), 8), :]
        by_shift = weights_z(code, range(9))
        sums = [jnp.zeros((8, 128), jnp.float32)] * count
        for at, weights in corners_of(code):
            for group in range(3):
                parts = gathered(
                    at,
                    by_shift,
                    lambda f, dz: padded[end, f, group, pl.ds(start + (4 + dz), 8), :],
                    count,
                )
                for f in range(count):
                    sums[f] = sums[f] + weights[group] * parts[f]
        return sums

    for end, start, first, shifts in ((0, 0, 4, range(0, 4)), (1, 120, 1, range(5, 9))):
        code = code_t[start : start + 8]
        by_shift = weights_z(code, shifts)
        sums = [sums_t[f, start : start + 8] for f in range(4)]
        for at, weights in corners_of(code):
            for group in range(3):
                parts = gathered(
                    at, by_shift, lambda f, k: only_past[end, f, group, first + k : first + k + 8]
                )
                for f in range(4):
                    sums[f] = sums[f] + weights[group] * parts[f]
        for f in range(4):
            moved_t[f, start : start + 8] = sums[f]

    def outer(step, carry):
        end, half = step // 2, step % 2
        sums = moved_tile(end, half, pl.multiple_of(8 * (end + half), 8), 3)
        flag = jnp.where(end == 0, inside[4], inside[5])
        for f in range(3):
            beyond_t[f, pl.ds(pl.multiple_of(112 * (1 - end) + 8 * half, 8), 8), :] = sums[f] * flag
        return carry

    for f in range(3):
        beyond_t[f] = jnp.zeros((128, 128), jnp.float32)
    lax.fori_loop(0, 4, outer, 0, unroll=2)
    for f in range(3):
        moved[f] = moved_t[f].T.reshape(8, 16, 128)
        beyond[f] = beyond_t[f].T.reshape(8, 16, 128)
    density[...] = moved_t[3].T.reshape(8, 16, 128)


def advect(velocity, density, offsets, eighths):
    f32 = jnp.float32
    turned = ((4, 128, 128), f32)

    def gather(group, *values):
        kernel = functools.partial(group_kernel, group)
        return call(kernel, [turned], inputs=len(values))(*values)[0]

    planes = ((4, 4, 16, 128), f32)
    fields = jnp.concatenate([velocity, density[None]], axis=0)
    low_planes, high_planes = call(pack_kernel, [planes, planes], inputs=1)(fields)
    low = shift_ring(high_planes, "gx", 1)
    high = shift_ring(low_planes, "gx", -1)
    code = (offsets[0] + 4) + (offsets[1] + 4) * 8 + (offsets[2] + 4) * 64
    code = code + eighths[0] * 512 + eighths[1] * 4096 + eighths[2] * 32768
    fields_t, code_t = call(own_kernel, [turned, ((128, 128), jnp.int32)], inputs=2)(
        fields, code.astype(f32)
    )
    sums_t = gather(0, code_t, fields_t)
    strip = ((4, 8, 8, 128), f32)
    to_low, to_high = call(rows_kernel, [strip, strip], inputs=4)(fields, low, high, sums_t)
    rows_low = shift_ring(to_high, "gy", 1)
    rows_high = shift_ring(to_low, "gy", -1)
    (planes_t,) = call(planes_kernel, [turned], inputs=2)(low, high)
    sums_t = gather(1, code_t, planes_t, sums_t)
    edge = ((384, 128), f32)
    rows_t, to_low, to_high = call(
        columns_kernel, [turned, edge, edge], inputs=6
    )(fields_t, planes_t, code_t, rows_low, rows_high, sums_t)
    columns_low = shift_ring(to_high, "gz", 1)
    columns_high = shift_ring(to_low, "gz", -1)
    scratch = [pltpu.VMEM((2, 4, 3, 24, 128), f32)]
    (sums_t,) = call(ends_kernel, [turned], scratch, inputs=5)(
        code_t, rows_t, sums_t, fields_t, planes_t
    )
    scratch = [
        pltpu.VMEM((4, 128, 128), f32),
        pltpu.VMEM((3, 128, 128), f32),
        pltpu.VMEM((2, 4, 3, 40, 128), f32),
        pltpu.VMEM((2, 16, 128), jnp.int32),
        pltpu.VMEM((2, 4, 3, 16, 128), f32),
    ]
    block = ((3, 8, 16, 128), f32)
    return call(
        edges_kernel, [block, ((8, 16, 128), f32), block], scratch, inputs=7
    )(code_t, sums_t, fields_t, planes_t, rows_t, columns_low, columns_high)


def roll(value, shift, dim):
    return pltpu.roll(value, shift % value.shape[dim], dim)


def neighbours(value):
    none = jnp.zeros_like(value[:1])
    summed = jnp.concatenate([value[1:], none], axis=0) + jnp.concatenate([none, value[:-1]], axis=0)
    summed = summed + roll(value, -1, 1) + roll(value, 1, 1)
    return summed + roll(value, -1, 2) + roll(value, 1, 2)


def grid_mask(inside, planes, rows, lanes):
    shape = (rows[0], lanes[0])
    row = lax.broadcasted_iota(jnp.int32, shape, 0)
    lane = lax.broadcasted_iota(jnp.int32, shape, 1)
    by_row = jnp.where(
        row < rows[1], 1.0, jnp.where(row < (rows[0] + rows[1]) // 2, inside[3], inside[2])
    )
    by_lane = jnp.where(
        lane < lanes[1], 1.0, jnp.where(lane < (lanes[0] + lanes[1]) // 2, inside[5], inside[4])
    )
    both = by_row * by_lane
    first, count, block = planes
    parts = [
        both * inside[0] if x < 0 else (both * inside[1] if x >= block else both)
        for x in range(first, first + count)
    ]
    return jnp.stack(parts, axis=0)


def smooth(source, spacing, mask, want_residual):
    relaxation = RELAX_WEIGHT / 6.0
    first = relaxation * spacing * source
    second = first + relaxation * (spacing * source - (6.0 * first - neighbours(first)))
    second = second * mask
    if not want_residual:
        return second
    residual = source - (6.0 * second - neighbours(second)) / spacing
    return second, residual * mask


def pick_lanes(value, index):
    parts = [
        jnp.take_along_axis(value[r : r + 8], index, axis=1, mode="promise_in_bounds")
        for r in range(0, value.shape[0], 8)
    ]
    return jnp.concatenate(parts, axis=0)


def lane_numbers(rows):
    return lax.broadcasted_iota(jnp.int32, (rows, 128), 1)


def row_numbers(rows):
    return lax.broadcasted_iota(jnp.int32, (rows, 128), 0)


def pair_sum(value):
    value = value + roll(value, -1, 1)
    return value + roll(value, -1, 2)


def restrict_fine(residual, halves):
    lane = lane_numbers(8)
    index = (lane * 2) & 127
    left = lane_numbers(16) < 64
    row = row_numbers(8)
    planes = []
    pairs = pair_sum(
        jnp.stack([residual[2 * p] + residual[2 * p + 1] for p in range(8)], axis=0)
    )
    for p in range(8):
        even = []
        for side in range(2):
            both = pairs[p, :, 128 * side : 128 * side + 128]
            halves[side, p, 0:16] = both[0:16]
            halves[side, p, 16:24] = jnp.where(row < 4, both[16:24], 0.0)
            halves[side, p, 24:32] = jnp.where(row >= 4, both[16:24], 0.0)
            even.append(pick_lanes(halves[side, p, pl.ds(0, 16, stride=2), :], index))
        planes.append(jnp.where(left, even[0], even[1]))
    return jnp.stack(planes, axis=0) * 0.125


def restrict_middle(residual, halves):
    index = (lane_numbers(8) * 2) & 127
    row, lane = row_numbers(16), lane_numbers(16)
    valid = ((row < 6) | (row >= 14)) & ((lane < 36) | (lane >= 124))
    pairs = pair_sum(
        jnp.stack([residual[2 * p] + residual[2 * p + 1] for p in range(6)], axis=0)
    )
    planes = []
    for p in range(6):
        halves[0, p, 0:16] = pairs[p]
        even = pick_lanes(halves[0, p, pl.ds(0, 8, stride=2), :], index)
        planes.append(jnp.where(valid, jnp.concatenate([even, even], axis=0), 0.0))
    return jnp.stack(planes, axis=0) * 0.125


def with_planes(value, count):
    none = jnp.zeros((count,) + value.shape[1:], value.dtype)
    return jnp.concatenate([none, value, none], axis=0)


def levels_kernel(
    moved, beyond, to_low, to_high, to_low_2, to_high_2, fine, middle, coarse, halves
):
    inside = inside_grid()
    def spread(a):
        block = jnp.concatenate([moved[a], beyond[a]], axis=2)
        block = jnp.concatenate([block, jnp.zeros((8, 8, 256), jnp.float32)], axis=1)
        return with_planes(block, 4)

    u = spread(0)
    none = jnp.zeros_like(u[:1])
    slope = jnp.concatenate([u[1:], none], axis=0) - jnp.concatenate([none, u[:-1]], axis=0)
    u = spread(1)
    slope = slope + (roll(u, -1, 1) - roll(u, 1, 1))
    u = spread(2)
    slope = slope + (roll(u, -1, 2) - roll(u, 1, 2))
    mask = grid_mask(inside, (-4, 16, 8), (24, 16), (256, 128))
    second, residual = smooth(slope * mask * -0.5, 1.0, mask, True)
    mask = grid_mask(inside, (-4, 12, 4), (16, 8), (128, 64))
    source = with_planes(restrict_fine(residual, halves), 2)
    second_1, residual = smooth(source, 4.0, mask, True)
    mask = grid_mask(inside, (-3, 8, 2), (16, 4), (128, 32))
    source = with_planes(restrict_middle(residual, halves), 1)
    second_2 = smooth(source, 16.0, mask, False)
    lane = lax.broadcasted_iota(jnp.int32, (1, 24, 256), 2)
    second = jnp.where((lane < 132) | (lane >= 252), second, 0.0)
    lane = lane_numbers(16)[None]
    second_1 = jnp.where((lane < 72) | (lane >= 120), second_1, 0.0)
    second_2 = jnp.where((lane < 40) | (lane >= 120), second_2, 0.0)
    fine[...] = second[3:13]
    middle[...] = second_1[3:9]
    coarse[...] = second_2[2:6]
    for out, at_0, at_1, at_2 in ((to_high, 11, 7, 4), (to_low, 2, 1, 0)):
        sides = None
        for k in range(3):
            out[24 * k : 24 * k + 24] = second[at_0 + k][:, 0:128]
            side = roll(second[at_0 + k][:, 128:256], 16 * k, 1)
            sides = side if sides is None else sides + side
        out[72:96] = sides
        for k in range(4):
            out[96 + 16 * k : 112 + 16 * k] = second_1[at_1 + k] + roll(second_2[at_2 + k], 80, 1)
    for k in range(2):
        to_high_2[16 * k : 16 * k + 16] = second_2[6 + k]
        to_low_2[16 * k : 16 * k + 16] = second_2[k]


def near_end(lane):
    return (lane < 8) | (lane >= 120)


def split_levels(both):
    lane = lane_numbers(both.shape[0])
    middle = jnp.where((lane < 72) | (lane >= 120), both, 0.0)
    coarse = jnp.where((lane >= 72) & (lane < 120), both, 0.0)
    return middle, roll(coarse, -80, 1)


def planes_sum_kernel(
    fine, middle, coarse, low, high, low_2, high_2, to_low, to_high, fine_o, middle_o, coarse_o
):
    inside = inside_grid()
    f = [fine[k] for k in range(10)]
    m = [middle[k] for k in range(6)]
    c = [coarse[k] for k in range(4)]
    lane = lane_numbers(24)
    for got, flag, at_0, at_1 in ((low, inside[0], 0, 0), (high, inside[1], 7, 2)):
        sides = got[72:96] * flag
        for k in range(3):
            side = jnp.where(near_end(lane), roll(sides, -16 * k, 1), 0.0)
            centre = got[24 * k : 24 * k + 24] * flag
            f[at_0 + k] = f[at_0 + k] + jnp.concatenate([centre, side], axis=1)
        for k in range(4):
            add_m, add_c = split_levels(got[96 + 16 * k : 112 + 16 * k] * flag)
            m[at_1 + k] = m[at_1 + k] + add_m
            c[k] = c[k] + add_c
    for k in range(2):
        c[k] = c[k] + low_2[16 * k : 16 * k + 16] * inside[6]
        c[2 + k] = c[2 + k] + high_2[16 * k : 16 * k + 16] * inside[7]
    c[0], c[3] = c[0] * inside[0], c[3] * inside[1]
    for k in range(10):
        fine_o[k] = f[k]
    for k in range(6):
        middle_o[k] = m[k]
    for k in range(4):
        coarse_o[k] = c[k]
    for out, at_0, at_1, at_2 in ((to_high, 15, 7, 3), (to_low, -2, -3, -3)):
        sides = None
        for k in range(10):
            rows = roll(f[k], -at_0, 0)[0:8]
            out[4 * k : 4 * k + 4] = rows[0:4, 0:128]
            side = roll(jnp.where(near_end(lane_numbers(8)), rows[:, 128:256], 0.0), 8 + 12 * k, 1)
            sides = side if sides is None else sides + side
        out[40:48] = sides
        for k in range(6):
            rows = roll(m[k], -at_1, 0)[0:8]
            if k < 4:
                rows = rows + roll(roll(c[k], -at_2, 0)[0:8], 80, 1)
            out[48 + 4 * k : 52 + 4 * k] = rows[0:4]


def four_lanes(rows):
    lane = lane_numbers(rows)
    return (lane < 4) | (lane >= 124)


def pressure_kernel(
    moved, fine, middle, coarse, low, high, velocity, pressure, halves
):
    inside = inside_grid()
    f = [fine[k] for k in range(10)]
    m = [middle[k] for k in range(6)]
    c = [coarse[k] for k in range(4)]
    row = row_numbers(8)

    def place(rows, count, first):
        none = jnp.zeros((count - 8,) + rows.shape[1:], jnp.float32)
        return roll(jnp.concatenate([rows, none], axis=0), first, 0)

    def four(got, at, flag):
        tile = got[at - at % 8 : at - at % 8 + 8] * flag
        tile = roll(tile, -4, 0) if at % 8 else tile
        return jnp.where(row < 4, tile, 0.0)

    for got, flag, at_0, at_1, at_2 in (
        (low, inside[2], -1, -1, -1),
        (high, inside[3], 14, 5, 1),
    ):
        sides = jnp.where(row < 3, got[40:48] * flag, 0.0)
        for k in range(10):
            side = jnp.where(four_lanes(8), roll(sides, -(8 + 12 * k), 1), 0.0)
            rows = jnp.where(row < 3, four(got, 4 * k, flag), 0.0)
            f[k] = f[k] + place(jnp.concatenate([rows, side], axis=1), 24, at_0)
        for k in range(6):
            add_m, add_c = split_levels(four(got, 48 + 4 * k, flag))
            m[k] = m[k] + place(add_m, 16, at_1)
            if k < 4:
                c[k] = c[k] + place(add_c, 16, at_2)
    lane = lane_numbers(8)
    to_middle = (lane >> 1) + jnp.where(lane < 96, 0, 64)
    for k in range(4):
        wide = pick_lanes(c[k], to_middle)
        halves[0, k, pl.ds(0, 16, stride=2), :] = wide
        halves[0, k, pl.ds(1, 16, stride=2), :] = wide
    for k in range(6):
        at = (k + 1) // 2
        tail = jnp.where(row < 4, halves[0, at, 8:16], halves[0, at, 24:32])
        m[k] = m[k] + jnp.concatenate([halves[0, at, 0:8], tail], axis=0)
    to_centre = lane >> 1
    to_side = to_centre + 64
    for k in range(6):
        for side, index in enumerate((to_centre, to_side)):
            wide = pick_lanes(m[k], index)
            halves[side, k, pl.ds(0, 16, stride=2), :] = wide
            halves[side, k, pl.ds(1, 16, stride=2), :] = wide
    for k in range(10):
        at = (k + 1) // 2
        sides = []
        for side in range(2):
            tail = jnp.where(row < 4, halves[side, at, 16:24], halves[side, at, 24:32])
            sides.append(jnp.concatenate([halves[side, at, 0:16], tail], axis=0))
        f[k] = f[k] + jnp.concatenate(sides, axis=1)
    for k in range(8):
        here = f[k + 1]
        pressure[k] = here[0:16, 0:128]
        velocity[0, k] = moved[0, k] - 0.5 * (f[k + 2][0:16, 0:128] - f[k][0:16, 0:128])
        slope = roll(here, -1, 0) - roll(here, 1, 0)
        velocity[1, k] = moved[1, k] - 0.5 * slope[0:16, 0:128]
        here = here[0:16]
        slope = roll(here, -1, 1) - roll(here, 1, 1)
        velocity[2, k] = moved[2, k] - 0.5 * slope[:, 0:128]


def project(moved, beyond):
    f32 = jnp.float32
    held = [((10, 24, 256), f32), ((6, 16, 128), f32), ((4, 16, 128), f32)]
    halves = [pltpu.VMEM((2, 8, 32, 128), f32)]
    side, side_2 = ((160, 128), f32), ((32, 128), f32)
    to_low, to_high, to_low_2, to_high_2, *sums = call(
        levels_kernel, [side, side, side_2, side_2] + held, halves, inputs=2
    )(moved, beyond)
    low = shift_ring(to_high, "gx", 1)
    high = shift_ring(to_low, "gx", -1)
    low_2 = shift_ring(to_high_2, "gx", 2)
    high_2 = shift_ring(to_low_2, "gx", -2)
    side = ((72, 128), f32)
    to_low, to_high, *sums = call(
        planes_sum_kernel, [side, side] + held, inputs=7
    )(*sums, low, high, low_2, high_2)
    low = shift_ring(to_high, "gy", 1)
    high = shift_ring(to_low, "gy", -1)
    return call(
        pressure_kernel,
        [((3, 8, 16, 128), f32), ((8, 16, 128), f32)],
        halves,
        inputs=6,
    )(moved, *sums, low, high)


def body(velocity, density, offsets, eighths):
    moved, new_density, past = advect(velocity, density, offsets, eighths)
    new_velocity, pressure = project(moved, past)
    return new_velocity, new_density, pressure


def solution(mesh):
    return jax.shard_map(
        body,
        mesh=mesh,
        in_specs=(
            P(None, "gx", "gy", "gz"),
            P("gx", "gy", "gz"),
            P(None, "gx", "gy", "gz"),
            P(None, "gx", "gy", "gz"),
        ),
        out_specs=(P(None, "gx", "gy", "gz"), P("gx", "gy", "gz"), P("gx", "gy", "gz")),
        check_vma=False,
    )
```

```python
import functools
import itertools

import jax
import jax.numpy as jnp
from jax import lax
from jax.experimental import pallas as pl
from jax.experimental.pallas import tpu as pltpu
from jax.sharding import PartitionSpec as P

RELAX_WEIGHT = 6.0 / 7.0
VMEM = pl.BlockSpec(memory_space=pltpu.VMEM)
PARAMS = pltpu.CompilerParams(vmem_limit_bytes=48 * 1024 * 1024)


def call(kernel, outs, scratch=(), inputs=0):
    return pl.pallas_call(
        kernel,
        out_shape=[jax.ShapeDtypeStruct(shape, dtype) for shape, dtype in outs],
        in_specs=[VMEM] * inputs,
        out_specs=[VMEM] * len(outs),
        scratch_shapes=list(scratch),
        compiler_params=PARAMS,
    )


def inside_grid():
    found = []
    for axis, step in (("gx", 1), ("gy", 1), ("gz", 1), ("gx", 2)):
        place, count = lax.axis_index(axis), lax.axis_size(axis)
        found.append(jnp.where(place >= step, 1.0, 0.0))
        found.append(jnp.where(place < count - step, 1.0, 0.0))
    return found


def shift_ring(value, axis, step):
    count = lax.axis_size(axis)
    return lax.ppermute(value, axis, [(i, (i + step) % count) for i in range(count)])


def shift_split(value, axis, step):
    axes = ("gx", "gy", "gz")
    counts = [lax.axis_size(name) for name in axes]
    pairs = []
    for source, place in enumerate(itertools.product(*[range(count) for count in counts])):
        goal = list(place)
        a = axes.index(axis)
        goal[a] = (goal[a] + (step if place[2] % 2 == 0 else -step)) % counts[a]
        pairs.append((source, (goal[0] * counts[1] + goal[1]) * counts[2] + goal[2]))
    return lax.ppermute(value, axes, pairs)


def second_core():
    return lax.axis_index("gz") % 2 == 1


class Either:
    def __init__(self, first, second):
        self.first, self.second = first, second

    def __getitem__(self, index):
        return jnp.where(second_core(), self.second[index], self.first[index])


def by_direction(first, second):
    return Either(first, second), Either(second, first)


def give(first, second, low, high):
    first[...] = jnp.where(second_core(), low[...], high[...])
    second[...] = jnp.where(second_core(), high[...], low[...])


def pack_kernel(fields, first, second):
    give(first, second, fields[:, 0:4], fields[:, 4:8])


def own_kernel(fields, code, fields_t, code_t):
    for f in range(4):
        fields_t[f] = fields[f].reshape(128, 128).T
    code_t[...] = code[...].reshape(128, 128).T.astype(jnp.int32)


def rows_kernel(fields, first, second, after, to_first, to_second, to_low, to_high):
    inside = inside_grid()
    low, high = by_direction(first, second)
    for f in range(4):
        for pair in range(8):
            for half in range(2):
                plane = 2 * pair + half
                if plane < 4:
                    rows = low[f, plane] * inside[0]
                elif plane >= 12:
                    rows = high[f, plane - 12] * inside[1]
                else:
                    rows = fields[f, plane - 4]
                to_low[f, pair, 4 * half : 4 * half + 4] = rows[0:4]
                to_high[f, pair, 4 * half : 4 * half + 4] = rows[12:16]
    give(to_first, to_second, to_low, to_high)


def planes_kernel(first, second, planes_t):
    inside = inside_grid()
    low, high = by_direction(first, second)
    for f in range(4):
        both = jnp.concatenate(
            [low[f].reshape(64, 128) * inside[0], high[f].reshape(64, 128) * inside[1]], axis=0
        )
        planes_t[f] = both.T


def columns_kernel(fields_t, planes_t, code_t, first, second, after, rows_t, to_low, to_high):
    inside = inside_grid()
    low, high = by_direction(first, second)
    for f in range(4):
        both = jnp.concatenate(
            [low[f].reshape(64, 128) * inside[2], high[f].reshape(64, 128) * inside[3]], axis=0
        )
        turned = both.T
        rows_t[f] = turned
        for group, source in enumerate((fields_t[f], planes_t[f], turned)):
            at = 24 * (3 * f + group)
            to_low[at : at + 24] = source[0:24]
            to_high[at : at + 24] = source[104:128]
    for out, first in ((to_low, 0), (to_high, 112)):
        code = code_t[first : first + 16]
        for k in range(6):
            out[288 + 16 * k : 304 + 16 * k] = ((code >> (3 * k)) & 7).astype(jnp.float32)


def corners_of(code):
    lane = lax.broadcasted_iota(jnp.int32, (8, 128), 1)
    x = (lane >> 4) + (code & 7)
    y = (lane & 15) + ((code >> 3) & 7)
    fx = ((code >> 9) & 7).astype(jnp.float32) / 8.0
    fy = ((code >> 12) & 7).astype(jnp.float32) / 8.0
    corners = []
    for cx in (0, 1):
        for cy in (0, 1):
            xc, yc = x + cx, y + cy
            low_x, high_x = xc < 4, xc >= 12
            in_rows = (yc < 4) | (yc >= 20)
            in_planes = low_x | high_x
            plane = xc - jnp.where(low_x, 0, jnp.where(high_x, 8, 4))
            by_rows = xc * 4 + (yc & 3) + jnp.where(yc >= 20, 64, 0)
            at = jnp.where(in_rows, by_rows, plane * 16 + yc - 4)
            weight = (fx if cx else 1.0 - fx) * (fy if cy else 1.0 - fy)
            in_block = jnp.where(in_rows, 0.0, weight)
            weights = (
                jnp.where(in_planes, 0.0, in_block),
                jnp.where(in_planes, in_block, 0.0),
                jnp.where(in_rows, weight, 0.0),
            )
            corners.append((at, weights))
    return corners


def weights_z(code, shifts):
    level = (code >> 6) & 7
    fz = ((code >> 15) & 7).astype(jnp.float32) / 8.0
    return [
        jnp.where(level == dz, 1.0 - fz, jnp.where(level == dz - 1, fz, 0.0)) for dz in shifts
    ]


def gathered(at, weights, rows_of, count=4):
    parts = [None] * count
    for shift, weight in enumerate(weights):
        for f in range(count):
            taken = jnp.take_along_axis(
                rows_of(f, shift), at, axis=1, mode="promise_in_bounds"
            )
            parts[f] = weight * taken if shift == 0 else parts[f] + weight * taken
    return parts


def group_kernel(group, code_t, source_t, *refs):
    before, after = refs[:-1], refs[-1]
    none = jnp.zeros((8, 128), jnp.float32)

    def tile(step, carry):
        start = pl.multiple_of(step * 8, 8)
        code = code_t[pl.ds(start, 8), :]
        by_shift = weights_z(code, range(9))
        sums = [before[0][f, pl.ds(start, 8), :] if before else none for f in range(4)]
        for at, weights in corners_of(code):
            parts = gathered(
                at, by_shift, lambda f, dz: source_t[f, pl.ds(start + (dz - 4), 8), :]
            )
            for f in range(4):
                sums[f] = sums[f] + weights[group] * parts[f]
        for f in range(4):
            after[f, pl.ds(start, 8), :] = sums[f]
        return carry

    lax.fori_loop(1, 15, tile, 0, unroll=7)


def ends_kernel(code_t, rows_t, before, fields_t, planes_t, after, padded):
    group_kernel(2, code_t, rows_t, before, after)
    none = jnp.zeros((8, 128), jnp.float32)
    for f in range(4):
        for group, source in enumerate((fields_t, planes_t, rows_t)):
            padded[0, f, group, 0:8] = none
            padded[0, f, group, 8:24] = source[f, 0:16]
            padded[1, f, group, 0:16] = source[f, 112:128]
            padded[1, f, group, 16:24] = none
    for end, start in ((0, 0), (1, 120)):
        code = code_t[start : start + 8]
        by_shift = weights_z(code, range(9))
        sums = [none] * 4
        for at, weights in corners_of(code):
            for group in range(3):
                parts = gathered(
                    at, by_shift, lambda f, dz: padded[end, f, group, 4 + dz : 12 + dz]
                )
                for f in range(4):
                    sums[f] = sums[f] + weights[group] * parts[f]
        for f in range(4):
            after[f, start : start + 8] = sums[f]


def edges_kernel(
    code_t, sums_t, fields_t, planes_t, rows_t, low, high,
    moved, density, beyond, moved_t, beyond_t, padded, codes, only_past,
):
    inside = inside_grid()
    none = jnp.zeros((8, 128), jnp.float32)
    for f in range(4):
        for group, source in enumerate((fields_t, planes_t, rows_t)):
            at = 24 * (3 * f + group)
            padded[0, f, group, 0:24] = low[at : at + 24] * inside[4]
            padded[0, f, group, 24:40] = source[f, 0:16]
            padded[1, f, group, 0:16] = source[f, 112:128]
            padded[1, f, group, 16:40] = high[at : at + 24] * inside[5]
            only_past[0, f, group, 0:8] = low[at + 16 : at + 24] * inside[4]
            only_past[0, f, group, 8:16] = none
            only_past[1, f, group, 0:8] = none
            only_past[1, f, group, 8:16] = high[at : at + 8] * inside[5]
    for end, got in ((0, low), (1, high)):
        code = jnp.zeros((16, 128), jnp.int32)
        for k in range(6):
            code = code + (got[288 + 16 * k : 304 + 16 * k].astype(jnp.int32) << (3 * k))
        codes[end] = code
    for f in range(4):
        moved_t[f] = sums_t[f]

    def moved_tile(end, half, start, count):
        code = codes[end, pl.ds(pl.multiple_of(8 * half, 8), 8), :]
        by_shift = weights_z(code, range(9))
        sums = [jnp.zeros((8, 128), jnp.float32)] * count
        for at, weights in corners_of(code):
            for group in range(3):
                parts = gathered(
                    at,
                    by_shift,
                    lambda f, dz: padded[end, f, group, pl.ds(start + (4 + dz), 8), :],
                    count,
                )
                for f in range(count):
                    sums[f] = sums[f] + weights[group] * parts[f]
        return sums

    for end, start, first, shifts in ((0, 0, 4, range(0, 4)), (1, 120, 1, range(5, 9))):
        code = code_t[start : start + 8]
        by_shift = weights_z(code, shifts)
        sums = [sums_t[f, start : start + 8] for f in range(4)]
        for at, weights in corners_of(code):
            for group in range(3):
                parts = gathered(
                    at, by_shift, lambda f, k: only_past[end, f, group, first + k : first + k + 8]
                )
                for f in range(4):
                    sums[f] = sums[f] + weights[group] * parts[f]
        for f in range(4):
            moved_t[f, start : start + 8] = sums[f]

    def outer(step, carry):
        end, half = step // 2, step % 2
        sums = moved_tile(end, half, pl.multiple_of(8 * (end + half), 8), 3)
        flag = jnp.where(end == 0, inside[4], inside[5])
        for f in range(3):
            beyond_t[f, pl.ds(pl.multiple_of(112 * (1 - end) + 8 * half, 8), 8), :] = sums[f] * flag
        return carry

    for f in range(3):
        beyond_t[f] = jnp.zeros((128, 128), jnp.float32)
    lax.fori_loop(0, 4, outer, 0, unroll=2)
    for f in range(3):
        moved[f] = moved_t[f].T.reshape(8, 16, 128)
        beyond[f] = beyond_t[f].T.reshape(8, 16, 128)
    density[...] = moved_t[3].T.reshape(8, 16, 128)


def advect(velocity, density, offsets, eighths):
    f32 = jnp.float32
    turned = ((4, 128, 128), f32)

    def gather(group, *values):
        kernel = functools.partial(group_kernel, group)
        return call(kernel, [turned], inputs=len(values))(*values)[0]

    planes = ((4, 4, 16, 128), f32)
    fields = jnp.concatenate([velocity, density[None]], axis=0)
    first, second = call(pack_kernel, [planes, planes], inputs=1)(fields)
    first = shift_split(first, "gx", 1)
    second = shift_split(second, "gx", -1)
    code = (offsets[0] + 4) + (offsets[1] + 4) * 8 + (offsets[2] + 4) * 64
    code = code + eighths[0] * 512 + eighths[1] * 4096 + eighths[2] * 32768
    fields_t, code_t = call(own_kernel, [turned, ((128, 128), jnp.int32)], inputs=2)(
        fields, code.astype(f32)
    )
    sums_t = gather(0, code_t, fields_t)
    strip = ((4, 8, 8, 128), f32)
    scratch = [pltpu.VMEM(*strip)] * 2
    to_first, to_second = call(rows_kernel, [strip, strip], scratch, inputs=4)(
        fields, first, second, sums_t
    )
    rows_first = shift_split(to_first, "gy", 1)
    rows_second = shift_split(to_second, "gy", -1)
    (planes_t,) = call(planes_kernel, [turned], inputs=2)(first, second)
    sums_t = gather(1, code_t, planes_t, sums_t)
    edge = ((384, 128), f32)
    rows_t, to_low, to_high = call(
        columns_kernel, [turned, edge, edge], inputs=6
    )(fields_t, planes_t, code_t, rows_first, rows_second, sums_t)
    columns_low = shift_ring(to_high, "gz", 1)
    columns_high = shift_ring(to_low, "gz", -1)
    scratch = [pltpu.VMEM((2, 4, 3, 24, 128), f32)]
    (sums_t,) = call(ends_kernel, [turned], scratch, inputs=5)(
        code_t, rows_t, sums_t, fields_t, planes_t
    )
    scratch = [
        pltpu.VMEM((4, 128, 128), f32),
        pltpu.VMEM((3, 128, 128), f32),
        pltpu.VMEM((2, 4, 3, 40, 128), f32),
        pltpu.VMEM((2, 16, 128), jnp.int32),
        pltpu.VMEM((2, 4, 3, 16, 128), f32),
    ]
    block = ((3, 8, 16, 128), f32)
    return call(
        edges_kernel, [block, ((8, 16, 128), f32), block], scratch, inputs=7
    )(code_t, sums_t, fields_t, planes_t, rows_t, columns_low, columns_high)


def roll(value, shift, dim):
    return pltpu.roll(value, shift % value.shape[dim], dim)


def neighbours(value):
    none = jnp.zeros_like(value[:1])
    summed = jnp.concatenate([value[1:], none], axis=0) + jnp.concatenate([none, value[:-1]], axis=0)
    summed = summed + roll(value, -1, 1) + roll(value, 1, 1)
    return summed + roll(value, -1, 2) + roll(value, 1, 2)


def grid_mask(inside, planes, rows, lanes):
    shape = (rows[0], lanes[0])
    row = lax.broadcasted_iota(jnp.int32, shape, 0)
    lane = lax.broadcasted_iota(jnp.int32, shape, 1)
    by_row = jnp.where(
        row < rows[1], 1.0, jnp.where(row < (rows[0] + rows[1]) // 2, inside[3], inside[2])
    )
    by_lane = jnp.where(
        lane < lanes[1], 1.0, jnp.where(lane < (lanes[0] + lanes[1]) // 2, inside[5], inside[4])
    )
    both = by_row * by_lane
    first, count, block = planes
    parts = [
        both * inside[0] if x < 0 else (both * inside[1] if x >= block else both)
        for x in range(first, first + count)
    ]
    return jnp.stack(parts, axis=0)


def smooth(source, spacing, mask, want_residual):
    relaxation = RELAX_WEIGHT / 6.0
    first = relaxation * spacing * source
    second = first + relaxation * (spacing * source - (6.0 * first - neighbours(first)))
    second = second * mask
    if not want_residual:
        return second
    residual = source - (6.0 * second - neighbours(second)) / spacing
    return second, residual * mask


def pick_lanes(value, index):
    parts = [
        jnp.take_along_axis(value[r : r + 8], index, axis=1, mode="promise_in_bounds")
        for r in range(0, value.shape[0], 8)
    ]
    return jnp.concatenate(parts, axis=0)


def lane_numbers(rows):
    return lax.broadcasted_iota(jnp.int32, (rows, 128), 1)


def row_numbers(rows):
    return lax.broadcasted_iota(jnp.int32, (rows, 128), 0)


def pair_sum(value):
    value = value + roll(value, -1, 1)
    return value + roll(value, -1, 2)


def restrict_fine(residual, halves):
    lane = lane_numbers(8)
    index = (lane * 2) & 127
    left = lane_numbers(16) < 64
    row = row_numbers(8)
    planes = []
    pairs = pair_sum(
        jnp.stack([residual[2 * p] + residual[2 * p + 1] for p in range(8)], axis=0)
    )
    for p in range(8):
        even = []
        for side in range(2):
            both = pairs[p, :, 128 * side : 128 * side + 128]
            halves[side, p, 0:16] = both[0:16]
            halves[side, p, 16:24] = jnp.where(row < 4, both[16:24], 0.0)
            halves[side, p, 24:32] = jnp.where(row >= 4, both[16:24], 0.0)
            even.append(pick_lanes(halves[side, p, pl.ds(0, 16, stride=2), :], index))
        planes.append(jnp.where(left, even[0], even[1]))
    return jnp.stack(planes, axis=0) * 0.125


def restrict_middle(residual, halves):
    index = (lane_numbers(8) * 2) & 127
    row, lane = row_numbers(16), lane_numbers(16)
    valid = ((row < 6) | (row >= 14)) & ((lane < 36) | (lane >= 124))
    pairs = pair_sum(
        jnp.stack([residual[2 * p] + residual[2 * p + 1] for p in range(6)], axis=0)
    )
    planes = []
    for p in range(6):
        halves[0, p, 0:16] = pairs[p]
        even = pick_lanes(halves[0, p, pl.ds(0, 8, stride=2), :], index)
        planes.append(jnp.where(valid, jnp.concatenate([even, even], axis=0), 0.0))
    return jnp.stack(planes, axis=0) * 0.125


def with_planes(value, count):
    none = jnp.zeros((count,) + value.shape[1:], value.dtype)
    return jnp.concatenate([none, value, none], axis=0)


def levels_kernel(
    moved, beyond, first, second_, first_2, second_2_, fine, middle, coarse, halves,
    to_low, to_high, to_low_2, to_high_2,
):
    inside = inside_grid()
    def spread(a):
        block = jnp.concatenate([moved[a], beyond[a]], axis=2)
        block = jnp.concatenate([block, jnp.zeros((8, 8, 256), jnp.float32)], axis=1)
        return with_planes(block, 4)

    u = spread(0)
    none = jnp.zeros_like(u[:1])
    slope = jnp.concatenate([u[1:], none], axis=0) - jnp.concatenate([none, u[:-1]], axis=0)
    u = spread(1)
    slope = slope + (roll(u, -1, 1) - roll(u, 1, 1))
    u = spread(2)
    slope = slope + (roll(u, -1, 2) - roll(u, 1, 2))
    mask = grid_mask(inside, (-4, 16, 8), (24, 16), (256, 128))
    second, residual = smooth(slope * mask * -0.5, 1.0, mask, True)
    mask = grid_mask(inside, (-4, 12, 4), (16, 8), (128, 64))
    source = with_planes(restrict_fine(residual, halves), 2)
    second_1, residual = smooth(source, 4.0, mask, True)
    mask = grid_mask(inside, (-3, 8, 2), (16, 4), (128, 32))
    source = with_planes(restrict_middle(residual, halves), 1)
    second_2 = smooth(source, 16.0, mask, False)
    lane = lax.broadcasted_iota(jnp.int32, (1, 24, 256), 2)
    second = jnp.where((lane < 132) | (lane >= 252), second, 0.0)
    lane = lane_numbers(16)[None]
    second_1 = jnp.where((lane < 72) | (lane >= 120), second_1, 0.0)
    second_2 = jnp.where((lane < 40) | (lane >= 120), second_2, 0.0)
    fine[...] = second[3:13]
    middle[...] = second_1[3:9]
    coarse[...] = second_2[2:6]
    for out, at_0, at_1, at_2 in ((to_high, 11, 7, 4), (to_low, 2, 1, 0)):
        sides = None
        for k in range(3):
            out[24 * k : 24 * k + 24] = second[at_0 + k][:, 0:128]
            side = roll(second[at_0 + k][:, 128:256], 16 * k, 1)
            sides = side if sides is None else sides + side
        out[72:96] = sides
        for k in range(4):
            out[96 + 16 * k : 112 + 16 * k] = second_1[at_1 + k] + roll(second_2[at_2 + k], 80, 1)
    for k in range(2):
        to_high_2[16 * k : 16 * k + 16] = second_2[6 + k]
        to_low_2[16 * k : 16 * k + 16] = second_2[k]
    give(first, second_, to_low, to_high)
    give(first_2, second_2_, to_low_2, to_high_2)


def near_end(lane):
    return (lane < 8) | (lane >= 120)


def split_levels(both):
    lane = lane_numbers(both.shape[0])
    middle = jnp.where((lane < 72) | (lane >= 120), both, 0.0)
    coarse = jnp.where((lane >= 72) & (lane < 120), both, 0.0)
    return middle, roll(coarse, -80, 1)


def planes_sum_kernel(
    fine, middle, coarse, first, second, first_2, second_2, to_first, to_second,
    fine_o, middle_o, coarse_o, to_low, to_high,
):
    inside = inside_grid()
    low, high = by_direction(first, second)
    low_2, high_2 = by_direction(first_2, second_2)
    f = [fine[k] for k in range(10)]
    m = [middle[k] for k in range(6)]
    c = [coarse[k] for k in range(4)]
    lane = lane_numbers(24)
    for got, flag, at_0, at_1 in ((low, inside[0], 0, 0), (high, inside[1], 7, 2)):
        sides = got[72:96] * flag
        for k in range(3):
            side = jnp.where(near_end(lane), roll(sides, -16 * k, 1), 0.0)
            centre = got[24 * k : 24 * k + 24] * flag
            f[at_0 + k] = f[at_0 + k] + jnp.concatenate([centre, side], axis=1)
        for k in range(4):
            add_m, add_c = split_levels(got[96 + 16 * k : 112 + 16 * k] * flag)
            m[at_1 + k] = m[at_1 + k] + add_m
            c[k] = c[k] + add_c
    for k in range(2):
        c[k] = c[k] + low_2[16 * k : 16 * k + 16] * inside[6]
        c[2 + k] = c[2 + k] + high_2[16 * k : 16 * k + 16] * inside[7]
    c[0], c[3] = c[0] * inside[0], c[3] * inside[1]
    for k in range(10):
        fine_o[k] = f[k]
    for k in range(6):
        middle_o[k] = m[k]
    for k in range(4):
        coarse_o[k] = c[k]
    for out, at_0, at_1, at_2 in ((to_high, 15, 7, 3), (to_low, -2, -3, -3)):
        sides = None
        for k in range(10):
            rows = roll(f[k], -at_0, 0)[0:8]
            out[4 * k : 4 * k + 4] = rows[0:4, 0:128]
            side = roll(jnp.where(near_end(lane_numbers(8)), rows[:, 128:256], 0.0), 8 + 12 * k, 1)
            sides = side if sides is None else sides + side
        out[40:48] = sides
        for k in range(6):
            rows = roll(m[k], -at_1, 0)[0:8]
            if k < 4:
                rows = rows + roll(roll(c[k], -at_2, 0)[0:8], 80, 1)
            out[48 + 4 * k : 52 + 4 * k] = rows[0:4]
    give(to_first, to_second, to_low, to_high)


def four_lanes(rows):
    lane = lane_numbers(rows)
    return (lane < 4) | (lane >= 124)


def pressure_kernel(
    moved, fine, middle, coarse, first, second, velocity, pressure, halves
):
    inside = inside_grid()
    low, high = by_direction(first, second)
    f = [fine[k] for k in range(10)]
    m = [middle[k] for k in range(6)]
    c = [coarse[k] for k in range(4)]
    row = row_numbers(8)

    def place(rows, count, first):
        none = jnp.zeros((count - 8,) + rows.shape[1:], jnp.float32)
        return roll(jnp.concatenate([rows, none], axis=0), first, 0)

    def four(got, at, flag):
        tile = got[at - at % 8 : at - at % 8 + 8] * flag
        tile = roll(tile, -4, 0) if at % 8 else tile
        return jnp.where(row < 4, tile, 0.0)

    for got, flag, at_0, at_1, at_2 in (
        (low, inside[2], -1, -1, -1),
        (high, inside[3], 14, 5, 1),
    ):
        sides = jnp.where(row < 3, got[40:48] * flag, 0.0)
        for k in range(10):
            side = jnp.where(four_lanes(8), roll(sides, -(8 + 12 * k), 1), 0.0)
            rows = jnp.where(row < 3, four(got, 4 * k, flag), 0.0)
            f[k] = f[k] + place(jnp.concatenate([rows, side], axis=1), 24, at_0)
        for k in range(6):
            add_m, add_c = split_levels(four(got, 48 + 4 * k, flag))
            m[k] = m[k] + place(add_m, 16, at_1)
            if k < 4:
                c[k] = c[k] + place(add_c, 16, at_2)
    lane = lane_numbers(8)
    to_middle = (lane >> 1) + jnp.where(lane < 96, 0, 64)
    for k in range(4):
        wide = pick_lanes(c[k], to_middle)
        halves[0, k, pl.ds(0, 16, stride=2), :] = wide
        halves[0, k, pl.ds(1, 16, stride=2), :] = wide
    for k in range(6):
        at = (k + 1) // 2
        tail = jnp.where(row < 4, halves[0, at, 8:16], halves[0, at, 24:32])
        m[k] = m[k] + jnp.concatenate([halves[0, at, 0:8], tail], axis=0)
    to_centre = lane >> 1
    to_side = to_centre + 64
    for k in range(6):
        for side, index in enumerate((to_centre, to_side)):
            wide = pick_lanes(m[k], index)
            halves[side, k, pl.ds(0, 16, stride=2), :] = wide
            halves[side, k, pl.ds(1, 16, stride=2), :] = wide
    for k in range(10):
        at = (k + 1) // 2
        sides = []
        for side in range(2):
            tail = jnp.where(row < 4, halves[side, at, 16:24], halves[side, at, 24:32])
            sides.append(jnp.concatenate([halves[side, at, 0:16], tail], axis=0))
        f[k] = f[k] + jnp.concatenate(sides, axis=1)
    for k in range(8):
        here = f[k + 1]
        pressure[k] = here[0:16, 0:128]
        velocity[0, k] = moved[0, k] - 0.5 * (f[k + 2][0:16, 0:128] - f[k][0:16, 0:128])
        slope = roll(here, -1, 0) - roll(here, 1, 0)
        velocity[1, k] = moved[1, k] - 0.5 * slope[0:16, 0:128]
        here = here[0:16]
        slope = roll(here, -1, 1) - roll(here, 1, 1)
        velocity[2, k] = moved[2, k] - 0.5 * slope[:, 0:128]


def project(moved, beyond):
    f32 = jnp.float32
    held = [((10, 24, 256), f32), ((6, 16, 128), f32), ((4, 16, 128), f32)]
    halves = [pltpu.VMEM((2, 8, 32, 128), f32)]
    side, side_2 = ((160, 128), f32), ((32, 128), f32)
    scratch = halves + [pltpu.VMEM(*side)] * 2 + [pltpu.VMEM(*side_2)] * 2
    first, second, first_2, second_2, *sums = call(
        levels_kernel, [side, side, side_2, side_2] + held, scratch, inputs=2
    )(moved, beyond)
    first = shift_split(first, "gx", 1)
    second = shift_split(second, "gx", -1)
    first_2 = shift_split(first_2, "gx", 2)
    second_2 = shift_split(second_2, "gx", -2)
    side = ((72, 128), f32)
    first, second, *sums = call(
        planes_sum_kernel, [side, side] + held, [pltpu.VMEM(*side)] * 2, inputs=7
    )(*sums, first, second, first_2, second_2)
    first = shift_split(first, "gy", 1)
    second = shift_split(second, "gy", -1)
    return call(
        pressure_kernel,
        [((3, 8, 16, 128), f32), ((8, 16, 128), f32)],
        halves,
        inputs=6,
    )(moved, *sums, first, second)


def body(velocity, density, offsets, eighths):
    moved, new_density, past = advect(velocity, density, offsets, eighths)
    new_velocity, pressure = project(moved, past)
    return new_velocity, new_density, pressure


def solution(mesh):
    return jax.shard_map(
        body,
        mesh=mesh,
        in_specs=(
            P(None, "gx", "gy", "gz"),
            P("gx", "gy", "gz"),
            P(None, "gx", "gy", "gz"),
            P(None, "gx", "gy", "gz"),
        ),
        out_specs=(P(None, "gx", "gy", "gz"), P("gx", "gy", "gz"), P("gx", "gy", "gz")),
        check_vma=False,
    )
```

```python
import functools

import jax
import jax.numpy as jnp
from jax import lax
from jax.experimental import pallas as pl
from jax.experimental.pallas import tpu as pltpu
from jax.sharding import PartitionSpec as P

RELAX_WEIGHT = 6.0 / 7.0
VMEM = pl.BlockSpec(memory_space=pltpu.VMEM)
PARAMS = pltpu.CompilerParams(vmem_limit_bytes=48 * 1024 * 1024)


def call(kernel, outs, scratch=(), inputs=0):
    return pl.pallas_call(
        kernel,
        out_shape=[jax.ShapeDtypeStruct(shape, dtype) for shape, dtype in outs],
        in_specs=[VMEM] * inputs,
        out_specs=[VMEM] * len(outs),
        scratch_shapes=list(scratch),
        compiler_params=PARAMS,
    )


def inside_grid():
    found = []
    for axis, step in (("gx", 1), ("gy", 1), ("gz", 1), ("gx", 2)):
        place, count = lax.axis_index(axis), lax.axis_size(axis)
        found.append(jnp.where(place >= step, 1.0, 0.0))
        found.append(jnp.where(place < count - step, 1.0, 0.0))
    return found


def shift_ring(value, axis, step):
    count = lax.axis_size(axis)
    return lax.ppermute(value, axis, [(i, (i + step) % count) for i in range(count)])


def pack_kernel(fields, low_planes, high_planes):
    low_planes[...] = fields[:, 0:4]
    high_planes[...] = fields[:, 4:8]


def own_kernel(fields, code, fields_t, code_t):
    for f in range(4):
        fields_t[f] = fields[f].reshape(128, 128).T
    code_t[...] = code[...].reshape(128, 128).T.astype(jnp.int32)


def rows_kernel(fields, low, high, after, to_low, to_high):
    inside = inside_grid()
    for f in range(4):
        for pair in range(8):
            for half in range(2):
                plane = 2 * pair + half
                if plane < 4:
                    rows = low[f, plane] * inside[0]
                elif plane >= 12:
                    rows = high[f, plane - 12] * inside[1]
                else:
                    rows = fields[f, plane - 4]
                to_low[f, pair, 4 * half : 4 * half + 4] = rows[0:4]
                to_high[f, pair, 4 * half : 4 * half + 4] = rows[12:16]


def planes_kernel(low, high, planes_t):
    inside = inside_grid()
    for f in range(4):
        both = jnp.concatenate(
            [low[f].reshape(64, 128) * inside[0], high[f].reshape(64, 128) * inside[1]], axis=0
        )
        planes_t[f] = both.T


def columns_kernel(fields_t, planes_t, code_t, low, high, after, rows_t, to_low, to_high):
    inside = inside_grid()
    for f in range(4):
        both = jnp.concatenate(
            [low[f].reshape(64, 128) * inside[2], high[f].reshape(64, 128) * inside[3]], axis=0
        )
        turned = both.T
        rows_t[f] = turned
        for group, source in enumerate((fields_t[f], planes_t[f], turned)):
            at = 24 * (3 * f + group)
            to_low[at : at + 24] = source[0:24]
            to_high[at : at + 24] = source[104:128]
    for out, first in ((to_low, 0), (to_high, 112)):
        code = code_t[first : first + 16]
        for k in range(6):
            out[288 + 16 * k : 304 + 16 * k] = ((code >> (3 * k)) & 7).astype(jnp.float32)


def corners_of(code):
    lane = lax.broadcasted_iota(jnp.int32, (8, 128), 1)
    x = (lane >> 4) + (code & 7)
    y = (lane & 15) + ((code >> 3) & 7)
    fx = ((code >> 9) & 7).astype(jnp.float32) / 8.0
    fy = ((code >> 12) & 7).astype(jnp.float32) / 8.0
    corners = []
    for cx in (0, 1):
        for cy in (0, 1):
            xc, yc = x + cx, y + cy
            low_x, high_x = xc < 4, xc >= 12
            in_rows = (yc < 4) | (yc >= 20)
            in_planes = low_x | high_x
            plane = xc - jnp.where(low_x, 0, jnp.where(high_x, 8, 4))
            by_rows = xc * 4 + (yc & 3) + jnp.where(yc >= 20, 64, 0)
            at = jnp.where(in_rows, by_rows, plane * 16 + yc - 4)
            weight = (fx if cx else 1.0 - fx) * (fy if cy else 1.0 - fy)
            in_block = jnp.where(in_rows, 0.0, weight)
            weights = (
                jnp.where(in_planes, 0.0, in_block),
                jnp.where(in_planes, in_block, 0.0),
                jnp.where(in_rows, weight, 0.0),
            )
            corners.append((at, weights))
    return corners


def weights_z(code, shifts):
    level = (code >> 6) & 7
    fz = ((code >> 15) & 7).astype(jnp.float32) / 8.0
    return [
        jnp.where(level == dz, 1.0 - fz, jnp.where(level == dz - 1, fz, 0.0)) for dz in shifts
    ]


def gathered(at, weights, rows_of, count=4):
    parts = [None] * count
    for shift, weight in enumerate(weights):
        for f in range(count):
            taken = jnp.take_along_axis(
                rows_of(f, shift), at, axis=1, mode="promise_in_bounds"
            )
            parts[f] = weight * taken if shift == 0 else parts[f] + weight * taken
    return parts


def group_kernel(group, code_t, source_t, *refs):
    before, after = refs[:-1], refs[-1]
    none = jnp.zeros((8, 128), jnp.float32)

    def tile(step, carry):
        start = pl.multiple_of(step * 8, 8)
        code = code_t[pl.ds(start, 8), :]
        by_shift = weights_z(code, range(9))
        sums = [before[0][f, pl.ds(start, 8), :] if before else none for f in range(3)]
        for at, weights in corners_of(code):
            parts = gathered(
                at, by_shift, lambda f, dz: source_t[f, pl.ds(start + (dz - 4), 8), :], 3
            )
            for f in range(3):
                sums[f] = sums[f] + weights[group] * parts[f]
        for f in range(3):
            after[f, pl.ds(start, 8), :] = sums[f]
        return carry

    lax.fori_loop(1, 15, tile, 0, unroll=7)


def ends_kernel(code_t, rows_t, before, fields_t, planes_t, after, padded):
    group_kernel(2, code_t, rows_t, before, after)
    none = jnp.zeros((8, 128), jnp.float32)
    for f in range(3):
        for group, source in enumerate((fields_t, planes_t, rows_t)):
            padded[0, f, group, 0:8] = none
            padded[0, f, group, 8:24] = source[f, 0:16]
            padded[1, f, group, 0:16] = source[f, 112:128]
            padded[1, f, group, 16:24] = none
    for end, start in ((0, 0), (1, 120)):
        code = code_t[start : start + 8]
        by_shift = weights_z(code, range(9))
        sums = [none] * 3
        for at, weights in corners_of(code):
            for group in range(3):
                parts = gathered(
                    at, by_shift, lambda f, dz: padded[end, f, group, 4 + dz : 12 + dz], 3
                )
                for f in range(3):
                    sums[f] = sums[f] + weights[group] * parts[f]
        for f in range(3):
            after[f, start : start + 8] = sums[f]


def edges_kernel(
    code_t, sums_t, fields_t, planes_t, rows_t, low, high,
    moved, beyond, moved_t, beyond_t, padded, codes, only_past,
):
    inside = inside_grid()
    none = jnp.zeros((8, 128), jnp.float32)
    for f in range(3):
        for group, source in enumerate((fields_t, planes_t, rows_t)):
            at = 24 * (3 * f + group)
            padded[0, f, group, 0:24] = low[at : at + 24] * inside[4]
            padded[0, f, group, 24:40] = source[f, 0:16]
            padded[1, f, group, 0:16] = source[f, 112:128]
            padded[1, f, group, 16:40] = high[at : at + 24] * inside[5]
            only_past[0, f, group, 0:8] = low[at + 16 : at + 24] * inside[4]
            only_past[0, f, group, 8:16] = none
            only_past[1, f, group, 0:8] = none
            only_past[1, f, group, 8:16] = high[at : at + 8] * inside[5]
    for end, got in ((0, low), (1, high)):
        code = jnp.zeros((16, 128), jnp.int32)
        for k in range(6):
            code = code + (got[288 + 16 * k : 304 + 16 * k].astype(jnp.int32) << (3 * k))
        codes[end] = code
    for f in range(3):
        moved_t[f] = sums_t[f]

    def moved_tile(end, half, start, count):
        code = codes[end, pl.ds(pl.multiple_of(8 * half, 8), 8), :]
        by_shift = weights_z(code, range(9))
        sums = [jnp.zeros((8, 128), jnp.float32)] * count
        for at, weights in corners_of(code):
            for group in range(3):
                parts = gathered(
                    at,
                    by_shift,
                    lambda f, dz: padded[end, f, group, pl.ds(start + (4 + dz), 8), :],
                    count,
                )
                for f in range(count):
                    sums[f] = sums[f] + weights[group] * parts[f]
        return sums

    for end, start, first, shifts in ((0, 0, 4, range(0, 4)), (1, 120, 1, range(5, 9))):
        code = code_t[start : start + 8]
        by_shift = weights_z(code, shifts)
        sums = [sums_t[f, start : start + 8] for f in range(3)]
        for at, weights in corners_of(code):
            for group in range(3):
                parts = gathered(
                    at,
                    by_shift,
                    lambda f, k: only_past[end, f, group, first + k : first + k + 8],
                    3,
                )
                for f in range(3):
                    sums[f] = sums[f] + weights[group] * parts[f]
        for f in range(3):
            moved_t[f, start : start + 8] = sums[f]

    def outer(step, carry):
        end, half = step // 2, step % 2
        sums = moved_tile(end, half, pl.multiple_of(8 * (end + half), 8), 3)
        flag = jnp.where(end == 0, inside[4], inside[5])
        for f in range(3):
            beyond_t[f, pl.ds(pl.multiple_of(112 * (1 - end) + 8 * half, 8), 8), :] = sums[f] * flag
        return carry

    for f in range(3):
        beyond_t[f] = jnp.zeros((128, 128), jnp.float32)
    lax.fori_loop(0, 4, outer, 0, unroll=2)
    for f in range(3):
        moved[f] = moved_t[f].T.reshape(8, 16, 128)
        beyond[f] = beyond_t[f].T.reshape(8, 16, 128)


def density_kernel(code_t, fields_t, planes_t, rows_t, low, high, after, density, done, padded, moved_t):
    inside = inside_grid()
    for group, source in enumerate((fields_t, planes_t, rows_t)):
        at = 24 * (9 + group)
        padded[group, 0:8] = low[at + 16 : at + 24] * inside[4]
        padded[group, 8:136] = source[3]
        padded[group, 136:144] = high[at : at + 8] * inside[5]

    def tile(step, carry):
        start = pl.multiple_of(step * 8, 8)
        code = code_t[pl.ds(start, 8), :]
        by_shift = weights_z(code, range(9))
        total = jnp.zeros((8, 128), jnp.float32)
        for at, weights in corners_of(code):
            for group in range(3):
                (part,) = gathered(
                    at, by_shift, lambda f, dz: padded[group, pl.ds(start + (4 + dz), 8), :], 1
                )
                total = total + weights[group] * part
        moved_t[pl.ds(start, 8), :] = total
        return carry

    lax.fori_loop(0, 16, tile, 0, unroll=4)
    density[...] = moved_t[...].T.reshape(8, 16, 128)
    done[...] = moved_t[0:8]


def advect(velocity, density, offsets, eighths):
    f32 = jnp.float32
    turned = ((4, 128, 128), f32)
    three = ((3, 128, 128), f32)

    def gather(group, *values):
        kernel = functools.partial(group_kernel, group)
        return call(kernel, [three], inputs=len(values))(*values)[0]

    planes = ((4, 4, 16, 128), f32)
    fields = jnp.concatenate([velocity, density[None]], axis=0)
    low_planes, high_planes = call(pack_kernel, [planes, planes], inputs=1)(fields)
    low = shift_ring(high_planes, "gx", 1)
    high = shift_ring(low_planes, "gx", -1)
    code = (offsets[0] + 4) + (offsets[1] + 4) * 8 + (offsets[2] + 4) * 64
    code = code + eighths[0] * 512 + eighths[1] * 4096 + eighths[2] * 32768
    fields_t, code_t = call(own_kernel, [turned, ((128, 128), jnp.int32)], inputs=2)(
        fields, code.astype(f32)
    )
    sums_t = gather(0, code_t, fields_t)
    strip = ((4, 8, 8, 128), f32)
    to_low, to_high = call(rows_kernel, [strip, strip], inputs=4)(fields, low, high, sums_t)
    rows_low = shift_ring(to_high, "gy", 1)
    rows_high = shift_ring(to_low, "gy", -1)
    (planes_t,) = call(planes_kernel, [turned], inputs=2)(low, high)
    sums_t = gather(1, code_t, planes_t, sums_t)
    edge = ((384, 128), f32)
    rows_t, to_low, to_high = call(
        columns_kernel, [turned, edge, edge], inputs=6
    )(fields_t, planes_t, code_t, rows_low, rows_high, sums_t)
    columns_low = shift_ring(to_high, "gz", 1)
    columns_high = shift_ring(to_low, "gz", -1)
    scratch = [pltpu.VMEM((2, 3, 3, 24, 128), f32)]
    (sums_t,) = call(ends_kernel, [three], scratch, inputs=5)(
        code_t, rows_t, sums_t, fields_t, planes_t
    )
    scratch = [
        pltpu.VMEM((3, 128, 128), f32),
        pltpu.VMEM((3, 128, 128), f32),
        pltpu.VMEM((2, 3, 3, 40, 128), f32),
        pltpu.VMEM((2, 16, 128), jnp.int32),
        pltpu.VMEM((2, 3, 3, 16, 128), f32),
    ]
    block = ((3, 8, 16, 128), f32)
    sources = (fields_t, planes_t, rows_t, columns_low, columns_high)
    moved, beyond = call(edges_kernel, [block, block], scratch, inputs=7)(
        code_t, sums_t, *sources
    )
    return moved, beyond, (code_t,) + sources


def roll(value, shift, dim):
    return pltpu.roll(value, shift % value.shape[dim], dim)


def neighbours(value):
    none = jnp.zeros_like(value[:1])
    summed = jnp.concatenate([value[1:], none], axis=0) + jnp.concatenate([none, value[:-1]], axis=0)
    summed = summed + roll(value, -1, 1) + roll(value, 1, 1)
    return summed + roll(value, -1, 2) + roll(value, 1, 2)


def grid_mask(inside, planes, rows, lanes):
    shape = (rows[0], lanes[0])
    row = lax.broadcasted_iota(jnp.int32, shape, 0)
    lane = lax.broadcasted_iota(jnp.int32, shape, 1)
    by_row = jnp.where(
        row < rows[1], 1.0, jnp.where(row < (rows[0] + rows[1]) // 2, inside[3], inside[2])
    )
    by_lane = jnp.where(
        lane < lanes[1], 1.0, jnp.where(lane < (lanes[0] + lanes[1]) // 2, inside[5], inside[4])
    )
    both = by_row * by_lane
    first, count, block = planes
    parts = [
        both * inside[0] if x < 0 else (both * inside[1] if x >= block else both)
        for x in range(first, first + count)
    ]
    return jnp.stack(parts, axis=0)


def smooth(source, spacing, mask, want_residual):
    relaxation = RELAX_WEIGHT / 6.0
    first = relaxation * spacing * source
    second = first + relaxation * (spacing * source - (6.0 * first - neighbours(first)))
    second = second * mask
    if not want_residual:
        return second
    residual = source - (6.0 * second - neighbours(second)) / spacing
    return second, residual * mask


def pick_lanes(value, index):
    parts = [
        jnp.take_along_axis(value[r : r + 8], index, axis=1, mode="promise_in_bounds")
        for r in range(0, value.shape[0], 8)
    ]
    return jnp.concatenate(parts, axis=0)


def lane_numbers(rows):
    return lax.broadcasted_iota(jnp.int32, (rows, 128), 1)


def row_numbers(rows):
    return lax.broadcasted_iota(jnp.int32, (rows, 128), 0)


def pair_sum(value):
    value = value + roll(value, -1, 1)
    return value + roll(value, -1, 2)


def restrict_fine(residual, halves):
    lane = lane_numbers(8)
    index = (lane * 2) & 127
    left = lane_numbers(16) < 64
    row = row_numbers(8)
    planes = []
    pairs = pair_sum(
        jnp.stack([residual[2 * p] + residual[2 * p + 1] for p in range(8)], axis=0)
    )
    for p in range(8):
        even = []
        for side in range(2):
            both = pairs[p, :, 128 * side : 128 * side + 128]
            halves[side, p, 0:16] = both[0:16]
            halves[side, p, 16:24] = jnp.where(row < 4, both[16:24], 0.0)
            halves[side, p, 24:32] = jnp.where(row >= 4, both[16:24], 0.0)
            even.append(pick_lanes(halves[side, p, pl.ds(0, 16, stride=2), :], index))
        planes.append(jnp.where(left, even[0], even[1]))
    return jnp.stack(planes, axis=0) * 0.125


def restrict_middle(residual, halves):
    index = (lane_numbers(8) * 2) & 127
    row, lane = row_numbers(16), lane_numbers(16)
    valid = ((row < 6) | (row >= 14)) & ((lane < 36) | (lane >= 124))
    pairs = pair_sum(
        jnp.stack([residual[2 * p] + residual[2 * p + 1] for p in range(6)], axis=0)
    )
    planes = []
    for p in range(6):
        halves[0, p, 0:16] = pairs[p]
        even = pick_lanes(halves[0, p, pl.ds(0, 8, stride=2), :], index)
        planes.append(jnp.where(valid, jnp.concatenate([even, even], axis=0), 0.0))
    return jnp.stack(planes, axis=0) * 0.125


def with_planes(value, count):
    none = jnp.zeros((count,) + value.shape[1:], value.dtype)
    return jnp.concatenate([none, value, none], axis=0)


def levels_kernel(
    moved, beyond, to_low, to_high, to_low_2, to_high_2, fine, middle, coarse, halves
):
    inside = inside_grid()
    def spread(a):
        block = jnp.concatenate([moved[a], beyond[a]], axis=2)
        block = jnp.concatenate([block, jnp.zeros((8, 8, 256), jnp.float32)], axis=1)
        return with_planes(block, 4)

    u = spread(0)
    none = jnp.zeros_like(u[:1])
    slope = jnp.concatenate([u[1:], none], axis=0) - jnp.concatenate([none, u[:-1]], axis=0)
    u = spread(1)
    slope = slope + (roll(u, -1, 1) - roll(u, 1, 1))
    u = spread(2)
    slope = slope + (roll(u, -1, 2) - roll(u, 1, 2))
    mask = grid_mask(inside, (-4, 16, 8), (24, 16), (256, 128))
    second, residual = smooth(slope * mask * -0.5, 1.0, mask, True)
    mask = grid_mask(inside, (-4, 12, 4), (16, 8), (128, 64))
    source = with_planes(restrict_fine(residual, halves), 2)
    second_1, residual = smooth(source, 4.0, mask, True)
    mask = grid_mask(inside, (-3, 8, 2), (16, 4), (128, 32))
    source = with_planes(restrict_middle(residual, halves), 1)
    second_2 = smooth(source, 16.0, mask, False)
    lane = lax.broadcasted_iota(jnp.int32, (1, 24, 256), 2)
    second = jnp.where((lane < 132) | (lane >= 252), second, 0.0)
    lane = lane_numbers(16)[None]
    second_1 = jnp.where((lane < 72) | (lane >= 120), second_1, 0.0)
    second_2 = jnp.where((lane < 40) | (lane >= 120), second_2, 0.0)
    fine[...] = second[3:13]
    middle[...] = second_1[3:9]
    coarse[...] = second_2[2:6]
    for out, at_0, at_1, at_2 in ((to_high, 11, 7, 4), (to_low, 2, 1, 0)):
        sides = None
        for k in range(3):
            out[24 * k : 24 * k + 24] = second[at_0 + k][:, 0:128]
            side = roll(second[at_0 + k][:, 128:256], 16 * k, 1)
            sides = side if sides is None else sides + side
        out[72:96] = sides
        for k in range(4):
            out[96 + 16 * k : 112 + 16 * k] = second_1[at_1 + k] + roll(second_2[at_2 + k], 80, 1)
    for k in range(2):
        to_high_2[16 * k : 16 * k + 16] = second_2[6 + k]
        to_low_2[16 * k : 16 * k + 16] = second_2[k]


def near_end(lane):
    return (lane < 8) | (lane >= 120)


def split_levels(both):
    lane = lane_numbers(both.shape[0])
    middle = jnp.where((lane < 72) | (lane >= 120), both, 0.0)
    coarse = jnp.where((lane >= 72) & (lane < 120), both, 0.0)
    return middle, roll(coarse, -80, 1)


def planes_sum_kernel(
    fine, middle, coarse, low, high, low_2, high_2, to_low, to_high, fine_o, middle_o, coarse_o
):
    inside = inside_grid()
    f = [fine[k] for k in range(10)]
    m = [middle[k] for k in range(6)]
    c = [coarse[k] for k in range(4)]
    lane = lane_numbers(24)
    for got, flag, at_0, at_1 in ((low, inside[0], 0, 0), (high, inside[1], 7, 2)):
        sides = got[72:96] * flag
        for k in range(3):
            side = jnp.where(near_end(lane), roll(sides, -16 * k, 1), 0.0)
            centre = got[24 * k : 24 * k + 24] * flag
            f[at_0 + k] = f[at_0 + k] + jnp.concatenate([centre, side], axis=1)
        for k in range(4):
            add_m, add_c = split_levels(got[96 + 16 * k : 112 + 16 * k] * flag)
            m[at_1 + k] = m[at_1 + k] + add_m
            c[k] = c[k] + add_c
    for k in range(2):
        c[k] = c[k] + low_2[16 * k : 16 * k + 16] * inside[6]
        c[2 + k] = c[2 + k] + high_2[16 * k : 16 * k + 16] * inside[7]
    c[0], c[3] = c[0] * inside[0], c[3] * inside[1]
    for k in range(10):
        fine_o[k] = f[k]
    for k in range(6):
        middle_o[k] = m[k]
    for k in range(4):
        coarse_o[k] = c[k]
    for out, at_0, at_1, at_2 in ((to_high, 15, 7, 3), (to_low, -2, -3, -3)):
        sides = None
        for k in range(10):
            rows = roll(f[k], -at_0, 0)[0:8]
            out[4 * k : 4 * k + 4] = rows[0:4, 0:128]
            side = roll(jnp.where(near_end(lane_numbers(8)), rows[:, 128:256], 0.0), 8 + 12 * k, 1)
            sides = side if sides is None else sides + side
        out[40:48] = sides
        for k in range(6):
            rows = roll(m[k], -at_1, 0)[0:8]
            if k < 4:
                rows = rows + roll(roll(c[k], -at_2, 0)[0:8], 80, 1)
            out[48 + 4 * k : 52 + 4 * k] = rows[0:4]


def four_lanes(rows):
    lane = lane_numbers(rows)
    return (lane < 4) | (lane >= 124)


def pressure_kernel(
    moved, fine, middle, coarse, low, high, after, velocity, pressure, halves
):
    inside = inside_grid()
    f = [fine[k] for k in range(10)]
    m = [middle[k] for k in range(6)]
    c = [coarse[k] for k in range(4)]
    row = row_numbers(8)

    def place(rows, count, first):
        none = jnp.zeros((count - 8,) + rows.shape[1:], jnp.float32)
        return roll(jnp.concatenate([rows, none], axis=0), first, 0)

    def four(got, at, flag):
        tile = got[at - at % 8 : at - at % 8 + 8] * flag
        tile = roll(tile, -4, 0) if at % 8 else tile
        return jnp.where(row < 4, tile, 0.0)

    for got, flag, at_0, at_1, at_2 in (
        (low, inside[2], -1, -1, -1),
        (high, inside[3], 14, 5, 1),
    ):
        sides = jnp.where(row < 3, got[40:48] * flag, 0.0)
        for k in range(10):
            side = jnp.where(four_lanes(8), roll(sides, -(8 + 12 * k), 1), 0.0)
            rows = jnp.where(row < 3, four(got, 4 * k, flag), 0.0)
            f[k] = f[k] + place(jnp.concatenate([rows, side], axis=1), 24, at_0)
        for k in range(6):
            add_m, add_c = split_levels(four(got, 48 + 4 * k, flag))
            m[k] = m[k] + place(add_m, 16, at_1)
            if k < 4:
                c[k] = c[k] + place(add_c, 16, at_2)
    lane = lane_numbers(8)
    to_middle = (lane >> 1) + jnp.where(lane < 96, 0, 64)
    for k in range(4):
        wide = pick_lanes(c[k], to_middle)
        halves[0, k, pl.ds(0, 16, stride=2), :] = wide
        halves[0, k, pl.ds(1, 16, stride=2), :] = wide
    for k in range(6):
        at = (k + 1) // 2
        tail = jnp.where(row < 4, halves[0, at, 8:16], halves[0, at, 24:32])
        m[k] = m[k] + jnp.concatenate([halves[0, at, 0:8], tail], axis=0)
    to_centre = lane >> 1
    to_side = to_centre + 64
    for k in range(6):
        for side, index in enumerate((to_centre, to_side)):
            wide = pick_lanes(m[k], index)
            halves[side, k, pl.ds(0, 16, stride=2), :] = wide
            halves[side, k, pl.ds(1, 16, stride=2), :] = wide
    for k in range(10):
        at = (k + 1) // 2
        sides = []
        for side in range(2):
            tail = jnp.where(row < 4, halves[side, at, 16:24], halves[side, at, 24:32])
            sides.append(jnp.concatenate([halves[side, at, 0:16], tail], axis=0))
        f[k] = f[k] + jnp.concatenate(sides, axis=1)
    for k in range(8):
        here = f[k + 1]
        pressure[k] = here[0:16, 0:128]
        velocity[0, k] = moved[0, k] - 0.5 * (f[k + 2][0:16, 0:128] - f[k][0:16, 0:128])
        slope = roll(here, -1, 0) - roll(here, 1, 0)
        velocity[1, k] = moved[1, k] - 0.5 * slope[0:16, 0:128]
        here = here[0:16]
        slope = roll(here, -1, 1) - roll(here, 1, 1)
        velocity[2, k] = moved[2, k] - 0.5 * slope[:, 0:128]


def project(moved, beyond, *sources):
    f32 = jnp.float32
    held = [((10, 24, 256), f32), ((6, 16, 128), f32), ((4, 16, 128), f32)]
    halves = [pltpu.VMEM((2, 8, 32, 128), f32)]
    side, side_2 = ((160, 128), f32), ((32, 128), f32)
    to_low, to_high, to_low_2, to_high_2, *sums = call(
        levels_kernel, [side, side, side_2, side_2] + held, halves, inputs=2
    )(moved, beyond)
    low = shift_ring(to_high, "gx", 1)
    high = shift_ring(to_low, "gx", -1)
    low_2 = shift_ring(to_high_2, "gx", 2)
    high_2 = shift_ring(to_low_2, "gx", -2)
    side = ((72, 128), f32)
    to_low, to_high, *sums = call(
        planes_sum_kernel, [side, side] + held, inputs=7
    )(*sums, low, high, low_2, high_2)
    low = shift_ring(to_high, "gy", 1)
    high = shift_ring(to_low, "gy", -1)
    scratch = [pltpu.VMEM((3, 144, 128), f32), pltpu.VMEM((128, 128), f32)]
    density, done = call(
        density_kernel, [((8, 16, 128), f32), ((8, 128), f32)], scratch, inputs=7
    )(*sources, sums[-1])
    velocity, pressure = call(
        pressure_kernel,
        [((3, 8, 16, 128), f32), ((8, 16, 128), f32)],
        halves,
        inputs=7,
    )(moved, *sums, low, high, done)
    return velocity, density, pressure


def body(velocity, density, offsets, eighths):
    moved, past, sources = advect(velocity, density, offsets, eighths)
    return project(moved, past, *sources)


def solution(mesh):
    return jax.shard_map(
        body,
        mesh=mesh,
        in_specs=(
            P(None, "gx", "gy", "gz"),
            P("gx", "gy", "gz"),
            P(None, "gx", "gy", "gz"),
            P(None, "gx", "gy", "gz"),
        ),
        out_specs=(P(None, "gx", "gy", "gz"), P("gx", "gy", "gz"), P("gx", "gy", "gz")),
        check_vma=False,
    )
```

```python
import functools

import jax
import jax.numpy as jnp
from jax import lax
from jax.experimental import pallas as pl
from jax.experimental.pallas import tpu as pltpu
from jax.sharding import PartitionSpec as P

RELAX_WEIGHT = 6.0 / 7.0
VMEM = pl.BlockSpec(memory_space=pltpu.VMEM)
PARAMS = pltpu.CompilerParams(vmem_limit_bytes=48 * 1024 * 1024)


def call(kernel, outs, scratch=(), inputs=0):
    return pl.pallas_call(
        kernel,
        out_shape=[jax.ShapeDtypeStruct(shape, dtype) for shape, dtype in outs],
        in_specs=[VMEM] * inputs,
        out_specs=[VMEM] * len(outs),
        scratch_shapes=list(scratch),
        compiler_params=PARAMS,
    )


def inside_grid():
    found = []
    for axis, step in (("gx", 1), ("gy", 1), ("gz", 1), ("gx", 2)):
        place, count = lax.axis_index(axis), lax.axis_size(axis)
        found.append(jnp.where(place >= step, 1.0, 0.0))
        found.append(jnp.where(place < count - step, 1.0, 0.0))
    return found


def shift_ring(value, axis, step):
    count = lax.axis_size(axis)
    return lax.ppermute(value, axis, [(i, (i + step) % count) for i in range(count)])


def pack_kernel(fields, low_planes, high_planes):
    low_planes[...] = fields[:, 0:4]
    high_planes[...] = fields[:, 4:8]


def own_kernel(fields, code, fields_t, code_t):
    for f in range(4):
        fields_t[f] = fields[f].reshape(128, 128).T
    code_t[...] = code[...].reshape(128, 128).T.astype(jnp.int32)


def rows_kernel(fields, low, high, after, to_low, to_high):
    inside = inside_grid()
    for f in range(4):
        for pair in range(8):
            for half in range(2):
                plane = 2 * pair + half
                if plane < 4:
                    rows = low[f, plane] * inside[0]
                elif plane >= 12:
                    rows = high[f, plane - 12] * inside[1]
                else:
                    rows = fields[f, plane - 4]
                to_low[f, pair, 4 * half : 4 * half + 4] = rows[0:4]
                to_high[f, pair, 4 * half : 4 * half + 4] = rows[12:16]


def planes_kernel(low, high, planes_t):
    inside = inside_grid()
    for f in range(4):
        both = jnp.concatenate(
            [low[f].reshape(64, 128) * inside[0], high[f].reshape(64, 128) * inside[1]], axis=0
        )
        planes_t[f] = both.T


def columns_kernel(fields_t, planes_t, code_t, low, high, after, rows_t, to_low, to_high):
    inside = inside_grid()
    for f in range(4):
        both = jnp.concatenate(
            [low[f].reshape(64, 128) * inside[2], high[f].reshape(64, 128) * inside[3]], axis=0
        )
        turned = both.T
        rows_t[f] = turned
        for group, source in enumerate((fields_t[f], planes_t[f], turned)):
            at = 24 * (3 * f + group)
            to_low[at : at + 24] = source[0:24]
            to_high[at : at + 24] = source[104:128]
    for out, first in ((to_low, 0), (to_high, 112)):
        code = code_t[first : first + 16]
        for k in range(6):
            out[288 + 16 * k : 304 + 16 * k] = ((code >> (3 * k)) & 7).astype(jnp.float32)


def corners_of(code):
    lane = lax.broadcasted_iota(jnp.int32, (8, 128), 1)
    x = (lane >> 4) + (code & 7)
    y = (lane & 15) + ((code >> 3) & 7)
    fx = ((code >> 9) & 7).astype(jnp.float32) / 8.0
    fy = ((code >> 12) & 7).astype(jnp.float32) / 8.0
    corners = []
    for cx in (0, 1):
        for cy in (0, 1):
            xc, yc = x + cx, y + cy
            low_x, high_x = xc < 4, xc >= 12
            in_rows = (yc < 4) | (yc >= 20)
            in_planes = low_x | high_x
            plane = xc - jnp.where(low_x, 0, jnp.where(high_x, 8, 4))
            by_rows = xc * 4 + (yc & 3) + jnp.where(yc >= 20, 64, 0)
            at = jnp.where(in_rows, by_rows, plane * 16 + yc - 4)
            weight = (fx if cx else 1.0 - fx) * (fy if cy else 1.0 - fy)
            in_block = jnp.where(in_rows, 0.0, weight)
            weights = (
                jnp.where(in_planes, 0.0, in_block),
                jnp.where(in_planes, in_block, 0.0),
                jnp.where(in_rows, weight, 0.0),
            )
            corners.append((at, weights))
    return corners


def weights_z(code, shifts):
    level = (code >> 6) & 7
    fz = ((code >> 15) & 7).astype(jnp.float32) / 8.0
    return [
        jnp.where(level == dz, 1.0 - fz, jnp.where(level == dz - 1, fz, 0.0)) for dz in shifts
    ]


def gathered(at, weights, rows_of, count=4):
    parts = [None] * count
    for shift, weight in enumerate(weights):
        for f in range(count):
            taken = jnp.take_along_axis(
                rows_of(f, shift), at, axis=1, mode="promise_in_bounds"
            )
            parts[f] = weight * taken if shift == 0 else parts[f] + weight * taken
    return parts


def group_kernel(group, code_t, source_t, *refs):
    before, after = refs[:-1], refs[-1]
    none = jnp.zeros((8, 128), jnp.float32)

    def tile(step, carry):
        start = pl.multiple_of(step * 8, 8)
        code = code_t[pl.ds(start, 8), :]
        by_shift = weights_z(code, range(9))
        sums = [before[0][f, pl.ds(start, 8), :] if before else none for f in range(3)]
        for at, weights in corners_of(code):
            parts = gathered(
                at, by_shift, lambda f, dz: source_t[f, pl.ds(start + (dz - 4), 8), :], 3
            )
            for f in range(3):
                sums[f] = sums[f] + weights[group] * parts[f]
        for f in range(3):
            after[f, pl.ds(start, 8), :] = sums[f]
        return carry

    lax.fori_loop(1, 15, tile, 0, unroll=7)


def ends_kernel(code_t, rows_t, before, fields_t, planes_t, after, padded):
    group_kernel(2, code_t, rows_t, before, after)
    none = jnp.zeros((8, 128), jnp.float32)
    for f in range(3):
        for group, source in enumerate((fields_t, planes_t, rows_t)):
            padded[0, f, group, 0:8] = none
            padded[0, f, group, 8:24] = source[f, 0:16]
            padded[1, f, group, 0:16] = source[f, 112:128]
            padded[1, f, group, 16:24] = none
    for end, start in ((0, 0), (1, 120)):
        code = code_t[start : start + 8]
        by_shift = weights_z(code, range(9))
        sums = [none] * 3
        for at, weights in corners_of(code):
            for group in range(3):
                parts = gathered(
                    at, by_shift, lambda f, dz: padded[end, f, group, 4 + dz : 12 + dz], 3
                )
                for f in range(3):
                    sums[f] = sums[f] + weights[group] * parts[f]
        for f in range(3):
            after[f, start : start + 8] = sums[f]


def edges_kernel(
    code_t, sums_t, fields_t, planes_t, rows_t, low, high,
    moved, beyond, moved_t, beyond_t, padded, codes, only_past,
):
    inside = inside_grid()
    none = jnp.zeros((8, 128), jnp.float32)
    for f in range(3):
        for group, source in enumerate((fields_t, planes_t, rows_t)):
            at = 24 * (3 * f + group)
            padded[0, f, group, 0:24] = low[at : at + 24] * inside[4]
            padded[0, f, group, 24:40] = source[f, 0:16]
            padded[1, f, group, 0:16] = source[f, 112:128]
            padded[1, f, group, 16:40] = high[at : at + 24] * inside[5]
            only_past[0, f, group, 0:8] = low[at + 16 : at + 24] * inside[4]
            only_past[0, f, group, 8:16] = none
            only_past[1, f, group, 0:8] = none
            only_past[1, f, group, 8:16] = high[at : at + 8] * inside[5]
    for end, got in ((0, low), (1, high)):
        code = jnp.zeros((16, 128), jnp.int32)
        for k in range(6):
            code = code + (got[288 + 16 * k : 304 + 16 * k].astype(jnp.int32) << (3 * k))
        codes[end] = code
    for f in range(3):
        moved_t[f] = sums_t[f]

    def moved_tile(end, half, start, count):
        code = codes[end, pl.ds(pl.multiple_of(8 * half, 8), 8), :]
        by_shift = weights_z(code, range(9))
        sums = [jnp.zeros((8, 128), jnp.float32)] * count
        for at, weights in corners_of(code):
            for group in range(3):
                parts = gathered(
                    at,
                    by_shift,
                    lambda f, dz: padded[end, f, group, pl.ds(start + (4 + dz), 8), :],
                    count,
                )
                for f in range(count):
                    sums[f] = sums[f] + weights[group] * parts[f]
        return sums

    for end, start, first, shifts in ((0, 0, 4, range(0, 4)), (1, 120, 1, range(5, 9))):
        code = code_t[start : start + 8]
        by_shift = weights_z(code, shifts)
        sums = [sums_t[f, start : start + 8] for f in range(3)]
        for at, weights in corners_of(code):
            for group in range(3):
                parts = gathered(
                    at,
                    by_shift,
                    lambda f, k: only_past[end, f, group, first + k : first + k + 8],
                    3,
                )
                for f in range(3):
                    sums[f] = sums[f] + weights[group] * parts[f]
        for f in range(3):
            moved_t[f, start : start + 8] = sums[f]

    def outer(step, carry):
        end, half = step // 2, step % 2
        sums = moved_tile(end, half, pl.multiple_of(8 * (end + half), 8), 3)
        flag = jnp.where(end == 0, inside[4], inside[5])
        for f in range(3):
            beyond_t[f, pl.ds(pl.multiple_of(112 * (1 - end) + 8 * half, 8), 8), :] = sums[f] * flag
        return carry

    for f in range(3):
        beyond_t[f] = jnp.zeros((128, 128), jnp.float32)
    lax.fori_loop(0, 4, outer, 0, unroll=2)
    for f in range(3):
        moved[f] = moved_t[f].T.reshape(8, 16, 128)
        beyond[f] = beyond_t[f].T.reshape(8, 16, 128)


def low_density_kernel(code_t, fields_t, planes_t, rows_t, low, high, after, half_t, padded):
    density_tiles(0, code_t, fields_t, planes_t, rows_t, low, high, half_t, padded)


def density_kernel(
    code_t, fields_t, planes_t, rows_t, low, high, half_t, after, density, done, padded, moved_t
):
    density_tiles(8, code_t, fields_t, planes_t, rows_t, low, high, moved_t, padded)
    done[...] = moved_t[0:8]
    whole = jnp.concatenate([half_t[...], moved_t[...]], axis=0)
    density[...] = whole.T.reshape(8, 16, 128)


def density_tiles(first, code_t, fields_t, planes_t, rows_t, low, high, moved_t, padded):
    inside = inside_grid()
    for group, source in enumerate((fields_t, planes_t, rows_t)):
        at = 24 * (9 + group)
        padded[group, 0:8] = low[at + 16 : at + 24] * inside[4]
        padded[group, 8:136] = source[3]
        padded[group, 136:144] = high[at : at + 8] * inside[5]

    def tile(step, carry):
        start = pl.multiple_of(step * 8, 8)
        code = code_t[pl.ds(start, 8), :]
        by_shift = weights_z(code, range(9))
        total = jnp.zeros((8, 128), jnp.float32)
        for at, weights in corners_of(code):
            for group in range(3):
                (part,) = gathered(
                    at, by_shift, lambda f, dz: padded[group, pl.ds(start + (4 + dz), 8), :], 1
                )
                total = total + weights[group] * part
        moved_t[pl.ds(pl.multiple_of(start - 8 * first, 8), 8), :] = total
        return carry

    lax.fori_loop(first, first + 8, tile, 0, unroll=4)


def advect(velocity, density, offsets, eighths):
    f32 = jnp.float32
    turned = ((4, 128, 128), f32)
    three = ((3, 128, 128), f32)

    def gather(group, *values):
        kernel = functools.partial(group_kernel, group)
        return call(kernel, [three], inputs=len(values))(*values)[0]

    planes = ((4, 4, 16, 128), f32)
    fields = jnp.concatenate([velocity, density[None]], axis=0)
    low_planes, high_planes = call(pack_kernel, [planes, planes], inputs=1)(fields)
    low = shift_ring(high_planes, "gx", 1)
    high = shift_ring(low_planes, "gx", -1)
    code = (offsets[0] + 4) + (offsets[1] + 4) * 8 + (offsets[2] + 4) * 64
    code = code + eighths[0] * 512 + eighths[1] * 4096 + eighths[2] * 32768
    fields_t, code_t = call(own_kernel, [turned, ((128, 128), jnp.int32)], inputs=2)(
        fields, code.astype(f32)
    )
    sums_t = gather(0, code_t, fields_t)
    strip = ((4, 8, 8, 128), f32)
    to_low, to_high = call(rows_kernel, [strip, strip], inputs=4)(fields, low, high, sums_t)
    rows_low = shift_ring(to_high, "gy", 1)
    rows_high = shift_ring(to_low, "gy", -1)
    (planes_t,) = call(planes_kernel, [turned], inputs=2)(low, high)
    sums_t = gather(1, code_t, planes_t, sums_t)
    edge = ((384, 128), f32)
    rows_t, to_low, to_high = call(
        columns_kernel, [turned, edge, edge], inputs=6
    )(fields_t, planes_t, code_t, rows_low, rows_high, sums_t)
    columns_low = shift_ring(to_high, "gz", 1)
    columns_high = shift_ring(to_low, "gz", -1)
    scratch = [pltpu.VMEM((2, 3, 3, 24, 128), f32)]
    (sums_t,) = call(ends_kernel, [three], scratch, inputs=5)(
        code_t, rows_t, sums_t, fields_t, planes_t
    )
    scratch = [
        pltpu.VMEM((3, 128, 128), f32),
        pltpu.VMEM((3, 128, 128), f32),
        pltpu.VMEM((2, 3, 3, 40, 128), f32),
        pltpu.VMEM((2, 16, 128), jnp.int32),
        pltpu.VMEM((2, 3, 3, 16, 128), f32),
    ]
    block = ((3, 8, 16, 128), f32)
    sources = (fields_t, planes_t, rows_t, columns_low, columns_high)
    moved, beyond = call(edges_kernel, [block, block], scratch, inputs=7)(
        code_t, sums_t, *sources
    )
    return moved, beyond, (code_t,) + sources


def roll(value, shift, dim):
    return pltpu.roll(value, shift % value.shape[dim], dim)


def neighbours(value):
    none = jnp.zeros_like(value[:1])
    summed = jnp.concatenate([value[1:], none], axis=0) + jnp.concatenate([none, value[:-1]], axis=0)
    summed = summed + roll(value, -1, 1) + roll(value, 1, 1)
    return summed + roll(value, -1, 2) + roll(value, 1, 2)


def grid_mask(inside, planes, rows, lanes):
    shape = (rows[0], lanes[0])
    row = lax.broadcasted_iota(jnp.int32, shape, 0)
    lane = lax.broadcasted_iota(jnp.int32, shape, 1)
    by_row = jnp.where(
        row < rows[1], 1.0, jnp.where(row < (rows[0] + rows[1]) // 2, inside[3], inside[2])
    )
    by_lane = jnp.where(
        lane < lanes[1], 1.0, jnp.where(lane < (lanes[0] + lanes[1]) // 2, inside[5], inside[4])
    )
    both = by_row * by_lane
    first, count, block = planes
    parts = [
        both * inside[0] if x < 0 else (both * inside[1] if x >= block else both)
        for x in range(first, first + count)
    ]
    return jnp.stack(parts, axis=0)


def smooth(source, spacing, mask, want_residual):
    relaxation = RELAX_WEIGHT / 6.0
    first = relaxation * spacing * source
    second = first + relaxation * (spacing * source - (6.0 * first - neighbours(first)))
    second = second * mask
    if not want_residual:
        return second
    residual = source - (6.0 * second - neighbours(second)) / spacing
    return second, residual * mask


def pick_lanes(value, index):
    parts = [
        jnp.take_along_axis(value[r : r + 8], index, axis=1, mode="promise_in_bounds")
        for r in range(0, value.shape[0], 8)
    ]
    return jnp.concatenate(parts, axis=0)


def lane_numbers(rows):
    return lax.broadcasted_iota(jnp.int32, (rows, 128), 1)


def row_numbers(rows):
    return lax.broadcasted_iota(jnp.int32, (rows, 128), 0)


def pair_sum(value):
    value = value + roll(value, -1, 1)
    return value + roll(value, -1, 2)


def restrict_fine(residual, halves):
    lane = lane_numbers(8)
    index = (lane * 2) & 127
    left = lane_numbers(16) < 64
    row = row_numbers(8)
    planes = []
    pairs = pair_sum(
        jnp.stack([residual[2 * p] + residual[2 * p + 1] for p in range(8)], axis=0)
    )
    for p in range(8):
        even = []
        for side in range(2):
            both = pairs[p, :, 128 * side : 128 * side + 128]
            halves[side, p, 0:16] = both[0:16]
            halves[side, p, 16:24] = jnp.where(row < 4, both[16:24], 0.0)
            halves[side, p, 24:32] = jnp.where(row >= 4, both[16:24], 0.0)
            even.append(pick_lanes(halves[side, p, pl.ds(0, 16, stride=2), :], index))
        planes.append(jnp.where(left, even[0], even[1]))
    return jnp.stack(planes, axis=0) * 0.125


def restrict_middle(residual, halves):
    index = (lane_numbers(8) * 2) & 127
    row, lane = row_numbers(16), lane_numbers(16)
    valid = ((row < 6) | (row >= 14)) & ((lane < 36) | (lane >= 124))
    pairs = pair_sum(
        jnp.stack([residual[2 * p] + residual[2 * p + 1] for p in range(6)], axis=0)
    )
    planes = []
    for p in range(6):
        halves[0, p, 0:16] = pairs[p]
        even = pick_lanes(halves[0, p, pl.ds(0, 8, stride=2), :], index)
        planes.append(jnp.where(valid, jnp.concatenate([even, even], axis=0), 0.0))
    return jnp.stack(planes, axis=0) * 0.125


def with_planes(value, count):
    none = jnp.zeros((count,) + value.shape[1:], value.dtype)
    return jnp.concatenate([none, value, none], axis=0)


def levels_kernel(
    moved, beyond, to_low, to_high, to_low_2, to_high_2, fine, middle, coarse, halves
):
    inside = inside_grid()
    def spread(a):
        block = jnp.concatenate([moved[a], beyond[a]], axis=2)
        block = jnp.concatenate([block, jnp.zeros((8, 8, 256), jnp.float32)], axis=1)
        return with_planes(block, 4)

    u = spread(0)
    none = jnp.zeros_like(u[:1])
    slope = jnp.concatenate([u[1:], none], axis=0) - jnp.concatenate([none, u[:-1]], axis=0)
    u = spread(1)
    slope = slope + (roll(u, -1, 1) - roll(u, 1, 1))
    u = spread(2)
    slope = slope + (roll(u, -1, 2) - roll(u, 1, 2))
    mask = grid_mask(inside, (-4, 16, 8), (24, 16), (256, 128))
    second, residual = smooth(slope * mask * -0.5, 1.0, mask, True)
    mask = grid_mask(inside, (-4, 12, 4), (16, 8), (128, 64))
    source = with_planes(restrict_fine(residual, halves), 2)
    second_1, residual = smooth(source, 4.0, mask, True)
    mask = grid_mask(inside, (-3, 8, 2), (16, 4), (128, 32))
    source = with_planes(restrict_middle(residual, halves), 1)
    second_2 = smooth(source, 16.0, mask, False)
    lane = lax.broadcasted_iota(jnp.int32, (1, 24, 256), 2)
    second = jnp.where((lane < 132) | (lane >= 252), second, 0.0)
    lane = lane_numbers(16)[None]
    second_1 = jnp.where((lane < 72) | (lane >= 120), second_1, 0.0)
    second_2 = jnp.where((lane < 40) | (lane >= 120), second_2, 0.0)
    fine[...] = second[3:13]
    middle[...] = second_1[3:9]
    coarse[...] = second_2[2:6]
    for out, at_0, at_1, at_2 in ((to_high, 11, 7, 4), (to_low, 2, 1, 0)):
        sides = None
        for k in range(3):
            out[24 * k : 24 * k + 24] = second[at_0 + k][:, 0:128]
            side = roll(second[at_0 + k][:, 128:256], 16 * k, 1)
            sides = side if sides is None else sides + side
        out[72:96] = sides
        for k in range(4):
            out[96 + 16 * k : 112 + 16 * k] = second_1[at_1 + k] + roll(second_2[at_2 + k], 80, 1)
    for k in range(2):
        to_high_2[16 * k : 16 * k + 16] = second_2[6 + k]
        to_low_2[16 * k : 16 * k + 16] = second_2[k]


def near_end(lane):
    return (lane < 8) | (lane >= 120)


def split_levels(both):
    lane = lane_numbers(both.shape[0])
    middle = jnp.where((lane < 72) | (lane >= 120), both, 0.0)
    coarse = jnp.where((lane >= 72) & (lane < 120), both, 0.0)
    return middle, roll(coarse, -80, 1)


def planes_sum_kernel(
    fine, middle, coarse, low, high, low_2, high_2, after, to_low, to_high,
    fine_o, middle_o, coarse_o,
):
    inside = inside_grid()
    f = [fine[k] for k in range(10)]
    m = [middle[k] for k in range(6)]
    c = [coarse[k] for k in range(4)]
    lane = lane_numbers(24)
    for got, flag, at_0, at_1 in ((low, inside[0], 0, 0), (high, inside[1], 7, 2)):
        sides = got[72:96] * flag
        for k in range(3):
            side = jnp.where(near_end(lane), roll(sides, -16 * k, 1), 0.0)
            centre = got[24 * k : 24 * k + 24] * flag
            f[at_0 + k] = f[at_0 + k] + jnp.concatenate([centre, side], axis=1)
        for k in range(4):
            add_m, add_c = split_levels(got[96 + 16 * k : 112 + 16 * k] * flag)
            m[at_1 + k] = m[at_1 + k] + add_m
            c[k] = c[k] + add_c
    for k in range(2):
        c[k] = c[k] + low_2[16 * k : 16 * k + 16] * inside[6]
        c[2 + k] = c[2 + k] + high_2[16 * k : 16 * k + 16] * inside[7]
    c[0], c[3] = c[0] * inside[0], c[3] * inside[1]
    for k in range(10):
        fine_o[k] = f[k]
    for k in range(6):
        middle_o[k] = m[k]
    for k in range(4):
        coarse_o[k] = c[k]
    for out, at_0, at_1, at_2 in ((to_high, 15, 7, 3), (to_low, -2, -3, -3)):
        sides = None
        for k in range(10):
            rows = roll(f[k], -at_0, 0)[0:8]
            out[4 * k : 4 * k + 4] = rows[0:4, 0:128]
            side = roll(jnp.where(near_end(lane_numbers(8)), rows[:, 128:256], 0.0), 8 + 12 * k, 1)
            sides = side if sides is None else sides + side
        out[40:48] = sides
        for k in range(6):
            rows = roll(m[k], -at_1, 0)[0:8]
            if k < 4:
                rows = rows + roll(roll(c[k], -at_2, 0)[0:8], 80, 1)
            out[48 + 4 * k : 52 + 4 * k] = rows[0:4]


def four_lanes(rows):
    lane = lane_numbers(rows)
    return (lane < 4) | (lane >= 124)


def pressure_kernel(
    moved, fine, middle, coarse, low, high, after, velocity, pressure, halves
):
    inside = inside_grid()
    f = [fine[k] for k in range(10)]
    m = [middle[k] for k in range(6)]
    c = [coarse[k] for k in range(4)]
    row = row_numbers(8)

    def place(rows, count, first):
        none = jnp.zeros((count - 8,) + rows.shape[1:], jnp.float32)
        return roll(jnp.concatenate([rows, none], axis=0), first, 0)

    def four(got, at, flag):
        tile = got[at - at % 8 : at - at % 8 + 8] * flag
        tile = roll(tile, -4, 0) if at % 8 else tile
        return jnp.where(row < 4, tile, 0.0)

    for got, flag, at_0, at_1, at_2 in (
        (low, inside[2], -1, -1, -1),
        (high, inside[3], 14, 5, 1),
    ):
        sides = jnp.where(row < 3, got[40:48] * flag, 0.0)
        for k in range(10):
            side = jnp.where(four_lanes(8), roll(sides, -(8 + 12 * k), 1), 0.0)
            rows = jnp.where(row < 3, four(got, 4 * k, flag), 0.0)
            f[k] = f[k] + place(jnp.concatenate([rows, side], axis=1), 24, at_0)
        for k in range(6):
            add_m, add_c = split_levels(four(got, 48 + 4 * k, flag))
            m[k] = m[k] + place(add_m, 16, at_1)
            if k < 4:
                c[k] = c[k] + place(add_c, 16, at_2)
    lane = lane_numbers(8)
    to_middle = (lane >> 1) + jnp.where(lane < 96, 0, 64)
    for k in range(4):
        wide = pick_lanes(c[k], to_middle)
        halves[0, k, pl.ds(0, 16, stride=2), :] = wide
        halves[0, k, pl.ds(1, 16, stride=2), :] = wide
    for k in range(6):
        at = (k + 1) // 2
        tail = jnp.where(row < 4, halves[0, at, 8:16], halves[0, at, 24:32])
        m[k] = m[k] + jnp.concatenate([halves[0, at, 0:8], tail], axis=0)
    to_centre = lane >> 1
    to_side = to_centre + 64
    for k in range(6):
        for side, index in enumerate((to_centre, to_side)):
            wide = pick_lanes(m[k], index)
            halves[side, k, pl.ds(0, 16, stride=2), :] = wide
            halves[side, k, pl.ds(1, 16, stride=2), :] = wide
    for k in range(10):
        at = (k + 1) // 2
        sides = []
        for side in range(2):
            tail = jnp.where(row < 4, halves[side, at, 16:24], halves[side, at, 24:32])
            sides.append(jnp.concatenate([halves[side, at, 0:16], tail], axis=0))
        f[k] = f[k] + jnp.concatenate(sides, axis=1)
    for k in range(8):
        here = f[k + 1]
        pressure[k] = here[0:16, 0:128]
        velocity[0, k] = moved[0, k] - 0.5 * (f[k + 2][0:16, 0:128] - f[k][0:16, 0:128])
        slope = roll(here, -1, 0) - roll(here, 1, 0)
        velocity[1, k] = moved[1, k] - 0.5 * slope[0:16, 0:128]
        here = here[0:16]
        slope = roll(here, -1, 1) - roll(here, 1, 1)
        velocity[2, k] = moved[2, k] - 0.5 * slope[:, 0:128]


def project(moved, beyond, *sources):
    f32 = jnp.float32
    held = [((10, 24, 256), f32), ((6, 16, 128), f32), ((4, 16, 128), f32)]
    halves = [pltpu.VMEM((2, 8, 32, 128), f32)]
    side, side_2 = ((160, 128), f32), ((32, 128), f32)
    to_low, to_high, to_low_2, to_high_2, *sums = call(
        levels_kernel, [side, side, side_2, side_2] + held, halves, inputs=2
    )(moved, beyond)
    low = shift_ring(to_high, "gx", 1)
    high = shift_ring(to_low, "gx", -1)
    low_2 = shift_ring(to_high_2, "gx", 2)
    high_2 = shift_ring(to_low_2, "gx", -2)
    padded = pltpu.VMEM((3, 144, 128), f32)
    (half_t,) = call(low_density_kernel, [((64, 128), f32)], [padded], inputs=7)(
        *sources, sums[-1]
    )
    side = ((72, 128), f32)
    to_low, to_high, *sums = call(
        planes_sum_kernel, [side, side] + held, inputs=8
    )(*sums, low, high, low_2, high_2, half_t)
    low = shift_ring(to_high, "gy", 1)
    high = shift_ring(to_low, "gy", -1)
    scratch = [padded, pltpu.VMEM((64, 128), f32)]
    density, done = call(
        density_kernel, [((8, 16, 128), f32), ((8, 128), f32)], scratch, inputs=8
    )(*sources, half_t, sums[-1])
    velocity, pressure = call(
        pressure_kernel,
        [((3, 8, 16, 128), f32), ((8, 16, 128), f32)],
        halves,
        inputs=7,
    )(moved, *sums, low, high, done)
    return velocity, density, pressure


def body(velocity, density, offsets, eighths):
    moved, past, sources = advect(velocity, density, offsets, eighths)
    return project(moved, past, *sources)


def solution(mesh):
    return jax.shard_map(
        body,
        mesh=mesh,
        in_specs=(
            P(None, "gx", "gy", "gz"),
            P("gx", "gy", "gz"),
            P(None, "gx", "gy", "gz"),
            P(None, "gx", "gy", "gz"),
        ),
        out_specs=(P(None, "gx", "gy", "gz"), P("gx", "gy", "gz"), P("gx", "gy", "gz")),
        check_vma=False,
    )
```

```python
import functools

import jax
import jax.numpy as jnp
from jax import lax
from jax.experimental import pallas as pl
from jax.experimental.pallas import tpu as pltpu
from jax.sharding import PartitionSpec as P

RELAX_WEIGHT = 6.0 / 7.0
VMEM = pl.BlockSpec(memory_space=pltpu.VMEM)
PARAMS = pltpu.CompilerParams(vmem_limit_bytes=48 * 1024 * 1024)


def call(kernel, outs, scratch=(), inputs=0):
    return pl.pallas_call(
        kernel,
        out_shape=[jax.ShapeDtypeStruct(shape, dtype) for shape, dtype in outs],
        in_specs=[VMEM] * inputs,
        out_specs=[VMEM] * len(outs),
        scratch_shapes=list(scratch),
        compiler_params=PARAMS,
    )


def inside_grid():
    found = []
    for axis, step in (("gx", 1), ("gy", 1), ("gz", 1), ("gx", 2)):
        place, count = lax.axis_index(axis), lax.axis_size(axis)
        found.append(jnp.where(place >= step, 1.0, 0.0))
        found.append(jnp.where(place < count - step, 1.0, 0.0))
    return found


def shift_ring(value, axis, step):
    count = lax.axis_size(axis)
    return lax.ppermute(value, axis, [(i, (i + step) % count) for i in range(count)])


def pack_kernel(fields, low_planes, high_planes):
    low_planes[...] = fields[:, 0:4]
    high_planes[...] = fields[:, 4:8]


def own_kernel(fields, code, fields_t, code_t):
    for f in range(4):
        fields_t[f] = fields[f].reshape(128, 128).T
    code_t[...] = code[...].reshape(128, 128).T.astype(jnp.int32)


def rows_kernel(fields, low, high, after, to_low, to_high):
    inside = inside_grid()
    for f in range(4):
        for pair in range(8):
            for half in range(2):
                plane = 2 * pair + half
                if plane < 4:
                    rows = low[f, plane] * inside[0]
                elif plane >= 12:
                    rows = high[f, plane - 12] * inside[1]
                else:
                    rows = fields[f, plane - 4]
                to_low[f, pair, 4 * half : 4 * half + 4] = rows[0:4]
                to_high[f, pair, 4 * half : 4 * half + 4] = rows[12:16]


def planes_kernel(low, high, planes_t):
    inside = inside_grid()
    for f in range(4):
        both = jnp.concatenate(
            [low[f].reshape(64, 128) * inside[0], high[f].reshape(64, 128) * inside[1]], axis=0
        )
        planes_t[f] = both.T


def columns_kernel(fields_t, planes_t, code_t, low, high, after, rows_t, to_low, to_high):
    inside = inside_grid()
    for f in range(4):
        both = jnp.concatenate(
            [low[f].reshape(64, 128) * inside[2], high[f].reshape(64, 128) * inside[3]], axis=0
        )
        turned = both.T
        rows_t[f] = turned
        for group, source in enumerate((fields_t[f], planes_t[f], turned)):
            at = 24 * (3 * f + group)
            to_low[at : at + 24] = source[0:24]
            to_high[at : at + 24] = source[104:128]
    for out, first in ((to_low, 0), (to_high, 112)):
        code = code_t[first : first + 16]
        for k in range(6):
            out[288 + 16 * k : 304 + 16 * k] = ((code >> (3 * k)) & 7).astype(jnp.float32)


def corners_of(code):
    lane = lax.broadcasted_iota(jnp.int32, (8, 128), 1)
    x = (lane >> 4) + (code & 7)
    y = (lane & 15) + ((code >> 3) & 7)
    fx = ((code >> 9) & 7).astype(jnp.float32) / 8.0
    fy = ((code >> 12) & 7).astype(jnp.float32) / 8.0
    corners = []
    for cx in (0, 1):
        for cy in (0, 1):
            xc, yc = x + cx, y + cy
            low_x, high_x = xc < 4, xc >= 12
            in_rows = (yc < 4) | (yc >= 20)
            in_planes = low_x | high_x
            plane = xc - jnp.where(low_x, 0, jnp.where(high_x, 8, 4))
            by_rows = xc * 4 + (yc & 3) + jnp.where(yc >= 20, 64, 0)
            at = jnp.where(in_rows, by_rows, plane * 16 + yc - 4)
            weight = (fx if cx else 1.0 - fx) * (fy if cy else 1.0 - fy)
            in_block = jnp.where(in_rows, 0.0, weight)
            weights = (
                jnp.where(in_planes, 0.0, in_block),
                jnp.where(in_planes, in_block, 0.0),
                jnp.where(in_rows, weight, 0.0),
            )
            corners.append((at, weights))
    return corners


def weights_z(code, shifts):
    level = (code >> 6) & 7
    fz = ((code >> 15) & 7).astype(jnp.float32) / 8.0
    return [
        jnp.where(level == dz, 1.0 - fz, jnp.where(level == dz - 1, fz, 0.0)) for dz in shifts
    ]


def gathered(at, weights, rows_of, count=4):
    parts = [None] * count
    for shift, weight in enumerate(weights):
        for f in range(count):
            taken = jnp.take_along_axis(
                rows_of(f, shift), at, axis=1, mode="promise_in_bounds"
            )
            parts[f] = weight * taken if shift == 0 else parts[f] + weight * taken
    return parts


def group_kernel(group, code_t, source_t, *refs):
    before, after = refs[:-1], refs[-1]
    none = jnp.zeros((8, 128), jnp.float32)

    def tile(step, carry):
        start = pl.multiple_of(step * 8, 8)
        code = code_t[pl.ds(start, 8), :]
        by_shift = weights_z(code, range(9))
        sums = [before[0][f, pl.ds(start, 8), :] if before else none for f in range(3)]
        for at, weights in corners_of(code):
            parts = gathered(
                at, by_shift, lambda f, dz: source_t[f, pl.ds(start + (dz - 4), 8), :], 3
            )
            for f in range(3):
                sums[f] = sums[f] + weights[group] * parts[f]
        for f in range(3):
            after[f, pl.ds(start, 8), :] = sums[f]
        return carry

    lax.fori_loop(1, 15, tile, 0, unroll=7)


def ends_kernel(code_t, rows_t, before, fields_t, planes_t, after, padded):
    group_kernel(2, code_t, rows_t, before, after)
    none = jnp.zeros((8, 128), jnp.float32)
    for f in range(3):
        for group, source in enumerate((fields_t, planes_t, rows_t)):
            padded[0, f, group, 0:8] = none
            padded[0, f, group, 8:24] = source[f, 0:16]
            padded[1, f, group, 0:16] = source[f, 112:128]
            padded[1, f, group, 16:24] = none
    for end, start in ((0, 0), (1, 120)):
        code = code_t[start : start + 8]
        by_shift = weights_z(code, range(9))
        sums = [none] * 3
        for at, weights in corners_of(code):
            for group in range(3):
                parts = gathered(
                    at, by_shift, lambda f, dz: padded[end, f, group, 4 + dz : 12 + dz], 3
                )
                for f in range(3):
                    sums[f] = sums[f] + weights[group] * parts[f]
        for f in range(3):
            after[f, start : start + 8] = sums[f]


def edges_kernel(
    code_t, sums_t, fields_t, planes_t, rows_t, low, high,
    moved, beyond, moved_t, beyond_t, padded, codes, only_past,
):
    inside = inside_grid()
    none = jnp.zeros((8, 128), jnp.float32)
    for f in range(3):
        for group, source in enumerate((fields_t, planes_t, rows_t)):
            at = 24 * (3 * f + group)
            padded[0, f, group, 0:24] = low[at : at + 24] * inside[4]
            padded[0, f, group, 24:40] = source[f, 0:16]
            padded[1, f, group, 0:16] = source[f, 112:128]
            padded[1, f, group, 16:40] = high[at : at + 24] * inside[5]
            only_past[0, f, group, 0:8] = low[at + 16 : at + 24] * inside[4]
            only_past[0, f, group, 8:16] = none
            only_past[1, f, group, 0:8] = none
            only_past[1, f, group, 8:16] = high[at : at + 8] * inside[5]
    for end, got in ((0, low), (1, high)):
        code = jnp.zeros((16, 128), jnp.int32)
        for k in range(6):
            code = code + (got[288 + 16 * k : 304 + 16 * k].astype(jnp.int32) << (3 * k))
        codes[end] = code
    for f in range(3):
        moved_t[f] = sums_t[f]

    def moved_tile(end, half, start, count):
        code = codes[end, pl.ds(pl.multiple_of(8 * half, 8), 8), :]
        by_shift = weights_z(code, range(9))
        sums = [jnp.zeros((8, 128), jnp.float32)] * count
        for at, weights in corners_of(code):
            for group in range(3):
                parts = gathered(
                    at,
                    by_shift,
                    lambda f, dz: padded[end, f, group, pl.ds(start + (4 + dz), 8), :],
                    count,
                )
                for f in range(count):
                    sums[f] = sums[f] + weights[group] * parts[f]
        return sums

    for end, start, first, shifts in ((0, 0, 4, range(0, 4)), (1, 120, 1, range(5, 9))):
        code = code_t[start : start + 8]
        by_shift = weights_z(code, shifts)
        sums = [sums_t[f, start : start + 8] for f in range(3)]
        for at, weights in corners_of(code):
            for group in range(3):
                parts = gathered(
                    at,
                    by_shift,
                    lambda f, k: only_past[end, f, group, first + k : first + k + 8],
                    3,
                )
                for f in range(3):
                    sums[f] = sums[f] + weights[group] * parts[f]
        for f in range(3):
            moved_t[f, start : start + 8] = sums[f]

    def outer(step, carry):
        end, half = step // 2, step % 2
        sums = moved_tile(end, half, pl.multiple_of(8 * (end + half), 8), 3)
        flag = jnp.where(end == 0, inside[4], inside[5])
        for f in range(3):
            beyond_t[f, pl.ds(pl.multiple_of(112 * (1 - end) + 8 * half, 8), 8), :] = sums[f] * flag
        return carry

    for f in range(3):
        beyond_t[f] = jnp.zeros((128, 128), jnp.float32)
    lax.fori_loop(0, 4, outer, 0, unroll=2)
    for f in range(3):
        moved[f] = moved_t[f].T.reshape(8, 16, 128)
        beyond[f] = beyond_t[f].T.reshape(8, 16, 128)


def low_density_kernel(code_t, fields_t, planes_t, rows_t, low, high, after, half_t, padded):
    density_tiles(0, code_t, fields_t, planes_t, rows_t, low, high, half_t, padded)


def density_kernel(
    code_t, fields_t, planes_t, rows_t, low, high, half_t, after, density, done, padded, moved_t
):
    density_tiles(8, code_t, fields_t, planes_t, rows_t, low, high, moved_t, padded)
    done[...] = moved_t[0:8]
    whole = jnp.concatenate([half_t[...], moved_t[...]], axis=0)
    density[...] = whole.T.reshape(8, 16, 128)


def density_tiles(first, code_t, fields_t, planes_t, rows_t, low, high, moved_t, padded):
    inside = inside_grid()
    for group, source in enumerate((fields_t, planes_t, rows_t)):
        at = 24 * (9 + group)
        padded[group, 0:8] = low[at + 16 : at + 24] * inside[4]
        padded[group, 8:136] = source[3]
        padded[group, 136:144] = high[at : at + 8] * inside[5]

    def tile(step, carry):
        start = pl.multiple_of(step * 8, 8)
        code = code_t[pl.ds(start, 8), :]
        by_shift = weights_z(code, range(9))
        total = jnp.zeros((8, 128), jnp.float32)
        for at, weights in corners_of(code):
            for group in range(3):
                (part,) = gathered(
                    at, by_shift, lambda f, dz: padded[group, pl.ds(start + (4 + dz), 8), :], 1
                )
                total = total + weights[group] * part
        moved_t[pl.ds(pl.multiple_of(start - 8 * first, 8), 8), :] = total
        return carry

    lax.fori_loop(first, first + 8, tile, 0, unroll=4)


def advect(velocity, density, offsets, eighths):
    f32 = jnp.float32
    turned = ((4, 128, 128), f32)
    three = ((3, 128, 128), f32)

    def gather(group, *values):
        kernel = functools.partial(group_kernel, group)
        return call(kernel, [three], inputs=len(values))(*values)[0]

    planes = ((4, 4, 16, 128), f32)
    fields = jnp.concatenate([velocity, density[None]], axis=0)
    low_planes, high_planes = call(pack_kernel, [planes, planes], inputs=1)(fields)
    low = shift_ring(high_planes, "gx", 1)
    high = shift_ring(low_planes, "gx", -1)
    code = (offsets[0] + 4) + (offsets[1] + 4) * 8 + (offsets[2] + 4) * 64
    code = code + eighths[0] * 512 + eighths[1] * 4096 + eighths[2] * 32768
    fields_t, code_t = call(own_kernel, [turned, ((128, 128), jnp.int32)], inputs=2)(
        fields, code.astype(f32)
    )
    sums_t = gather(0, code_t, fields_t)
    strip = ((4, 8, 8, 128), f32)
    to_low, to_high = call(rows_kernel, [strip, strip], inputs=4)(fields, low, high, sums_t)
    rows_low = shift_ring(to_high, "gy", 1)
    rows_high = shift_ring(to_low, "gy", -1)
    (planes_t,) = call(planes_kernel, [turned], inputs=2)(low, high)
    sums_t = gather(1, code_t, planes_t, sums_t)
    edge = ((384, 128), f32)
    rows_t, to_low, to_high = call(
        columns_kernel, [turned, edge, edge], inputs=6
    )(fields_t, planes_t, code_t, rows_low, rows_high, sums_t)
    columns_low = shift_ring(to_high, "gz", 1)
    columns_high = shift_ring(to_low, "gz", -1)
    scratch = [pltpu.VMEM((2, 3, 3, 24, 128), f32)]
    (sums_t,) = call(ends_kernel, [three], scratch, inputs=5)(
        code_t, rows_t, sums_t, fields_t, planes_t
    )
    scratch = [
        pltpu.VMEM((3, 128, 128), f32),
        pltpu.VMEM((3, 128, 128), f32),
        pltpu.VMEM((2, 3, 3, 40, 128), f32),
        pltpu.VMEM((2, 16, 128), jnp.int32),
        pltpu.VMEM((2, 3, 3, 16, 128), f32),
    ]
    block = ((3, 8, 16, 128), f32)
    sources = (fields_t, planes_t, rows_t, columns_low, columns_high)
    moved, beyond = call(edges_kernel, [block, block], scratch, inputs=7)(
        code_t, sums_t, *sources
    )
    return moved, beyond, (code_t,) + sources


def roll(value, shift, dim):
    return pltpu.roll(value, shift % value.shape[dim], dim)


def neighbours(value):
    none = jnp.zeros_like(value[:1])
    summed = jnp.concatenate([value[1:], none], axis=0) + jnp.concatenate([none, value[:-1]], axis=0)
    summed = summed + roll(value, -1, 1) + roll(value, 1, 1)
    return summed + roll(value, -1, 2) + roll(value, 1, 2)


def grid_mask(inside, planes, rows, lanes):
    shape = (rows[0], lanes[0])
    row = lax.broadcasted_iota(jnp.int32, shape, 0)
    lane = lax.broadcasted_iota(jnp.int32, shape, 1)
    by_row = jnp.where(
        row < rows[1], 1.0, jnp.where(row < (rows[0] + rows[1]) // 2, inside[3], inside[2])
    )
    by_lane = jnp.where(
        lane < lanes[1], 1.0, jnp.where(lane < (lanes[0] + lanes[1]) // 2, inside[5], inside[4])
    )
    both = by_row * by_lane
    first, count, block = planes
    parts = [
        both * inside[0] if x < 0 else (both * inside[1] if x >= block else both)
        for x in range(first, first + count)
    ]
    return jnp.stack(parts, axis=0)


def smooth(source, spacing, mask, want_residual):
    relaxation = RELAX_WEIGHT / 6.0
    first = relaxation * spacing * source
    second = first + relaxation * (spacing * source - (6.0 * first - neighbours(first)))
    second = second * mask
    if not want_residual:
        return second
    residual = source - (6.0 * second - neighbours(second)) / spacing
    return second, residual * mask


def pick_lanes(value, index):
    parts = [
        jnp.take_along_axis(value[r : r + 8], index, axis=1, mode="promise_in_bounds")
        for r in range(0, value.shape[0], 8)
    ]
    return jnp.concatenate(parts, axis=0)


def lane_numbers(rows):
    return lax.broadcasted_iota(jnp.int32, (rows, 128), 1)


def row_numbers(rows):
    return lax.broadcasted_iota(jnp.int32, (rows, 128), 0)


def pair_sum(value):
    value = value + roll(value, -1, 1)
    return value + roll(value, -1, 2)


def restrict_fine(residual, halves):
    lane = lane_numbers(8)
    index = (lane * 2) & 127
    left = lane_numbers(16) < 64
    row = row_numbers(8)
    planes = []
    pairs = pair_sum(
        jnp.stack([residual[2 * p] + residual[2 * p + 1] for p in range(8)], axis=0)
    )
    for p in range(8):
        even = []
        for side in range(2):
            both = pairs[p, :, 128 * side : 128 * side + 128]
            halves[side, p, 0:16] = both[0:16]
            halves[side, p, 16:24] = jnp.where(row < 4, both[16:24], 0.0)
            halves[side, p, 24:32] = jnp.where(row >= 4, both[16:24], 0.0)
            even.append(pick_lanes(halves[side, p, pl.ds(0, 16, stride=2), :], index))
        planes.append(jnp.where(left, even[0], even[1]))
    return jnp.stack(planes, axis=0) * 0.125


def restrict_middle(residual, halves):
    index = (lane_numbers(8) * 2) & 127
    row, lane = row_numbers(16), lane_numbers(16)
    valid = ((row < 6) | (row >= 14)) & ((lane < 36) | (lane >= 124))
    pairs = pair_sum(
        jnp.stack([residual[2 * p] + residual[2 * p + 1] for p in range(6)], axis=0)
    )
    planes = []
    for p in range(6):
        halves[0, p, 0:16] = pairs[p]
        even = pick_lanes(halves[0, p, pl.ds(0, 8, stride=2), :], index)
        planes.append(jnp.where(valid, jnp.concatenate([even, even], axis=0), 0.0))
    return jnp.stack(planes, axis=0) * 0.125


def with_planes(value, count):
    none = jnp.zeros((count,) + value.shape[1:], value.dtype)
    return jnp.concatenate([none, value, none], axis=0)


def levels_kernel(
    moved, beyond, to_low, to_high, to_low_2, to_high_2, fine, middle, coarse, halves
):
    inside = inside_grid()
    def spread(a):
        block = jnp.concatenate([moved[a], beyond[a]], axis=2)
        block = jnp.concatenate([block, jnp.zeros((8, 8, 256), jnp.float32)], axis=1)
        return with_planes(block, 4)

    u = spread(0)
    none = jnp.zeros_like(u[:1])
    slope = jnp.concatenate([u[1:], none], axis=0) - jnp.concatenate([none, u[:-1]], axis=0)
    u = spread(1)
    slope = slope + (roll(u, -1, 1) - roll(u, 1, 1))
    u = spread(2)
    slope = slope + (roll(u, -1, 2) - roll(u, 1, 2))
    mask = grid_mask(inside, (-4, 16, 8), (24, 16), (256, 128))
    second, residual = smooth(slope * mask * -0.5, 1.0, mask, True)
    mask = grid_mask(inside, (-4, 12, 4), (16, 8), (128, 64))
    source = with_planes(restrict_fine(residual, halves), 2)
    second_1, residual = smooth(source, 4.0, mask, True)
    mask = grid_mask(inside, (-3, 8, 2), (16, 4), (128, 32))
    source = with_planes(restrict_middle(residual, halves), 1)
    second_2 = smooth(source, 16.0, mask, False)
    lane = lax.broadcasted_iota(jnp.int32, (1, 24, 256), 2)
    second = jnp.where((lane < 132) | (lane >= 252), second, 0.0)
    lane = lane_numbers(16)[None]
    second_1 = jnp.where((lane < 72) | (lane >= 120), second_1, 0.0)
    second_2 = jnp.where((lane < 40) | (lane >= 120), second_2, 0.0)
    fine[...] = second[3:13]
    middle[...] = second_1[3:9]
    coarse[...] = second_2[2:6]
    for out, at_0, at_1, at_2 in ((to_high, 11, 7, 4), (to_low, 2, 1, 0)):
        sides = None
        for k in range(3):
            out[24 * k : 24 * k + 24] = second[at_0 + k][:, 0:128]
            side = roll(second[at_0 + k][:, 128:256], 16 * k, 1)
            sides = side if sides is None else sides + side
        out[72:96] = sides
        for k in range(4):
            out[96 + 16 * k : 112 + 16 * k] = second_1[at_1 + k] + roll(second_2[at_2 + k], 80, 1)
    for k in range(2):
        to_high_2[16 * k : 16 * k + 16] = second_2[6 + k]
        to_low_2[16 * k : 16 * k + 16] = second_2[k]


def near_end(lane):
    return (lane < 8) | (lane >= 120)


def split_levels(both):
    lane = lane_numbers(both.shape[0])
    middle = jnp.where((lane < 72) | (lane >= 120), both, 0.0)
    coarse = jnp.where((lane >= 72) & (lane < 120), both, 0.0)
    return middle, roll(coarse, -80, 1)


def planes_sum_kernel(
    fine, middle, coarse, low, high, low_2, high_2, after, to_low, to_high,
    fine_o, middle_o, coarse_o,
):
    inside = inside_grid()
    f = [fine[k] for k in range(10)]
    m = [middle[k] for k in range(6)]
    c = [coarse[k] for k in range(4)]
    lane = lane_numbers(24)
    for got, flag, at_0, at_1 in ((low, inside[0], 0, 0), (high, inside[1], 7, 2)):
        sides = got[72:96] * flag
        for k in range(3):
            side = jnp.where(near_end(lane), roll(sides, -16 * k, 1), 0.0)
            centre = got[24 * k : 24 * k + 24] * flag
            f[at_0 + k] = f[at_0 + k] + jnp.concatenate([centre, side], axis=1)
        for k in range(4):
            add_m, add_c = split_levels(got[96 + 16 * k : 112 + 16 * k] * flag)
            m[at_1 + k] = m[at_1 + k] + add_m
            c[k] = c[k] + add_c
    for k in range(2):
        c[k] = c[k] + low_2[16 * k : 16 * k + 16] * inside[6]
        c[2 + k] = c[2 + k] + high_2[16 * k : 16 * k + 16] * inside[7]
    c[0], c[3] = c[0] * inside[0], c[3] * inside[1]
    for k in range(10):
        fine_o[k] = f[k]
    for k in range(6):
        middle_o[k] = m[k]
    for k in range(4):
        coarse_o[k] = c[k]
    for out, at_0, at_1, at_2 in ((to_high, 15, 7, 3), (to_low, -2, -3, -3)):
        sides = None
        for k in range(10):
            rows = roll(f[k], -at_0, 0)[0:8]
            out[4 * k : 4 * k + 4] = rows[0:4, 0:128]
            side = roll(jnp.where(near_end(lane_numbers(8)), rows[:, 128:256], 0.0), 8 + 12 * k, 1)
            sides = side if sides is None else sides + side
        out[40:48] = sides
        for k in range(6):
            rows = roll(m[k], -at_1, 0)[0:8]
            if k < 4:
                rows = rows + roll(roll(c[k], -at_2, 0)[0:8], 80, 1)
            out[48 + 4 * k : 52 + 4 * k] = rows[0:4]


def four_lanes(rows):
    lane = lane_numbers(rows)
    return (lane < 4) | (lane >= 124)


def pressure_kernel(
    moved, fine, middle, coarse, low, high, after, velocity, pressure, halves
):
    inside = inside_grid()
    f = [fine[k] for k in range(10)]
    m = [middle[k] for k in range(6)]
    c = [coarse[k] for k in range(4)]
    row = row_numbers(8)

    def place(rows, count, first):
        none = jnp.zeros((count - 8,) + rows.shape[1:], jnp.float32)
        return roll(jnp.concatenate([rows, none], axis=0), first, 0)

    def four(got, at, flag):
        tile = got[at - at % 8 : at - at % 8 + 8] * flag
        tile = roll(tile, -4, 0) if at % 8 else tile
        return jnp.where(row < 4, tile, 0.0)

    for got, flag, at_0, at_1, at_2 in (
        (low, inside[2], -1, -1, -1),
        (high, inside[3], 14, 5, 1),
    ):
        sides = jnp.where(row < 3, got[40:48] * flag, 0.0)
        for k in range(10):
            side = jnp.where(four_lanes(8), roll(sides, -(8 + 12 * k), 1), 0.0)
            rows = jnp.where(row < 3, four(got, 4 * k, flag), 0.0)
            f[k] = f[k] + place(jnp.concatenate([rows, side], axis=1), 24, at_0)
        for k in range(6):
            add_m, add_c = split_levels(four(got, 48 + 4 * k, flag))
            m[k] = m[k] + place(add_m, 16, at_1)
            if k < 4:
                c[k] = c[k] + place(add_c, 16, at_2)
    lane = lane_numbers(8)
    to_middle = (lane >> 1) + jnp.where(lane < 96, 0, 64)
    for k in range(4):
        wide = pick_lanes(c[k], to_middle)
        halves[0, k, pl.ds(0, 16, stride=2), :] = wide
        halves[0, k, pl.ds(1, 16, stride=2), :] = wide
    for k in range(6):
        at = (k + 1) // 2
        tail = jnp.where(row < 4, halves[0, at, 8:16], halves[0, at, 24:32])
        m[k] = m[k] + jnp.concatenate([halves[0, at, 0:8], tail], axis=0)
    to_centre = lane >> 1
    to_side = to_centre + 64
    for k in range(6):
        for side, index in enumerate((to_centre, to_side)):
            wide = pick_lanes(m[k], index)
            halves[side, k, pl.ds(0, 16, stride=2), :] = wide
            halves[side, k, pl.ds(1, 16, stride=2), :] = wide
    for k in range(10):
        at = (k + 1) // 2
        sides = []
        for side in range(2):
            tail = jnp.where(row < 4, halves[side, at, 16:24], halves[side, at, 24:32])
            sides.append(jnp.concatenate([halves[side, at, 0:16], tail], axis=0))
        f[k] = f[k] + jnp.concatenate(sides, axis=1)
    for k in range(8):
        here = f[k + 1]
        pressure[k] = here[0:16, 0:128]
        velocity[0, k] = moved[0, k] - 0.5 * (f[k + 2][0:16, 0:128] - f[k][0:16, 0:128])
        slope = roll(here, -1, 0) - roll(here, 1, 0)
        velocity[1, k] = moved[1, k] - 0.5 * slope[0:16, 0:128]
        here = here[0:16]
        slope = roll(here, -1, 1) - roll(here, 1, 1)
        velocity[2, k] = moved[2, k] - 0.5 * slope[:, 0:128]


def project(moved, beyond, *sources):
    f32 = jnp.float32
    held = [((10, 24, 256), f32), ((6, 16, 128), f32), ((4, 16, 128), f32)]
    halves = [pltpu.VMEM((2, 8, 32, 128), f32)]
    side, side_2 = ((160, 128), f32), ((32, 128), f32)
    to_low, to_high, to_low_2, to_high_2, *sums = call(
        levels_kernel, [side, side, side_2, side_2] + held, halves, inputs=2
    )(moved, beyond)
    low_2 = shift_ring(to_high_2, "gx", 2)
    high_2 = shift_ring(to_low_2, "gx", -2)
    low = shift_ring(to_high, "gx", 1)
    high = shift_ring(to_low, "gx", -1)
    padded = pltpu.VMEM((3, 144, 128), f32)
    (half_t,) = call(low_density_kernel, [((64, 128), f32)], [padded], inputs=7)(
        *sources, sums[-1]
    )
    side = ((72, 128), f32)
    to_low, to_high, *sums = call(
        planes_sum_kernel, [side, side] + held, inputs=8
    )(*sums, low, high, low_2, high_2, half_t)
    low = shift_ring(to_high, "gy", 1)
    high = shift_ring(to_low, "gy", -1)
    scratch = [padded, pltpu.VMEM((64, 128), f32)]
    density, done = call(
        density_kernel, [((8, 16, 128), f32), ((8, 128), f32)], scratch, inputs=8
    )(*sources, half_t, sums[-1])
    velocity, pressure = call(
        pressure_kernel,
        [((3, 8, 16, 128), f32), ((8, 16, 128), f32)],
        halves,
        inputs=7,
    )(moved, *sums, low, high, done)
    return velocity, density, pressure


def body(velocity, density, offsets, eighths):
    moved, past, sources = advect(velocity, density, offsets, eighths)
    return project(moved, past, *sources)


def solution(mesh):
    return jax.shard_map(
        body,
        mesh=mesh,
        in_specs=(
            P(None, "gx", "gy", "gz"),
            P("gx", "gy", "gz"),
            P(None, "gx", "gy", "gz"),
            P(None, "gx", "gy", "gz"),
        ),
        out_specs=(P(None, "gx", "gy", "gz"), P("gx", "gy", "gz"), P("gx", "gy", "gz")),
        check_vma=False,
    )
```
